32 devices in a mesh: segment: 2 (over x), dp: 16 (over z, y, core).
Axes of the slice: x: 2, y: 2, z: 4, core: 2. Of those that a mesh axis runs over, the one named last changes fastest.
Arguments:
- boundary: bfloat16 [2, 2, 16, 512, 768], P('segment', None, 'dp'), may hold values from -6 to 6
- lengths: int32 [2, 16], P(None, 'dp'), may hold values from 20 to 512, as said below
- ln1_gain: float32 [2, 768], P('segment', 'dp'), may hold values from 0.5 to 1.5
- ln1_bias: float32 [2, 768], P('segment', 'dp'), may hold values from -2 to 2
- value_weight: float32 [2, 768, 768], P('segment', 'dp'), may hold values from -0.21875 to 0.21875
- value_bias: float32 [2, 768], P('segment', 'dp'), may hold values from -2 to 2
- out_weight: float32 [2, 768, 768], P('segment', 'dp'), may hold values from -0.625 to 0.625
- out_bias: float32 [2, 768], P('segment', 'dp'), may hold values from -2 to 2
- ln2_gain: float32 [2, 768], P('segment', 'dp'), may hold values from 0.5 to 1.5
- ln2_bias: float32 [2, 768], P('segment', 'dp'), may hold values from -2 to 2
- ffn_in: float32 [2, 768, 3072], P('segment', 'dp'), may hold values from -0.21875 to 0.21875
- ffn_in_bias: float32 [2, 3072], P('segment', 'dp'), may hold values from -2 to 2
- ffn_out: float32 [2, 3072, 768], P('segment', 'dp'), may hold values from -0.15625 to 0.15625
- ffn_out_bias: float32 [2, 768], P('segment', 'dp'), may hold values from -2 to 2
- dense_first: float32 [768, 768], P(('segment', 'dp')), may hold values from -0.21875 to 0.21875
- dense_first_bias: float32 [768], P(('segment', 'dp')), may hold values from -2 to 2
- dense_second: float32 [768, 6144], P(('segment', 'dp')), may hold values from -0.5 to 0.5
- dense_second_bias: float32 [6144], P(('segment', 'dp')), may hold values from -3 to 3
- random_table: float32 [6144, 512], P(('segment', 'dp')), may hold values from -8 to 8
Outputs:
- layer_outputs: bfloat16 [2, 2, 16, 512, 768], P('segment', None, 'dp')
- input_grads: bfloat16 [2, 2, 16, 512, 768], P('segment', None, 'dp')
- grad_ln1_gain: float32 [2, 768], P('segment', 'dp')
- grad_ln1_bias: float32 [2, 768], P('segment', 'dp')
- grad_value_weight: float32 [2, 768, 768], P('segment', 'dp')
- grad_value_bias: float32 [2, 768], P('segment', 'dp')
- grad_out_weight: float32 [2, 768, 768], P('segment', 'dp')
- grad_out_bias: float32 [2, 768], P('segment', 'dp')
- grad_ln2_gain: float32 [2, 768], P('segment', 'dp')
- grad_ln2_bias: float32 [2, 768], P('segment', 'dp')
- grad_ffn_in: float32 [2, 768, 3072], P('segment', 'dp')
- grad_ffn_in_bias: float32 [2, 3072], P('segment', 'dp')
- grad_ffn_out: float32 [2, 3072, 768], P('segment', 'dp')
- grad_ffn_out_bias: float32 [2, 768], P('segment', 'dp')
- grad_dense_first: float32 [768, 768], P(('segment', 'dp'))
- grad_dense_first_bias: float32 [768], P(('segment', 'dp'))
- grad_dense_second: float32 [768, 6144], P(('segment', 'dp'))
- grad_dense_second_bias: float32 [6144], P(('segment', 'dp'))
- grad_random_table: float32 [6144, 512], P(('segment', 'dp'))
The draws below stay inside these ranges and needn't reach their ends.
Inputs may be any that keep to these rules, and one draw needn't show every extreme that they name: `lengths`: each item's used positions; at least one item has exactly 512.
All inputs are finite; a program needn't handle non-finite values.
Results may differ from the reference program's by a relative error of at most 0.028.
Values may be sent and summed in bfloat16 or wider, within the bound.
A program may use at most 512 MiB of HBM per device.

```python
import jax
import jax.numpy as jnp
from jax import lax

D = 768
HEADS = 12
HEAD_DIM = 64
FF = 3072
SLOTS = 512
MIN_LENGTH = 20
MICRO = 2
ITEMS = 16


def draw_lengths(key, part):
    key = jax.random.fold_in(key, 7)
    first_key, second_key = jax.random.split(key)
    drawn = jax.random.randint(first_key, (MICRO * ITEMS,), MIN_LENGTH, SLOTS + 1)
    chosen = jax.random.randint(second_key, (), 0, MICRO * ITEMS)
    places = jnp.arange(MICRO * ITEMS)
    drawn = jnp.where(places == chosen, SLOTS, drawn)
    return drawn.reshape(MICRO, ITEMS).astype(jnp.int32)


def steps_of(own_key, shape, pieces, least, high):
    def one(axis_at, blocks):
        steps = jax.random.uniform(jax.random.fold_in(jax.random.fold_in(own_key, 6), axis_at), (blocks,), jnp.float32, least / len(pieces), high / len(pieces))
        return jnp.repeat(jnp.exp(steps), shape[axis_at] // blocks).reshape((-1,) + (1,) * (len(shape) - axis_at - 1))

    loudness = one(*pieces[0])
    for cut in pieces[1:]:
        loudness = loudness * one(*cut)
    return loudness


def scatter_about(key, extent, scale, bound, cuts=(), held_as=jnp.bfloat16):
    level = steps_of(key, extent, cuts, -0.22, 0.18) if cuts else 1.0
    values = jax.random.normal(key, extent, jnp.float32) * scale * level
    return jnp.minimum(jnp.maximum(values, -bound), bound).astype(held_as)


def setup_inputs(seed: int = 0) -> dict:
    arg_keys = jax.random.split(jax.random.key(seed), 20)
    boundary = scatter_about(arg_keys[0], (2, MICRO, ITEMS, SLOTS, D), 1.0, 6.0, ((0, 2), (2, 16)))
    lengths = draw_lengths(jax.random.fold_in(arg_keys[19], 71), 0)
    ln1_gain = jnp.clip(1.0 + 0.1 * jax.random.normal(arg_keys[2], (2, D), jnp.float32), 0.5, 1.5)
    ln1_bias = scatter_about(arg_keys[3], (2, D), 0.3, 2.0, ((0, 2), (1, 16)), jnp.float32)
    value_weight = scatter_about(arg_keys[4], (2, D, D), D ** -0.5, 0.21875, ((0, 2), (1, 16)), jnp.float32)
    value_bias = scatter_about(arg_keys[5], (2, D), 0.3, 2.0, ((0, 2), (1, 16)), jnp.float32)
    out_weight = scatter_about(arg_keys[6], (2, D, D), (D // 8) ** -0.5, 0.625, ((0, 2), (1, 16)), jnp.float32)
    out_bias = scatter_about(arg_keys[7], (2, D), 0.3, 2.0, ((0, 2), (1, 16)), jnp.float32)
    ln2_gain = jnp.clip(1.0 + 0.1 * jax.random.normal(arg_keys[8], (2, D), jnp.float32), 0.5, 1.5)
    ln2_bias = scatter_about(arg_keys[9], (2, D), 0.3, 2.0, ((0, 2), (1, 16)), jnp.float32)
    ffn_in = scatter_about(arg_keys[10], (2, D, FF), D ** -0.5, 0.21875, ((0, 2), (1, 16)), jnp.float32)
    ffn_in_bias = scatter_about(arg_keys[11], (2, FF), 0.3, 2.0, ((0, 2), (1, 16)), jnp.float32)
    ffn_out = scatter_about(arg_keys[12], (2, FF, D), (FF // 2) ** -0.5, 0.15625, ((0, 2), (1, 16)), jnp.float32)
    ffn_out_bias = scatter_about(arg_keys[13], (2, D), 0.3, 2.0, ((0, 2), (1, 16)), jnp.float32)
    dense_first = scatter_about(arg_keys[14], (D, D), D ** -0.5, 0.21875, ((0, 32),), jnp.float32)
    dense_first_bias = scatter_about(arg_keys[15], (D,), 0.3, 2.0, ((0, 32),), jnp.float32)
    dense_second = scatter_about(arg_keys[16], (D, HEADS * SLOTS), (D // 6) ** -0.5, 0.5, ((0, 32),), jnp.float32)
    dense_second_bias = scatter_about(arg_keys[17], (HEADS * SLOTS,), 0.5, 3.0, ((0, 32),), jnp.float32)
    random_table = scatter_about(arg_keys[18], (HEADS * SLOTS, SLOTS), 1.5, 8.0, ((0, 32),), jnp.float32)
    return dict(boundary=boundary, lengths=lengths, ln1_gain=ln1_gain, ln1_bias=ln1_bias, value_weight=value_weight, value_bias=value_bias, out_weight=out_weight, out_bias=out_bias, ln2_gain=ln2_gain, ln2_bias=ln2_bias, ffn_in=ffn_in, ffn_in_bias=ffn_in_bias, ffn_out=ffn_out, ffn_out_bias=ffn_out_bias, dense_first=dense_first, dense_first_bias=dense_first_bias, dense_second=dense_second, dense_second_bias=dense_second_bias, random_table=random_table)


EPSILON = 1e-05
GELU_SCALE = 0.7978845608028654

@jax.custom_vjp
def low(v):
    return lax.optimization_barrier(v.astype(jnp.bfloat16)).astype(jnp.float32)

@jax.custom_vjp
def low_back(v):
    return v

def low_keep(v):
    return (low(v), None)

def low_pass(kept, grad):
    return (grad,)

def back_keep(v):
    return (v, None)

def back_low(kept, grad):
    return (low(grad),)
low.defvjp(low_keep, low_pass)
low_back.defvjp(back_keep, back_low)

def layer_norm(rows, gain, shift):
    centre = rows - lax.optimization_barrier(jnp.mean(rows, axis=-1, keepdims=True))
    spread = lax.optimization_barrier(jnp.mean(centre * centre, axis=-1, keepdims=True))
    return centre * lax.rsqrt(spread + EPSILON) * gain + shift

def smooth_gate(value):
    return 0.5 * value * (1.0 + jnp.tanh(GELU_SCALE * (value + 0.044715 * value * value * value)))

def widest(left, right):
    return jnp.dot(left, right, precision=lax.Precision.HIGHEST)

def probabilities(logits, length):
    places = lax.broadcasted_iota(jnp.int32, logits.shape, 2)
    valid = places < length
    masked = jnp.where(valid, logits, -1e+30)
    top = lax.optimization_barrier(jnp.max(masked, axis=-1, keepdims=True))
    expo = jnp.where(valid, jnp.exp(masked - top), 0.0)
    return expo / lax.optimization_barrier(jnp.sum(expo, axis=-1, keepdims=True))

def one_item(common, synth, rows, length, dense):
    gain_one, bias_one, value_w, value_b, out_w, out_b, gain_two, bias_two, inner_w, inner_b, outer_w, outer_b = common
    normed = low(layer_norm(rows, gain_one, bias_one))
    values = low(low_back(widest(normed, value_w) + value_b))
    if dense:
        first = low_back(widest(normed, synth[0]) + synth[1])
        gated = low(smooth_gate(first))
        flat_logits = low_back(widest(gated, synth[2]) + synth[3])
        logits = flat_logits.reshape(SLOTS, HEADS, SLOTS).transpose(1, 0, 2)
    else:
        logits = synth[0].reshape(HEADS, SLOTS, SLOTS)
    probs = low(probabilities(logits, length))
    heads = values.reshape(SLOTS, HEADS, HEAD_DIM)
    mixed = jnp.einsum('hqk,khd->qhd', probs, heads, precision=lax.Precision.HIGHEST).reshape(SLOTS, D)
    mixed = low(low_back(mixed))
    hidden = rows + low_back(widest(mixed, out_w) + out_b)
    normed_two = low(layer_norm(hidden, gain_two, bias_two))
    inner = low_back(widest(normed_two, inner_w) + inner_b)
    active = low(smooth_gate(inner))
    return hidden + low_back(widest(active, outer_w) + outer_b)

def layer(params, rows, lens, dense):
    common = tuple((low(w) for w in params['common']))
    synth = tuple((low(w) for w in params['synth']))

    def step(pair):
        return one_item(common, synth, pair[0], pair[1], dense)
    return lax.map(jax.checkpoint(step), (rows, lens))

def reference(boundary, lengths, ln1_gain, ln1_bias, value_weight, value_bias, out_weight, out_bias, ln2_gain, ln2_bias, ffn_in, ffn_in_bias, ffn_out, ffn_out_bias, dense_first, dense_first_bias, dense_second, dense_second_bias, random_table):
    stacked = (ln1_gain, ln1_bias, value_weight, value_bias, out_weight, out_bias, ln2_gain, ln2_bias, ffn_in, ffn_in_bias, ffn_out, ffn_out_bias)
    first_params = {'common': tuple((w[0] for w in stacked)), 'synth': (dense_first, dense_first_bias, dense_second, dense_second_bias)}
    second_params = {'common': tuple((w[1] for w in stacked)), 'synth': (random_table,)}
    count = MICRO * ITEMS
    first_in = boundary[0].astype(jnp.float32).reshape(count, SLOTS, D)
    cotangent = boundary[1].astype(jnp.float32).reshape(count, SLOTS, D)
    lens = lengths.reshape(count).astype(jnp.int32)

    def dense_layer(params, rows):
        return layer(params, rows, lens, True)

    def random_layer(params, rows):
        return layer(params, rows, lens, False)
    out_one, back_one = jax.vjp(dense_layer, first_params, first_in)
    middle = low(out_one)
    out_two, back_two = jax.vjp(random_layer, second_params, middle)
    grad_two, grad_middle = back_two(cotangent)
    grad_one, grad_first = back_one(low(grad_middle))
    shape = (2, MICRO, ITEMS, SLOTS, D)
    layer_outputs = jnp.stack([out_one, out_two]).reshape(shape).astype(jnp.bfloat16)
    input_grads = jnp.stack([grad_first, grad_middle]).reshape(shape).astype(jnp.bfloat16)
    common_grads = tuple((jnp.stack([grad_one['common'][k], grad_two['common'][k]]) for k in range(12)))
    return (layer_outputs, input_grads, common_grads[0], common_grads[1], common_grads[2], common_grads[3], common_grads[4], common_grads[5], common_grads[6], common_grads[7], common_grads[8], common_grads[9], common_grads[10], common_grads[11], grad_one['synth'][0], grad_one['synth'][1], grad_one['synth'][2], grad_one['synth'][3], grad_two['synth'][0])
```

```python
import functools
import math
from typing import Any, NamedTuple

import jax
import jax.numpy as jnp
from jax import lax
from jax.experimental import pallas as pl
from jax.experimental.pallas import tpu as pltpu
from jax.sharding import PartitionSpec as P

MESH = pl.DeviceIdType.MESH
HEADS = 12
EPSILON = 1e-05
GELU_SCALE = 0.7978845608028654
AXES = ("segment", "dp")


def half(value):
    return value.astype(jnp.bfloat16)


def wide(value):
    return value.astype(jnp.float32)


def mm(left, right):
    return jnp.dot(left, right, preferred_element_type=jnp.float32)


def mm_tn(left, right):
    return lax.dot_general(left, right, (((0,), (0,)), ((), ())), preferred_element_type=jnp.float32)


def mm_nt(left, right):
    return lax.dot_general(left, right, (((1,), (1,)), ((), ())), preferred_element_type=jnp.float32)


class Place:
    def __init__(self, nz):
        self.nz = nz
        self.x = lax.axis_index("segment")
        d = lax.axis_index("dp")
        self.c = d % 2
        self.y = (d // 2) % 2
        self.z = d // 4
        par = self.z % 2
        self.q = par * ((self.z + 1) // 2) + (1 - par) * ((nz - self.z // 2) % nz)

    def z_at(self, q):
        nz = self.nz
        upper = ((q + nz - 1) % nz) // (nz // 2)
        return (1 - upper) * (2 * q - 1) + upper * ((2 * (nz - q)) % (2 * nz))

    def ring_z(self, back):
        return self.z_at((self.q + 2 * self.nz - back) % self.nz)

    def device(self, x=None, z=None, y=None, c=None):
        x = self.x if x is None else x
        z = self.z if z is None else z
        y = self.y if y is None else y
        c = self.c if c is None else c
        return (x, (z * 2 + y) * 2 + c)

    def other(self, axis):
        return self.device(**{axis: 1 - getattr(self, axis)})

    def succ(self):
        return self.device(z=self.z_at((self.q + 1) % self.nz))

    def pred(self):
        return self.device(z=self.ring_z(1))


def greet(place):
    barrier = pltpu.get_barrier_semaphore()
    peers = [place.other("x"), place.other("y"), place.other("c"), place.succ(), place.pred()]
    for peer in peers:
        pl.semaphore_signal(barrier, inc=1, device_id=peer, device_id_type=MESH)
    pl.semaphore_wait(barrier, len(peers))


def block_of(ref, place, c, z, x=None, y=None):
    xs = pl.ds(0, 2) if x is None else x
    ys = pl.ds(0, 2) if y is None else y
    return ref.at[xs, z, ys, c]


def gather_kernel(orders, nz, *refs):
    n = len(orders)
    ins, outs = refs[:n], refs[n : 2 * n]
    send, recv, local = refs[2 * n :]
    place = Place(nz)
    greet(place)
    started = []

    def put(i, k, src, dst, device):
        copy = pltpu.make_async_remote_copy(
            src_ref=src,
            dst_ref=dst,
            send_sem=send.at[i, k],
            recv_sem=recv.at[i, k],
            device_id=device,
            device_id_type=MESH,
        )
        copy.start()
        started.append(copy)
        return copy

    copies = [dict() for _ in orders]

    def stage(i, t):
        first, second, third = orders[i]
        out, mine = outs[i], copies[i]

        def shard(z, **at):
            return block_of(out, place, place.c, z, **at)

        def own(axis, z):
            return shard(z, **{axis: getattr(place, axis)})

        one = shard(place.z, x=place.x, y=place.y)
        if t == 0:
            mine["own"] = pltpu.make_async_copy(ins[i], one, local.at[i])
            mine["own"].start()
        if second == "z":
            if t == 0:
                mine["p"] = put(i, 0, ins[i], one, place.other(first))
                return
            if t == 1:
                mine["own"].wait()
                mine["p"].wait_recv()
            elif t <= nz:
                mine["z", t - 1].wait_recv()
            if t <= nz:
                z = place.ring_z(t - 1)
                block = own(third, z)
                if t < nz:
                    mine["z", t] = put(i, t, block, block, place.succ())
                mine["l", t] = put(i, nz + t, block, block, place.other(third))
                mine["c", t] = put(i, 2 * nz + t, block, block, place.other("c"))
            if t >= 2:
                mine["l", t - 1].wait_recv()
                z = place.ring_z(t - 2)
                block = shard(z, **{third: 1 - getattr(place, third)})
                mine["d", t - 1] = put(i, 3 * nz + t - 1, block, block, place.other("c"))
        else:
            if t <= nz - 1:
                if t > 0:
                    mine["z", t].wait_recv()
                z = place.ring_z(t)
                src = ins[i] if t == 0 else shard(z, x=place.x, y=place.y)
                dst = shard(z, x=place.x, y=place.y)
                if t < nz - 1:
                    mine["z", t + 1] = put(i, t, src, dst, place.succ())
                mine["p", t + 1] = put(i, nz + t, src, dst, place.other(second))
            if 1 <= t <= nz:
                if t == 1:
                    mine["own"].wait()
                mine["p", t].wait_recv()
                block = own(third, place.ring_z(t - 1))
                mine["l", t] = put(i, 2 * nz + t, block, block, place.other(third))
                mine["c", t] = put(i, 3 * nz + t, block, block, place.other("c"))
            if t >= 2:
                mine["l", t - 1].wait_recv()
                block = shard(place.ring_z(t - 2), **{third: 1 - getattr(place, third)})
                mine["d", t - 1] = put(i, 4 * nz + t - 1, block, block, place.other("c"))

    stages = nz + 2
    for t in range(stages + n - 1):
        for i in range(n):
            if 0 <= t - i < stages:
                stage(i, t - i)
    for mine in copies:
        for key, copy in mine.items():
            if key[0] in "cd":
                copy.wait_recv()
    for copy in started:
        copy.wait_send()


def gather_all(shards, orders, mesh):
    nx, ndp = mesh.shape["segment"], mesh.shape["dp"]
    if nx != 2 or ndp % 8:
        return [lax.all_gather(s, AXES, axis=0) for s in shards]
    nz, n = ndp // 4, len(shards)
    slots = 5 * nz + 2
    outs = pl.pallas_call(
        functools.partial(gather_kernel, orders, nz),
        out_shape=[jax.ShapeDtypeStruct((2, nz, 2, 2) + s.shape, s.dtype) for s in shards],
        in_specs=[pl.BlockSpec(memory_space=pl.ANY)] * n,
        out_specs=[pl.BlockSpec(memory_space=pl.ANY)] * n,
        scratch_shapes=[
            pltpu.SemaphoreType.DMA((n, slots)),
            pltpu.SemaphoreType.DMA((n, slots)),
            pltpu.SemaphoreType.DMA((n,)),
        ],
        compiler_params=pltpu.CompilerParams(collective_id=0, has_side_effects=True),
        name="gather_weights",
    )(*shards)
    return [o.reshape((nx * ndp,) + s.shape) for o, s in zip(outs, shards)]


def add_to(dst, src):
    lead = dst.shape[:-2]

    def one(j, carry):
        at = (j // 2, j % 2) if len(lead) == 2 else (j,)[: len(lead)]
        at = at + (slice(None), slice(None))
        dst[at] = dst[at] + src[at]
        return carry

    if lead:
        lax.fori_loop(0, math.prod(lead), one, 0)
    else:
        dst[...] = dst[...] + src[...]


def scatter_kernel(orders, nz, *refs):
    n = len(orders)
    ins, outs = refs[:n], refs[n : 2 * n]
    accs, stages, firsts, rings, lasts = (refs[(2 + j) * n : (3 + j) * n] for j in range(5))
    send, recv, local = refs[7 * n :]
    place = Place(nz)
    greet(place)
    started = []

    def put(i, k, src, dst, device):
        copy = pltpu.make_async_remote_copy(
            src_ref=src,
            dst_ref=dst,
            send_sem=send.at[i, k],
            recv_sem=recv.at[i, k],
            device_id=device,
            device_id_type=MESH,
        )
        copy.start()
        started.append(copy)
        return copy

    live = [dict() for _ in orders]

    def load(i, k):
        copy = pltpu.make_async_copy(
            block_of(ins[i], place, place.c, place.ring_z(k)), stages[i].at[k % 2], local.at[i, k % 2]
        )
        copy.start()
        live[i]["o", k] = copy

    def stage(i, s):
        first, second, third = orders[i]
        acc, mine = accs[i], live[i]
        early, ring, late = firsts[i], rings[i], lasts[i]

        def part(k, flip=0, flip2=None):
            own = {axis: getattr(place, axis) for axis in "xy"}
            own[first] = own[first] + flip * (1 - 2 * own[first])
            if flip2 is None:
                own["xy".replace(first, "")] = pl.ds(0, 2)
            else:
                other = "xy".replace(first, "")
                own[other] = own[other] + flip2 * (1 - 2 * own[other])
            return acc.at[k - 1, own["x"], own["y"]]

        if s == 0:
            for k in range(1, nz + 1):
                src = block_of(ins[i], place, 1 - place.c, place.ring_z(k))
                mine["c", k] = put(i, k, src, acc.at[k - 1], place.other("c"))
            load(i, 1)
            load(i, 2)
        if 1 <= s <= nz:
            k = s
            mine["c", k].wait_recv()
            mine["o", k].wait()
            add_to(acc.at[k - 1], stages[i].at[k % 2])
            if k + 2 <= nz:
                load(i, k + 2)
            mine["p", k] = put(i, nz + k, part(k, 1), early.at[k - 1], place.other(first))
        if 2 <= s <= nz + 1:
            k = s - 1
            mine["p", k].wait_recv()
            add_to(part(k), early.at[k - 1])
        if second == "z":
            if s == 2:
                mine["z", 1] = put(i, 2 * nz + 1, part(1), ring.at[0], place.succ())
            if 3 <= s <= nz + 1:
                t = s - 2
                mine["z", t].wait_recv()
                add_to(ring.at[t - 1], part(t + 1))
                if t < nz - 1:
                    mine["z", t + 1] = put(i, 2 * nz + t + 1, ring.at[t - 1], ring.at[t], place.succ())
                else:
                    there = 1 - getattr(place, third)
                    mine["l"] = put(i, 3 * nz + 1, ring.at[t - 1, there], late, place.other(third))
            if s == nz + 2:
                mine["l"].wait_recv()
                outs[i][...] = wide(ring[nz - 2, getattr(place, third)]) + wide(late[...])
        else:
            if 2 <= s <= nz + 1:
                k = s - 1
                mine["l", k] = put(i, 3 * nz + k, part(k, 0, 1), late.at[k - 1], place.other(second))
            if 3 <= s <= nz + 2:
                k = s - 2
                mine["l", k].wait_recv()
                add_to(part(k, 0, 0), late.at[k - 1])
                if k == 1:
                    mine["z", 1] = put(i, 2 * nz + 1, part(1, 0, 0), ring.at[0], place.succ())
                else:
                    t = k - 1
                    mine["z", t].wait_recv()
                    if t < nz - 1:
                        add_to(ring.at[t - 1], part(t + 1, 0, 0))
                        mine["z", t + 1] = put(i, 2 * nz + t + 1, ring.at[t - 1], ring.at[t], place.succ())
                    else:
                        outs[i][...] = wide(ring[t - 1]) + wide(part(nz, 0, 0)[...])

    stages_of = nz + 3
    for t in range(stages_of + n - 1):
        for i in range(n):
            if 0 <= t - i < stages_of:
                stage(i, t - i)
    for copy in started:
        copy.wait_send()


def scatter_all(grads, orders, mesh):
    nx, ndp = mesh.shape["segment"], mesh.shape["dp"]
    if nx != 2 or ndp != 16:
        return [wide(lax.psum_scatter(g, AXES, scatter_dimension=0, tiled=False)) for g in grads]
    nz, n = ndp // 4, len(grads)

    def scratch(lead):
        return [pltpu.VMEM(lead(o) + g.shape[1:], g.dtype) for o, g in zip(orders, grads)]

    slots = 4 * nz + 2
    return pl.pallas_call(
        functools.partial(scatter_kernel, orders, nz),
        out_shape=[jax.ShapeDtypeStruct(g.shape[1:], jnp.float32) for g in grads],
        in_specs=[pl.BlockSpec(memory_space=pl.ANY)] * n,
        out_specs=[pl.BlockSpec(memory_space=pltpu.VMEM)] * n,
        scratch_shapes=scratch(lambda o: (nz, 2, 2))
        + scratch(lambda o: (2, 2, 2))
        + scratch(lambda o: (nz, 2))
        + scratch(lambda o: (nz - 1, 2) if o[1] == "z" else (nz - 1,))
        + scratch(lambda o: () if o[1] == "z" else (nz,))
        + [
            pltpu.SemaphoreType.DMA((n, slots)),
            pltpu.SemaphoreType.DMA((n, slots)),
            pltpu.SemaphoreType.DMA((n, 2)),
        ],
        compiler_params=pltpu.CompilerParams(
            collective_id=1, has_side_effects=True, vmem_limit_bytes=62 * 2**20
        ),
        name="sum_gradients",
    )(*[g.reshape((2, nz, 2, 2) + g.shape[1:]) for g in grads])


def norm_parts(rows):
    centre = rows - jnp.mean(rows, axis=-1, keepdims=True)
    inv = lax.rsqrt(jnp.mean(centre * centre, axis=-1, keepdims=True) + EPSILON)
    return centre * inv, inv


def norm_back(grad, normal, inv, gain):
    m = grad * gain
    part = inv * (
        m - jnp.mean(m, axis=-1, keepdims=True) - normal * jnp.mean(m * normal, axis=-1, keepdims=True)
    )
    return part, jnp.sum(grad * normal, axis=0), jnp.sum(grad, axis=0)


def sums(value):
    return jnp.sum(wide(value), axis=0)


def gelu(t):
    return 0.5 * t * (1.0 + jnp.tanh(GELU_SCALE * (t + 0.044715 * t * t * t)))


def gelu_slope(t):
    th = jnp.tanh(GELU_SCALE * (t + 0.044715 * t * t * t))
    return 0.5 * (1.0 + th) + 0.5 * t * (1.0 - th * th) * GELU_SCALE * (1.0 + 3 * 0.044715 * t * t)


def softmax(logits, length):
    valid = lax.broadcasted_iota(jnp.int32, logits.shape, 2) < length
    masked = jnp.where(valid, logits, -1e30)
    expo = jnp.where(valid, jnp.exp(masked - jnp.max(masked, axis=2, keepdims=True)), 0.0)
    return expo / jnp.sum(expo, axis=2, keepdims=True)


class Layer(NamedTuple):
    ln1_gain: Any
    ln1_bias: Any
    value_weight: Any
    value_bias: Any
    out_weight: Any
    out_bias: Any
    ln2_gain: Any
    ln2_bias: Any
    ffn_in: Any
    ffn_in_bias: Any
    ffn_out: Any
    ffn_out_bias: Any


class Synth(NamedTuple):
    first: Any
    first_bias: Any
    second: Any
    second_bias: Any
    table: Any


def forward(rows, length, w, synth, dense):
    slots, d = rows.shape
    n1, r1 = norm_parts(rows)
    a = half(n1 * w.ln1_gain + w.ln1_bias)
    v = half(mm(a, w.value_weight) + w.value_bias)
    if dense:
        f = mm(a, synth.first) + synth.first_bias
        p = half(gelu(f))
        logits = mm(p, synth.second) + synth.second_bias
        logits = logits.reshape(slots, HEADS, slots).transpose(1, 0, 2)
    else:
        f = p = None
        logits = wide(synth.table).reshape(HEADS, slots, slots)
    probs = half(softmax(logits, length))
    heads = v.reshape(slots, HEADS, d // HEADS)
    mixed = jnp.einsum("hqk,khd->qhd", probs, heads, preferred_element_type=jnp.float32)
    c = half(mixed.reshape(slots, d))
    hid = rows + mm(c, w.out_weight) + w.out_bias
    n2, r2 = norm_parts(hid)
    b = half(n2 * w.ln2_gain + w.ln2_bias)
    z = mm(b, w.ffn_in) + w.ffn_in_bias
    q = half(gelu(z))
    y = hid + mm(q, w.ffn_out) + w.ffn_out_bias
    return half(y), (n1, r1, a, f, p, probs, v, c, n2, r2, b, half(gelu_slope(z)), q)


def backward(g, saved, w, synth, dense):
    n1, r1, a, f, p, probs, v, c, n2, r2, b, slope, q = saved
    slots, d = g.shape
    gy = half(g)
    gz = half(mm_nt(gy, w.ffn_out) * slope)
    part, g_gain2, g_bias2 = norm_back(mm_nt(gz, w.ffn_in), n2, r2, w.ln2_gain)
    ghid = wide(g) + part
    gatt = half(ghid)
    gc = half(mm_nt(gatt, w.out_weight)).reshape(slots, HEADS, d // HEADS)
    heads = v.reshape(slots, HEADS, d // HEADS)
    dprobs = jnp.einsum("qhd,khd->hqk", gc, heads, preferred_element_type=jnp.float32)
    gv = half(
        jnp.einsum("hqk,qhd->khd", probs, gc, preferred_element_type=jnp.float32).reshape(slots, d)
    )
    probs = wide(probs)
    dlogits = probs * (dprobs - jnp.sum(probs * dprobs, axis=2, keepdims=True))
    ga = mm_nt(gv, w.value_weight)
    if dense:
        gb = half(dlogits.transpose(1, 0, 2).reshape(slots, HEADS * slots))
        gf = half(mm_nt(gb, synth.second) * gelu_slope(f))
        ga = ga + mm_nt(gf, synth.first)
        g_synth = Synth(mm_tn(a, gf), sums(gf), mm_tn(p, gb), sums(gb), None)
    else:
        g_synth = Synth(None, None, None, None, dlogits.reshape(HEADS * slots, slots))
    part, g_gain1, g_bias1 = norm_back(ga, n1, r1, w.ln1_gain)
    g_layer = Layer(
        g_gain1,
        g_bias1,
        mm_tn(a, gv),
        sums(gv),
        mm_tn(c, gatt),
        sums(gatt),
        g_gain2,
        g_bias2,
        mm_tn(b, gz),
        sums(gz),
        mm_tn(q, gy),
        sums(gy),
    )
    return half(ghid + part), g_layer, g_synth


def is_matrix(k):
    return k < 12 and k in (2, 4, 8, 10) or k in (12, 14, 16)


MATRICES = (2, 8, 10, 14, 16, 4, 12)
VECTORS = tuple(k for k in range(17) if not is_matrix(k))
ORDERS = ("zxy", "zxy", "xzy", "yzx", "yzx", "zxy", "yzx", "xzy")
SUM_ORDERS = tuple(o[::-1] for o in ORDERS)


def per_device(mesh, boundary, lengths, *parts):
    nx, ndp = mesh.shape["segment"], mesh.shape["dp"]
    devices = nx * ndp
    s = lax.axis_index("segment")
    first = s == 0
    swap = [(0, 1), (1, 0)]
    own = boundary[0, :, 0]
    received = lax.ppermute(jnp.where(first, own[1], own[0]), "segment", swap)
    rows = jnp.where(first, own[0], received)
    cotangent = jnp.where(first, received, own[1])
    length = jnp.where(first, lengths[0, 0], lengths[1, 0])

    flat = jnp.concatenate([parts[k].reshape(-1) for k in VECTORS])
    sizes = [parts[k].size for k in VECTORS]
    lanes = -(-flat.size // 2048) * 16
    packed = half(jnp.pad(flat, (0, lanes * 128 - flat.size)).reshape(lanes, 128))
    shards = [half(parts[k].reshape(parts[k].shape[-2:])) for k in MATRICES] + [packed]
    gathered = gather_all(shards, ORDERS, mesh)

    full = {}
    for k, g in zip(MATRICES, gathered):
        full[k] = g.reshape((nx, ndp * g.shape[1]) + g.shape[2:]) if k < 12 else g.reshape(-1, g.shape[2])
    vec = wide(gathered[-1].reshape(devices, lanes * 128))
    at = 0
    for k, size in zip(VECTORS, sizes):
        piece = vec[:, at : at + size]
        at += size
        full[k] = piece.reshape(nx, ndp * size) if k < 12 else piece.reshape(devices * size)
    layers = [Layer(*[full[k][j] for k in range(12)]) for j in range(2)]
    synth = Synth(*[full[k] for k in range(12, 17)])

    out0, saved0 = forward(wide(rows), length, layers[0], synth, True)
    out1, saved1 = forward(wide(out0), length, layers[1], synth, False)
    gin1, layer1, synth1 = backward(cotangent, saved1, layers[1], synth, False)
    gin0, layer0, synth0 = backward(gin1, saved0, layers[0], synth, True)

    def swapped(for_first, for_second):
        got = lax.ppermute(jnp.where(first, for_second, for_first), "segment", swap)
        return jnp.stack([jnp.where(first, for_first, got), jnp.where(first, got, for_second)])[None, :, None]

    layer_outputs = swapped(out0, out1)
    input_grads = swapped(gin0, gin1)

    grads = [jnp.stack([half(g0), half(g1)]) if is_matrix(k) else jnp.stack([g0, g1]) for k, (g0, g1) in enumerate(zip(layer0, layer1))]
    grads += list(synth0[:4]) + [synth1.table]
    lists = [half(grads[k]).reshape((devices,) + parts[k].shape[-2:]) for k in MATRICES]
    vec = jnp.concatenate([grads[k].reshape(devices, -1) for k in VECTORS], axis=1)
    vec = jnp.pad(vec, ((0, 0), (0, lanes * 128 - vec.shape[1]))).reshape(devices, lanes, 128)
    summed = scatter_all(lists + [vec], SUM_ORDERS, mesh)
    result = {k: g.reshape(parts[k].shape) for k, g in zip(MATRICES, summed)}
    vec = summed[-1].reshape(-1)
    at = 0
    for k, size in zip(VECTORS, sizes):
        result[k] = vec[at : at + size].reshape(parts[k].shape)
        at += size
    return (layer_outputs, input_grads) + tuple(result[k] for k in range(17))


def solution(mesh):
    layer = [P("segment", "dp")] * 12
    layer[2] = layer[4] = layer[8] = layer[10] = P("segment", "dp", None)
    both = P(AXES)
    rows = P(AXES, None)
    boundary = P("segment", None, "dp", None, None)
    weights = tuple(layer) + (rows, both, rows, both, rows)
    return jax.shard_map(
        functools.partial(per_device, mesh),
        mesh=mesh,
        in_specs=(boundary, P(None, "dp")) + weights,
        out_specs=(boundary, boundary) + weights,
        check_vma=False,
    )
```

```python
import functools
import math
from typing import Any, NamedTuple

import jax
import jax.numpy as jnp
from jax import lax
from jax.experimental import pallas as pl
from jax.experimental.pallas import tpu as pltpu
from jax.sharding import PartitionSpec as P

MESH = pl.DeviceIdType.MESH
HEADS = 12
EPSILON = 1e-05
GELU_SCALE = 0.7978845608028654
AXES = ("segment", "dp")


def half(value):
    return value.astype(jnp.bfloat16)


def wide(value):
    return value.astype(jnp.float32)


def mm(left, right):
    return jnp.dot(left, right, preferred_element_type=jnp.float32)


def mm_tn(left, right):
    return lax.dot_general(left, right, (((0,), (0,)), ((), ())), preferred_element_type=jnp.float32)


def mm_nt(left, right):
    return lax.dot_general(left, right, (((1,), (1,)), ((), ())), preferred_element_type=jnp.float32)


class Place:
    def __init__(self, nz):
        self.nz = nz
        self.x = lax.axis_index("segment")
        d = lax.axis_index("dp")
        self.c = d % 2
        self.y = (d // 2) % 2
        self.z = d // 4
        par = self.z % 2
        self.q = par * ((self.z + 1) // 2) + (1 - par) * ((nz - self.z // 2) % nz)

    def z_at(self, q):
        nz = self.nz
        upper = ((q + nz - 1) % nz) // (nz // 2)
        return (1 - upper) * (2 * q - 1) + upper * ((2 * (nz - q)) % (2 * nz))

    def ring_z(self, back):
        return self.z_at((self.q + 2 * self.nz - back) % self.nz)

    def device(self, x=None, z=None, y=None, c=None):
        x = self.x if x is None else x
        z = self.z if z is None else z
        y = self.y if y is None else y
        c = self.c if c is None else c
        return (x, (z * 2 + y) * 2 + c)

    def other(self, axis):
        return self.device(**{axis: 1 - getattr(self, axis)})

    def succ(self):
        return self.device(z=self.z_at((self.q + 1) % self.nz))

    def pred(self):
        return self.device(z=self.ring_z(1))


def greet(place):
    barrier = pltpu.get_barrier_semaphore()
    peers = [place.other("x"), place.other("y"), place.other("c"), place.succ(), place.pred()]
    for peer in peers:
        pl.semaphore_signal(barrier, inc=1, device_id=peer, device_id_type=MESH)
    pl.semaphore_wait(barrier, len(peers))


def block_of(ref, place, c, z, x=None, y=None):
    xs = pl.ds(0, 2) if x is None else x
    ys = pl.ds(0, 2) if y is None else y
    return ref.at[xs, z, ys, c]


def gather_kernel(orders, nz, *refs):
    n = len(orders)
    ins, outs = refs[:n], refs[n : 2 * n]
    send, recv, local = refs[2 * n :]
    place = Place(nz)
    greet(place)
    started = []

    def put(i, k, src, dst, device):
        copy = pltpu.make_async_remote_copy(
            src_ref=src,
            dst_ref=dst,
            send_sem=send.at[i, k],
            recv_sem=recv.at[i, k],
            device_id=device,
            device_id_type=MESH,
        )
        copy.start()
        started.append(copy)
        return copy

    copies = [dict() for _ in orders]

    def stage(i, t):
        first, second, third = orders[i]
        out, mine = outs[i], copies[i]

        def shard(z, **at):
            return block_of(out, place, place.c, z, **at)

        def own(axis, z):
            return shard(z, **{axis: getattr(place, axis)})

        one = shard(place.z, x=place.x, y=place.y)
        if t == 0:
            mine["own"] = pltpu.make_async_copy(ins[i], one, local.at[i])
            mine["own"].start()
        if second == "z":
            if t == 0:
                mine["p"] = put(i, 0, ins[i], one, place.other(first))
                return
            if t == 1:
                mine["own"].wait()
                mine["p"].wait_recv()
            elif t <= nz:
                mine["z", t - 1].wait_recv()
            if t <= nz:
                z = place.ring_z(t - 1)
                block = own(third, z)
                if t < nz:
                    mine["z", t] = put(i, t, block, block, place.succ())
                mine["l", t] = put(i, nz + t, block, block, place.other(third))
                mine["c", t] = put(i, 2 * nz + t, block, block, place.other("c"))
            if t >= 2:
                mine["l", t - 1].wait_recv()
                z = place.ring_z(t - 2)
                block = shard(z, **{third: 1 - getattr(place, third)})
                mine["d", t - 1] = put(i, 3 * nz + t - 1, block, block, place.other("c"))
        else:
            if t <= nz - 1:
                if t > 0:
                    mine["z", t].wait_recv()
                z = place.ring_z(t)
                src = ins[i] if t == 0 else shard(z, x=place.x, y=place.y)
                dst = shard(z, x=place.x, y=place.y)
                if t < nz - 1:
                    mine["z", t + 1] = put(i, t, src, dst, place.succ())
                mine["p", t + 1] = put(i, nz + t, src, dst, place.other(second))
            if 1 <= t <= nz:
                if t == 1:
                    mine["own"].wait()
                mine["p", t].wait_recv()
                block = own(third, place.ring_z(t - 1))
                mine["l", t] = put(i, 2 * nz + t, block, block, place.other(third))
                mine["c", t] = put(i, 3 * nz + t, block, block, place.other("c"))
            if t >= 2:
                mine["l", t - 1].wait_recv()
                block = shard(place.ring_z(t - 2), **{third: 1 - getattr(place, third)})
                mine["d", t - 1] = put(i, 4 * nz + t - 1, block, block, place.other("c"))

    stages = nz + 2
    for t in range(stages + n - 1):
        for i in range(n):
            if 0 <= t - i < stages:
                stage(i, t - i)
    for mine in copies:
        for key, copy in mine.items():
            if key[0] in "cd":
                copy.wait_recv()
    for copy in started:
        copy.wait_send()


def gather_all(shards, orders, mesh):
    nx, ndp = mesh.shape["segment"], mesh.shape["dp"]
    if nx != 2 or ndp % 8:
        return [lax.all_gather(s, AXES, axis=0) for s in shards]
    nz, n = ndp // 4, len(shards)
    slots = 5 * nz + 2
    outs = pl.pallas_call(
        functools.partial(gather_kernel, orders, nz),
        out_shape=[jax.ShapeDtypeStruct((2, nz, 2, 2) + s.shape, s.dtype) for s in shards],
        in_specs=[pl.BlockSpec(memory_space=pl.ANY)] * n,
        out_specs=[pl.BlockSpec(memory_space=pl.ANY)] * n,
        scratch_shapes=[
            pltpu.SemaphoreType.DMA((n, slots)),
            pltpu.SemaphoreType.DMA((n, slots)),
            pltpu.SemaphoreType.DMA((n,)),
        ],
        compiler_params=pltpu.CompilerParams(collective_id=0, has_side_effects=True),
        name="gather_weights",
    )(*shards)
    return [o.reshape((nx * ndp,) + s.shape) for o, s in zip(outs, shards)]


def add_to(dst, src):
    lead = dst.shape[:-2]

    def one(j, carry):
        at = (j // 2, j % 2) if len(lead) == 2 else (j,)[: len(lead)]
        at = at + (slice(None), slice(None))
        dst[at] = dst[at] + src[at]
        return carry

    if lead:
        lax.fori_loop(0, math.prod(lead), one, 0)
    else:
        dst[...] = dst[...] + src[...]


def scatter_kernel(orders, nz, *refs):
    n = len(orders)
    ins, outs = refs[:n], refs[n : 2 * n]
    accs, stages, firsts, rings, lasts = (refs[(2 + j) * n : (3 + j) * n] for j in range(5))
    send, recv, local = refs[7 * n :]
    place = Place(nz)
    greet(place)
    started = []

    def put(i, k, src, dst, device):
        copy = pltpu.make_async_remote_copy(
            src_ref=src,
            dst_ref=dst,
            send_sem=send.at[i, k],
            recv_sem=recv.at[i, k],
            device_id=device,
            device_id_type=MESH,
        )
        copy.start()
        started.append(copy)
        return copy

    live = [dict() for _ in orders]

    def load(i, k):
        copy = pltpu.make_async_copy(
            block_of(ins[i], place, place.c, place.ring_z(k)), stages[i].at[k % 2], local.at[i, k % 2]
        )
        copy.start()
        live[i]["o", k] = copy

    def stage(i, s):
        first, second, third = orders[i]
        acc, mine = accs[i], live[i]
        early, ring, late = firsts[i], rings[i], lasts[i]

        def part(k, flip=0, flip2=None):
            own = {axis: getattr(place, axis) for axis in "xy"}
            own[first] = own[first] + flip * (1 - 2 * own[first])
            if flip2 is None:
                own["xy".replace(first, "")] = pl.ds(0, 2)
            else:
                other = "xy".replace(first, "")
                own[other] = own[other] + flip2 * (1 - 2 * own[other])
            return acc.at[k - 1, own["x"], own["y"]]

        if s == 0:
            for k in range(1, nz + 1):
                src = block_of(ins[i], place, 1 - place.c, place.ring_z(k))
                mine["c", k] = put(i, k, src, acc.at[k - 1], place.other("c"))
            load(i, 1)
            load(i, 2)
        if 1 <= s <= nz:
            k = s
            mine["c", k].wait_recv()
            mine["o", k].wait()
            add_to(acc.at[k - 1], stages[i].at[k % 2])
            if k + 2 <= nz:
                load(i, k + 2)
            mine["p", k] = put(i, nz + k, part(k, 1), early.at[k - 1], place.other(first))
        if 2 <= s <= nz + 1:
            k = s - 1
            mine["p", k].wait_recv()
            add_to(part(k), early.at[k - 1])
        if second == "z":
            if s == 2:
                mine["z", 1] = put(i, 2 * nz + 1, part(1), ring.at[0], place.succ())
            if 3 <= s <= nz + 1:
                t = s - 2
                mine["z", t].wait_recv()
                add_to(ring.at[t - 1], part(t + 1))
                if t < nz - 1:
                    mine["z", t + 1] = put(i, 2 * nz + t + 1, ring.at[t - 1], ring.at[t], place.succ())
                else:
                    there = 1 - getattr(place, third)
                    mine["l"] = put(i, 3 * nz + 1, ring.at[t - 1, there], late, place.other(third))
            if s == nz + 2:
                mine["l"].wait_recv()
                outs[i][...] = wide(ring[nz - 2, getattr(place, third)]) + wide(late[...])
        else:
            if 2 <= s <= nz + 1:
                k = s - 1
                mine["l", k] = put(i, 3 * nz + k, part(k, 0, 1), late.at[k - 1], place.other(second))
            if 3 <= s <= nz + 2:
                k = s - 2
                mine["l", k].wait_recv()
                add_to(part(k, 0, 0), late.at[k - 1])
                if k == 1:
                    mine["z", 1] = put(i, 2 * nz + 1, part(1, 0, 0), ring.at[0], place.succ())
                else:
                    t = k - 1
                    mine["z", t].wait_recv()
                    if t < nz - 1:
                        add_to(ring.at[t - 1], part(t + 1, 0, 0))
                        mine["z", t + 1] = put(i, 2 * nz + t + 1, ring.at[t - 1], ring.at[t], place.succ())
                    else:
                        outs[i][...] = wide(ring[t - 1]) + wide(part(nz, 0, 0)[...])

    stages_of = nz + 3
    for t in range(stages_of + n - 1):
        for i in range(n):
            if 0 <= t - i < stages_of:
                stage(i, t - i)
    for copy in started:
        copy.wait_send()


def scatter_all(grads, orders, mesh):
    nx, ndp = mesh.shape["segment"], mesh.shape["dp"]
    if nx != 2 or ndp != 16:
        return [wide(lax.psum_scatter(g, AXES, scatter_dimension=0, tiled=False)) for g in grads]
    nz, n = ndp // 4, len(grads)

    def scratch(lead):
        return [pltpu.VMEM(lead(o) + g.shape[1:], g.dtype) for o, g in zip(orders, grads)]

    slots = 4 * nz + 2
    return pl.pallas_call(
        functools.partial(scatter_kernel, orders, nz),
        out_shape=[jax.ShapeDtypeStruct(g.shape[1:], jnp.float32) for g in grads],
        in_specs=[pl.BlockSpec(memory_space=pl.ANY)] * n,
        out_specs=[pl.BlockSpec(memory_space=pltpu.VMEM)] * n,
        scratch_shapes=scratch(lambda o: (nz, 2, 2))
        + scratch(lambda o: (2, 2, 2))
        + scratch(lambda o: (nz, 2))
        + scratch(lambda o: (nz - 1, 2) if o[1] == "z" else (nz - 1,))
        + scratch(lambda o: () if o[1] == "z" else (nz,))
        + [
            pltpu.SemaphoreType.DMA((n, slots)),
            pltpu.SemaphoreType.DMA((n, slots)),
            pltpu.SemaphoreType.DMA((n, 2)),
        ],
        compiler_params=pltpu.CompilerParams(
            collective_id=1, has_side_effects=True, vmem_limit_bytes=62 * 2**20
        ),
        name="sum_gradients",
    )(*[g.reshape((2, nz, 2, 2) + g.shape[1:]) for g in grads])


ROWS = 256
GAIN1, BIAS1, VALUE_B, OUT_B, GAIN2, BIAS2, OUTER_B, FIRST_B = range(8)


def chunks(rows, size=ROWS):
    return [slice(at, at + size) for at in range(0, rows, size)]


def norm_parts(rows):
    centre = rows - jnp.mean(rows, axis=-1, keepdims=True)
    inv = lax.rsqrt(jnp.mean(centre * centre, axis=-1, keepdims=True) + EPSILON)
    return centre * inv, inv


def row_loop(rows, body, init):
    return lax.fori_loop(0, rows // 128, lambda j, c: body(pl.ds(pl.multiple_of(j * 128, 128), 128), c), init)


def norm_into(read, write, gain, shift, rows):
    def body(r, carry):
        write[r, :] = half(norm_parts(read(r))[0] * gain + shift)
        return carry

    row_loop(rows, body, 0)


def norm_back(read, grad, gain, rows, done):
    def body(r, carry):
        normal, inv = norm_parts(read(r))
        m_hat = grad(r)
        m = m_hat * gain
        part = inv * (
            m - jnp.mean(m, axis=-1, keepdims=True) - normal * jnp.mean(m * normal, axis=-1, keepdims=True)
        )
        done(r, part)
        return carry[0] + sums(m_hat * normal), carry[1] + sums(m_hat)

    zero = jnp.zeros_like(gain)
    return row_loop(rows, body, (zero, zero))


def sums(value):
    return jnp.sum(wide(value), axis=0, keepdims=True)


def gelu_both(t):
    square = t * t
    s = 0.5 + 0.5 * jnp.tanh(t * (GELU_SCALE + GELU_SCALE * 0.044715 * square))
    value = t * s
    slope = s + value * (1.0 - s) * (2 * GELU_SCALE + 6 * GELU_SCALE * 0.044715 * square)
    return value, slope


def forward_kernel(dense, pairs, parts, length_ref, x_ref, vec_ref, value_ref, out_ref, *refs):
    if dense:
        first_ref, first_b, second_ref, second_b, *refs = refs
        inner_ref, inner_b, outer_ref, y_ref, a_ref, v_ref, probs_ref, c_ref, hid_ref, b_ref, q_ref, slope_ref, *refs = refs
        p_ref, first_slope, acc = refs
    else:
        table_ref, *refs = refs
        inner_ref, inner_b, outer_ref, y_ref, a_ref, v_ref, probs_ref, c_ref, hid_ref, b_ref, q_ref, slope_ref, acc = refs
    i = pl.program_id(0)
    rows, width = x_ref.shape
    head = width // HEADS

    def vec(k):
        return vec_ref[0, k : k + 1, :]

    @pl.when(i == 0)
    def _():
        norm_into(lambda r: wide(x_ref[r, :]), a_ref, vec(GAIN1), vec(BIAS1), rows)
        for r in chunks(rows):
            v_ref[r] = half(mm(a_ref[r], value_ref[0]) + vec(VALUE_B))
            if dense:
                value, slope = gelu_both(mm(a_ref[r], first_ref[...]) + first_b[...])
                p_ref[r] = half(value)
                first_slope[r] = half(slope)

    @pl.when(i < pairs)
    def _():
        at = pl.ds(pl.multiple_of(i * 2 * head, 2 * head), 2 * head)
        v = v_ref[:, at]
        slots = probs_ref.shape[2]
        hidden_keys = lax.broadcasted_iota(jnp.int32, (1, slots), 1) >= length_ref[0]
        shut = jnp.where(hidden_keys, -1e30, 0.0)
        lower = lax.broadcasted_iota(jnp.int32, (1, 2 * head), 1) < head
        for r in chunks(rows):
            mixed = []
            for h in range(2):
                if dense:
                    cols = slice(h * slots, (h + 1) * slots)
                    logits = mm(p_ref[r], second_ref[:, cols]) + jnp.where(hidden_keys, -1e30, second_b[:, cols])
                else:
                    logits = wide(table_ref[h * slots + r.start : h * slots + r.stop, :]) + shut
                expo = jnp.exp(logits - jnp.max(logits, axis=1, keepdims=True))
                probs = half(expo * (1.0 / jnp.sum(expo, axis=1, keepdims=True)))
                probs_ref[h, r] = probs
                mixed.append(mm(probs, v))
            c_ref[r, at] = half(jnp.where(lower, mixed[0], mixed[1]))

    @pl.when(i == pairs - 1)
    def _():
        for r in chunks(rows):
            hid_ref[r] = wide(x_ref[r]) + mm(c_ref[r], out_ref[0]) + vec(OUT_B)
        norm_into(lambda r: hid_ref[r, :], b_ref, vec(GAIN2), vec(BIAS2), rows)

    @pl.when(i >= pairs)
    def _():
        for r in chunks(rows):
            value, slope = gelu_both(mm(b_ref[r], inner_ref[0]) + inner_b[0])
            q = half(value)
            q_ref[r] = q
            slope_ref[r] = half(slope)
            more = mm(q, outer_ref[0])

            @pl.when(i == pairs)
            def _():
                acc[r] = more

            @pl.when(i > pairs)
            def _():
                acc[r] += more

    @pl.when(i == pairs + parts - 1)
    def _():
        for r in chunks(rows):
            y_ref[r] = half(hid_ref[r] + acc[r] + vec(OUTER_B))


def backward_kernel(dense, layer, pairs, parts, *refs):
    g_ref, x_ref, hid_ref, b_ref, c_ref, a_ref, v_ref, q_ref, slope_ref, probs_ref, vec_ref, *refs = refs
    inner_ref, outer_ref, out_ref, value_ref, *refs = refs
    if dense:
        p_ref, first_slope, first_ref, second_ref, *refs = refs
    if layer == 0:
        refs = refs[6:]
    gx_ref, g_outer, g_inner, g_out, g_value, g_vec, g_inner_b, *refs = refs
    if dense:
        g_first, g_second, g_second_b, *refs = refs
    else:
        g_table, *refs = refs
    acc, ghid, gatt, gc_ref, gv_ref, db, *refs = refs
    i = pl.program_id(0)
    rows, width = x_ref.shape
    head = width // HEADS

    def vec(k):
        return vec_ref[0, k : k + 1, :]

    def put(k, value):
        g_vec[0, k : k + 1, :] = value

    @pl.when(i < parts)
    def _():
        gy = g_ref[...]
        for r in chunks(rows):
            gz = half(mm_nt(g_ref[r], outer_ref[0]) * wide(slope_ref[r]))
            db[0, r] = gz
            more = mm_nt(gz, inner_ref[0])

            @pl.when(i == 0)
            def _():
                acc[r] = more

            @pl.when(i > 0)
            def _():
                acc[r] += more

        gz = db[0]
        g_outer[0] = half(mm_tn(q_ref[...], gy))
        g_inner[0] = half(mm_tn(b_ref[...], gz))
        g_inner_b[0] = sums(gz)

    @pl.when(i == parts - 1)
    def _():
        def done(r, part):
            total = wide(g_ref[r, :]) + part
            ghid[r, :] = total
            gatt[r, :] = half(total)

        gain, shift = norm_back(lambda r: hid_ref[r, :], lambda r: acc[r, :], vec(GAIN2), rows, done)
        put(GAIN2, gain)
        put(BIAS2, shift)
        put(OUTER_B, sums(g_ref[...]))
        put(OUT_B, sums(gatt[...]))
        g_out[0] = half(mm_tn(c_ref[...], gatt[...]))
        for r in chunks(rows):
            gc_ref[r] = half(mm_nt(gatt[r], out_ref[0]))

    @pl.when(i >= parts)
    def _():
        at = pl.ds(pl.multiple_of((i - parts) * 2 * head, 2 * head), 2 * head)
        slots = probs_ref.shape[2]
        lower = lax.broadcasted_iota(jnp.int32, (1, 2 * head), 1) < head
        v, gc = v_ref[:, at], gc_ref[:, at]
        values = []
        for h in range(2):
            mine = lower if h == 0 else jnp.logical_not(lower)
            v_own = jnp.where(mine, v, jnp.zeros_like(v))
            cols = slice(h * slots, (h + 1) * slots)
            for r in chunks(rows):
                probs = wide(probs_ref[h, r])
                weighed = probs * mm_nt(gc_ref[r, at], v_own)
                grad = half(weighed - probs * jnp.sum(weighed, axis=1, keepdims=True))
                db[h, r] = grad
                if not dense:
                    g_table[h * slots + r.start : h * slots + r.stop, :] = grad
            values.append(mm_tn(probs_ref[h], gc))
            if dense:
                grad = db[h]
                g_second[:, cols] = half(mm_tn(p_ref[...], grad))
                g_second_b[:, cols] = sums(grad)
                for r in chunks(rows):
                    more = mm_nt(db[h, r], second_ref[:, cols])
                    if h == 0:

                        @pl.when(i == parts)
                        def _():
                            acc[r] = more

                        @pl.when(i > parts)
                        def _():
                            acc[r] += more

                    else:
                        acc[r] += more
        gv_ref[:, at] = half(jnp.where(lower, values[0], values[1]))

    @pl.when(i == pairs + parts - 1)
    def _():
        gv = gv_ref[...]
        put(VALUE_B, sums(gv))
        g_value[0] = half(mm_tn(a_ref[...], gv))
        if dense:
            for r in chunks(rows):
                gatt[r] = half(acc[r] * wide(first_slope[r]))
            gf = gatt[...]
            put(FIRST_B, sums(gf))
            g_first[...] = half(mm_tn(a_ref[...], gf))
        else:
            put(FIRST_B, jnp.zeros((1, width), jnp.float32))
        for r in chunks(rows):
            ga = mm_nt(gv_ref[r], value_ref[0])
            if dense:
                ga = ga + mm_nt(gatt[r], first_ref[...])
            acc[r] = ga

        def done(r, part):
            gx_ref[r, :] = half(ghid[r, :] + part)

        gain, shift = norm_back(lambda r: wide(x_ref[r, :]), lambda r: acc[r, :], vec(GAIN1), rows, done)
        put(GAIN1, gain)
        put(BIAS1, shift)


class Weights(NamedTuple):
    vectors: Any
    value: Any
    out: Any
    inner: Any
    inner_b: Any
    outer: Any
    first: Any
    first_b: Any
    second: Any
    second_b: Any
    table: Any


def whole(shape, *at):
    at = tuple(at)
    block = (1,) * len(at) + tuple(shape[len(at) :])
    return pl.BlockSpec(block, lambda i: at + (0,) * (len(shape) - len(at)), pipeline_mode=pl.Buffered(1))


def whole_out(shape, *at):
    at = tuple(at)
    block = (1,) * len(at) + tuple(shape[len(at) :])
    return pl.BlockSpec(block, lambda i: at + (0,) * (len(shape) - len(at)))


class Saved(NamedTuple):
    a: Any
    v: Any
    probs: Any
    c: Any
    hid: Any
    b: Any
    q: Any
    slope: Any
    p: Any = None
    first_slope: Any = None


def sizes_of(x, w):
    rows, width = x.shape
    parts = w.inner.shape[2] // 512
    return rows, width, HEADS // 2, parts, w.inner.shape[2] // parts


def forward(x, length, w, layer):
    dense = layer == 0
    rows, width, pairs, parts, part = sizes_of(x, w)
    slots = rows

    def pair(i):
        return jnp.minimum(i, pairs - 1)

    def piece(i):
        return jnp.maximum(i - pairs, 0)

    ins = [length, x, w.vectors, w.value, w.out]
    specs = [pl.BlockSpec(memory_space=pltpu.SMEM), whole(x.shape), whole(w.vectors.shape, layer)]
    specs += [whole(w.value.shape, layer), whole(w.out.shape, layer)]
    if dense:
        ins += [w.first, w.first_b, w.second, w.second_b]
        specs += [
            whole(w.first.shape),
            whole(w.first_b.shape),
            pl.BlockSpec((width, 2 * slots), lambda i: (0, pair(i))),
            pl.BlockSpec((1, 2 * slots), lambda i: (0, pair(i))),
        ]
    else:
        ins += [w.table]
        specs += [pl.BlockSpec((2 * slots, slots), lambda i: (pair(i), 0))]
    ins += [w.inner, w.inner_b, w.outer]
    specs += [
        pl.BlockSpec((1, width, part), lambda i: (layer, 0, piece(i))),
        pl.BlockSpec((1, 1, part), lambda i: (layer, 0, piece(i))),
        pl.BlockSpec((1, part, width), lambda i: (layer, piece(i), 0)),
    ]
    wide_half = jax.ShapeDtypeStruct((rows, width), jnp.bfloat16)
    hidden = jax.ShapeDtypeStruct((rows, part * parts), jnp.bfloat16)
    outs = [wide_half] * 3 + [jax.ShapeDtypeStruct((2 * pairs, rows, slots), jnp.bfloat16), wide_half]
    outs += [jax.ShapeDtypeStruct((rows, width), jnp.float32), wide_half, hidden, hidden]
    row_block = whole_out((rows, width))
    hidden_block = pl.BlockSpec((rows, part), lambda i: (0, piece(i)))
    out_specs = [row_block] * 3 + [pl.BlockSpec((2, rows, slots), lambda i: (pair(i), 0, 0))]
    out_specs += [row_block] * 3 + [hidden_block] * 2
    if dense:
        outs += [wide_half] * 2
        out_specs += [row_block] * 2
    y, *saved = pl.pallas_call(
        functools.partial(forward_kernel, dense, pairs, parts),
        grid=(pairs + parts,),
        out_shape=outs,
        in_specs=specs,
        out_specs=out_specs,
        scratch_shapes=[pltpu.VMEM((rows, width), jnp.float32)],
        compiler_params=pltpu.CompilerParams(vmem_limit_bytes=56 * 2**20),
        name=f"forward_{layer}",
    )(*ins)
    return y, Saved(*saved)


def backward(g, x, saved, w, layer, before):
    dense = layer == 0
    rows, width, pairs, parts, part = sizes_of(x, w)
    slots = rows

    def pair(i):
        return jnp.maximum(i - parts, 0)

    def piece(i):
        return jnp.minimum(i, parts - 1)

    hidden_block = pl.BlockSpec((rows, part), lambda i: (0, piece(i)))
    ins = [g, x, saved.hid, saved.b, saved.c, saved.a, saved.v, saved.q, saved.slope, saved.probs, w.vectors]
    specs = [whole((rows, width))] * 7 + [hidden_block] * 2
    specs += [pl.BlockSpec((2, rows, slots), lambda i: (pair(i), 0, 0)), whole(w.vectors.shape, layer)]
    ins += [w.inner, w.outer, w.out, w.value]
    inner_block = pl.BlockSpec((1, width, part), lambda i: (layer, 0, piece(i)))
    outer_block = pl.BlockSpec((1, part, width), lambda i: (layer, piece(i), 0))
    specs += [inner_block, outer_block, whole(w.out.shape, layer), whole(w.value.shape, layer)]
    second_block = pl.BlockSpec((width, 2 * slots), lambda i: (0, pair(i)))
    if dense:
        ins += [saved.p, saved.first_slope, w.first, w.second]
        specs += [whole((rows, width))] * 2 + [whole(w.first.shape), second_block]
    aliases = {}
    if before is not None:
        aliases = {len(ins) + j: 1 + j for j in range(6)}
        ins += list(before)
        specs += [pl.BlockSpec(memory_space=pl.ANY)] * 6

    def like(shape, dtype=jnp.bfloat16):
        return jax.ShapeDtypeStruct(shape, dtype)

    outs = [like((rows, width)), like(w.outer.shape), like(w.inner.shape), like(w.out.shape), like(w.value.shape)]
    outs += [like((2, 8, width), jnp.float32), like(w.inner_b.shape, jnp.float32)]
    out_specs = [whole_out((rows, width)), outer_block, inner_block]
    out_specs += [whole_out(w.out.shape, layer), whole_out(w.value.shape, layer), whole_out((2, 8, width), layer)]
    out_specs += [pl.BlockSpec((1, 1, part), lambda i: (layer, 0, piece(i)))]
    if dense:
        outs += [like(w.first.shape), like(w.second.shape), like(w.second_b.shape, jnp.float32)]
        out_specs += [whole_out(w.first.shape), second_block, pl.BlockSpec((1, 2 * slots), lambda i: (0, pair(i)))]
    else:
        outs += [like(w.table.shape)]
        out_specs += [pl.BlockSpec((2 * slots, slots), lambda i: (pair(i), 0))]
    gx, *grads = pl.pallas_call(
        functools.partial(backward_kernel, dense, layer, pairs, parts),
        grid=(pairs + parts,),
        out_shape=outs,
        in_specs=specs,
        out_specs=out_specs,
        scratch_shapes=[
            pltpu.VMEM((rows, width), jnp.float32),
            pltpu.VMEM((rows, width), jnp.float32),
            pltpu.VMEM((rows, width), jnp.bfloat16),
            pltpu.VMEM((rows, width), jnp.bfloat16),
            pltpu.VMEM((rows, width), jnp.bfloat16),
            pltpu.VMEM((2, rows, slots), jnp.bfloat16),
        ],
        input_output_aliases=aliases,
        compiler_params=pltpu.CompilerParams(vmem_limit_bytes=60 * 2**20),
        name=f"backward_{layer}",
    )(*ins)
    return gx, grads[:6], grads[6:]


MATRICES = (2, 8, 10, 14, 16, 4, 12)
ROW_VECTORS = (0, 1, 3, 5, 6, 7, 11)
VECTORS = ROW_VECTORS + (9, 13, 15)
ORDERS = ("zxy", "zxy", "xzy", "yzx", "yzx", "zxy", "yzx", "xzy")
SUM_ORDERS = tuple(o[::-1] for o in ORDERS)


def per_device(mesh, boundary, lengths, *parts):
    nx, ndp = mesh.shape["segment"], mesh.shape["dp"]
    devices = nx * ndp
    first = lax.axis_index("segment") == 0
    swap = [(0, 1), (1, 0)]
    own = boundary[0, :, 0]
    received = lax.ppermute(jnp.where(first, own[1], own[0]), "segment", swap)
    rows = jnp.where(first, own[0], received)
    cotangent = jnp.where(first, received, own[1])
    length = jnp.where(first, lengths[0], lengths[1])

    flat = jnp.concatenate([parts[k].reshape(-1) for k in VECTORS])
    sizes = [parts[k].size for k in VECTORS]
    lanes = -(-flat.size // 2048) * 16
    packed = half(jnp.pad(flat, (0, lanes * 128 - flat.size)).reshape(lanes, 128))
    shards = [half(parts[k].reshape(parts[k].shape[-2:])) for k in MATRICES] + [packed]
    gathered = gather_all(shards, ORDERS, mesh)

    full = {}
    for k, g in zip(MATRICES, gathered):
        full[k] = g.reshape((nx, ndp * g.shape[1]) + g.shape[2:]) if k < 12 else g.reshape(-1, g.shape[2])
    vec = wide(gathered[-1].reshape(devices, lanes * 128))
    count, size = len(ROW_VECTORS), sizes[0]
    bounds = [count * size]
    for k in VECTORS[count:]:
        bounds.append(bounds[-1] + parts[k].size)
    vectors = vec[:, : bounds[0]].reshape(nx, ndp, count, size).transpose(0, 2, 1, 3).reshape(nx, count, -1)
    inner_b, first_b, second_b = (vec[:, lo:hi] for lo, hi in zip(bounds, bounds[1:]))
    w = Weights(
        vectors,
        full[2],
        full[4],
        full[8],
        inner_b.reshape(nx, 1, -1),
        full[10],
        full[12],
        first_b.reshape(1, -1),
        full[14],
        second_b.reshape(1, -1),
        full[16],
    )

    out0, saved0 = forward(rows, length, w, 0)
    out1, saved1 = forward(out0, length, w, 1)
    gin1, both, synth1 = backward(cotangent, out0, saved1, w, 1, None)
    gin0, both, synth0 = backward(gin1, rows, saved0, w, 0, both)

    def swapped(for_first, for_second):
        got = lax.ppermute(jnp.where(first, for_second, for_first), "segment", swap)
        return jnp.stack([jnp.where(first, for_first, got), jnp.where(first, got, for_second)])[None, :, None]

    layer_outputs = swapped(out0, out1)
    input_grads = swapped(gin0, gin1)

    g_outer, g_inner, g_out, g_value, g_vec, g_inner_b = both
    g_first, g_second, g_second_b = synth0
    matrices = (g_value, g_inner, g_outer, g_second, synth1[0], g_out, g_first)
    lists = [g.reshape((devices,) + parts[k].shape[-2:]) for k, g in zip(MATRICES, matrices)]
    vec = [g_vec[:, :count].reshape(nx, count, ndp, size).transpose(0, 2, 1, 3).reshape(devices, count * size)]
    vec += [g.reshape(devices, -1) for g in (g_inner_b, g_vec[0, FIRST_B], g_second_b)]
    vec = jnp.concatenate(vec, axis=1)
    vec = jnp.pad(vec, ((0, 0), (0, lanes * 128 - vec.shape[1]))).reshape(devices, lanes, 128)
    summed = scatter_all(lists + [vec], SUM_ORDERS, mesh)
    result = {k: g.reshape(parts[k].shape) for k, g in zip(MATRICES, summed)}
    vec = summed[-1].reshape(-1)
    at = 0
    for k, size in zip(VECTORS, sizes):
        result[k] = vec[at : at + size].reshape(parts[k].shape)
        at += size
    return (layer_outputs, input_grads) + tuple(result[k] for k in range(17))


def solution(mesh):
    layer = [P("segment", "dp")] * 12
    layer[2] = layer[4] = layer[8] = layer[10] = P("segment", "dp", None)
    both = P(AXES)
    rows = P(AXES, None)
    boundary = P("segment", None, "dp", None, None)
    weights = tuple(layer) + (rows, both, rows, both, rows)
    return jax.shard_map(
        functools.partial(per_device, mesh),
        mesh=mesh,
        in_specs=(boundary, P(None, "dp")) + weights,
        out_specs=(boundary, boundary) + weights,
        check_vma=False,
    )
```

```python
import functools
import math
from typing import Any, NamedTuple

import jax
import jax.numpy as jnp
from jax import lax
from jax.experimental import pallas as pl
from jax.experimental.pallas import tpu as pltpu
from jax.sharding import PartitionSpec as P

MESH = pl.DeviceIdType.MESH
HEADS = 12
EPSILON = 1e-05
GELU_SCALE = 0.7978845608028654
AXES = ("segment", "dp")


def half(value):
    return value.astype(jnp.bfloat16)


def wide(value):
    return value.astype(jnp.float32)


def mm(left, right):
    return jnp.dot(left, right, preferred_element_type=jnp.float32)


def mm_tn(left, right):
    return lax.dot_general(left, right, (((0,), (0,)), ((), ())), preferred_element_type=jnp.float32)


def mm_nt(left, right):
    return lax.dot_general(left, right, (((1,), (1,)), ((), ())), preferred_element_type=jnp.float32)


class Place:
    def __init__(self, nz):
        self.nz = nz
        self.x = lax.axis_index("segment")
        d = lax.axis_index("dp")
        self.c = d % 2
        self.y = (d // 2) % 2
        self.z = d // 4
        par = self.z % 2
        self.q = par * ((self.z + 1) // 2) + (1 - par) * ((nz - self.z // 2) % nz)

    def z_at(self, q):
        nz = self.nz
        upper = ((q + nz - 1) % nz) // (nz // 2)
        return (1 - upper) * (2 * q - 1) + upper * ((2 * (nz - q)) % (2 * nz))

    def ring_z(self, back):
        return self.z_at((self.q + 2 * self.nz - back) % self.nz)

    def device(self, x=None, z=None, y=None, c=None):
        x = self.x if x is None else x
        z = self.z if z is None else z
        y = self.y if y is None else y
        c = self.c if c is None else c
        return (x, (z * 2 + y) * 2 + c)

    def other(self, axis):
        return self.device(**{axis: 1 - getattr(self, axis)})

    def succ(self):
        return self.device(z=self.z_at((self.q + 1) % self.nz))

    def pred(self):
        return self.device(z=self.ring_z(1))


def greet(place):
    barrier = pltpu.get_barrier_semaphore()
    peers = [place.other("x"), place.other("y"), place.other("c"), place.succ(), place.pred()]
    for peer in peers:
        pl.semaphore_signal(barrier, inc=1, device_id=peer, device_id_type=MESH)
    pl.semaphore_wait(barrier, len(peers))


def block_of(ref, place, c, z, x=None, y=None):
    xs = pl.ds(0, 2) if x is None else x
    ys = pl.ds(0, 2) if y is None else y
    return ref.at[xs, z, ys, c]


def gather_kernel(plan, nz, *refs):
    orders, starts = zip(*plan)
    n = len(orders)
    ins, outs = refs[:n], refs[n : 2 * n]
    send, recv, local = refs[2 * n :]
    place = Place(nz)
    greet(place)
    started = []

    def put(i, k, src, dst, device):
        copy = pltpu.make_async_remote_copy(
            src_ref=src,
            dst_ref=dst,
            send_sem=send.at[i, k],
            recv_sem=recv.at[i, k],
            device_id=device,
            device_id_type=MESH,
        )
        copy.start()
        started.append(copy)
        return copy

    copies = [dict() for _ in orders]

    def stage(i, t):
        first, second, third = orders[i]
        out, mine = outs[i], copies[i]

        def shard(z, **at):
            return block_of(out, place, place.c, z, **at)

        def own(axis, z):
            return shard(z, **{axis: getattr(place, axis)})

        one = shard(place.z, x=place.x, y=place.y)
        if t == 0:
            mine["own"] = pltpu.make_async_copy(ins[i], one, local.at[i])
            mine["own"].start()
        if second == "z":
            if t == 0:
                mine["p"] = put(i, 0, ins[i], one, place.other(first))
                return
            if t == 1:
                mine["own"].wait()
                mine["p"].wait_recv()
            elif t <= nz:
                mine["z", t - 1].wait_recv()
            if t <= nz:
                z = place.ring_z(t - 1)
                block = own(third, z)
                if t < nz:
                    mine["z", t] = put(i, t, block, block, place.succ())
                mine["l", t] = put(i, nz + t, block, block, place.other(third))
                mine["c", t] = put(i, 2 * nz + t, block, block, place.other("c"))
            if t >= 2:
                mine["l", t - 1].wait_recv()
                z = place.ring_z(t - 2)
                block = shard(z, **{third: 1 - getattr(place, third)})
                mine["d", t - 1] = put(i, 3 * nz + t - 1, block, block, place.other("c"))
        else:
            if t <= nz - 1:
                if t > 0:
                    mine["z", t].wait_recv()
                z = place.ring_z(t)
                src = ins[i] if t == 0 else shard(z, x=place.x, y=place.y)
                dst = shard(z, x=place.x, y=place.y)
                if t < nz - 1:
                    mine["z", t + 1] = put(i, t, src, dst, place.succ())
                mine["p", t + 1] = put(i, nz + t, src, dst, place.other(second))
            if 1 <= t <= nz:
                if t == 1:
                    mine["own"].wait()
                mine["p", t].wait_recv()
                block = own(third, place.ring_z(t - 1))
                mine["l", t] = put(i, 2 * nz + t, block, block, place.other(third))
                mine["c", t] = put(i, 3 * nz + t, block, block, place.other("c"))
            if t >= 2:
                mine["l", t - 1].wait_recv()
                block = shard(place.ring_z(t - 2), **{third: 1 - getattr(place, third)})
                mine["d", t - 1] = put(i, 4 * nz + t - 1, block, block, place.other("c"))

    stages = nz + 2
    for t in range(stages + max(starts)):
        for i in range(n):
            if 0 <= t - starts[i] < stages:
                stage(i, t - starts[i])
    for mine in copies:
        for key, copy in mine.items():
            if key[0] in "cd":
                copy.wait_recv()
    for copy in started:
        copy.wait_send()


def gather_all(shards, plan, mesh):
    nx, ndp = mesh.shape["segment"], mesh.shape["dp"]
    if nx != 2 or ndp % 8:
        return [lax.all_gather(s, AXES, axis=0) for s in shards]
    nz, n = ndp // 4, len(shards)
    slots = 5 * nz + 2
    outs = pl.pallas_call(
        functools.partial(gather_kernel, plan, nz),
        out_shape=[jax.ShapeDtypeStruct((2, nz, 2, 2) + s.shape, s.dtype) for s in shards],
        in_specs=[pl.BlockSpec(memory_space=pl.ANY)] * n,
        out_specs=[pl.BlockSpec(memory_space=pl.ANY)] * n,
        scratch_shapes=[
            pltpu.SemaphoreType.DMA((n, slots)),
            pltpu.SemaphoreType.DMA((n, slots)),
            pltpu.SemaphoreType.DMA((n,)),
        ],
        compiler_params=pltpu.CompilerParams(collective_id=0, has_side_effects=True),
        name="gather_weights",
    )(*shards)
    return [o.reshape((nx * ndp,) + s.shape) for o, s in zip(outs, shards)]


def add_to(dst, src):
    lead = dst.shape[:-2]

    def one(j, carry):
        at = (j // 2, j % 2) if len(lead) == 2 else (j,)[: len(lead)]
        at = at + (slice(None), slice(None))
        dst[at] = dst[at] + src[at]
        return carry

    if lead:
        lax.fori_loop(0, math.prod(lead), one, 0)
    else:
        dst[...] = dst[...] + src[...]


def scatter_kernel(plan, nz, *refs):
    orders, starts = zip(*plan)
    n = len(orders)
    ins, outs = refs[:n], refs[n : 2 * n]
    accs, stages, firsts, rings, lasts = (refs[(2 + j) * n : (3 + j) * n] for j in range(5))
    send, recv, local = refs[7 * n :]
    place = Place(nz)
    greet(place)
    started = []

    def put(i, k, src, dst, device):
        copy = pltpu.make_async_remote_copy(
            src_ref=src,
            dst_ref=dst,
            send_sem=send.at[i, k],
            recv_sem=recv.at[i, k],
            device_id=device,
            device_id_type=MESH,
        )
        copy.start()
        started.append(copy)
        return copy

    live = [dict() for _ in orders]

    def load(i, k):
        copy = pltpu.make_async_copy(
            block_of(ins[i], place, place.c, place.ring_z(k)), stages[i].at[k % 2], local.at[i, k % 2]
        )
        copy.start()
        live[i]["o", k] = copy

    def stage(i, s):
        first, second, third = orders[i]
        acc, mine = accs[i], live[i]
        early, ring, late = firsts[i], rings[i], lasts[i]

        def part(k, flip=0, flip2=None):
            own = {axis: getattr(place, axis) for axis in "xy"}
            own[first] = own[first] + flip * (1 - 2 * own[first])
            if flip2 is None:
                own["xy".replace(first, "")] = pl.ds(0, 2)
            else:
                other = "xy".replace(first, "")
                own[other] = own[other] + flip2 * (1 - 2 * own[other])
            return acc.at[k - 1, own["x"], own["y"]]

        if s == 0:
            for k in range(1, nz + 1):
                src = block_of(ins[i], place, 1 - place.c, place.ring_z(k))
                mine["c", k] = put(i, k, src, acc.at[k - 1], place.other("c"))
            load(i, 1)
            load(i, 2)
        if 1 <= s <= nz:
            k = s
            mine["c", k].wait_recv()
            mine["o", k].wait()
            add_to(acc.at[k - 1], stages[i].at[k % 2])
            if k + 2 <= nz:
                load(i, k + 2)
            mine["p", k] = put(i, nz + k, part(k, 1), early.at[k - 1], place.other(first))
        if 2 <= s <= nz + 1:
            k = s - 1
            mine["p", k].wait_recv()
            add_to(part(k), early.at[k - 1])
        if second == "z":
            if s == 2:
                mine["z", 1] = put(i, 2 * nz + 1, part(1), ring.at[0], place.succ())
            if 3 <= s <= nz + 1:
                t = s - 2
                mine["z", t].wait_recv()
                add_to(ring.at[t - 1], part(t + 1))
                if t < nz - 1:
                    mine["z", t + 1] = put(i, 2 * nz + t + 1, ring.at[t - 1], ring.at[t], place.succ())
                else:
                    there = 1 - getattr(place, third)
                    mine["l"] = put(i, 3 * nz + 1, ring.at[t - 1, there], late, place.other(third))
            if s == nz + 2:
                mine["l"].wait_recv()
                outs[i][...] = wide(ring[nz - 2, getattr(place, third)]) + wide(late[...])
        else:
            if 2 <= s <= nz + 1:
                k = s - 1
                mine["l", k] = put(i, 3 * nz + k, part(k, 0, 1), late.at[k - 1], place.other(second))
            if 3 <= s <= nz + 2:
                k = s - 2
                mine["l", k].wait_recv()
                add_to(part(k, 0, 0), late.at[k - 1])
                if k == 1:
                    mine["z", 1] = put(i, 2 * nz + 1, part(1, 0, 0), ring.at[0], place.succ())
                else:
                    t = k - 1
                    mine["z", t].wait_recv()
                    if t < nz - 1:
                        add_to(ring.at[t - 1], part(t + 1, 0, 0))
                        mine["z", t + 1] = put(i, 2 * nz + t + 1, ring.at[t - 1], ring.at[t], place.succ())
                    else:
                        outs[i][...] = wide(ring[t - 1]) + wide(part(nz, 0, 0)[...])

    stages_of = nz + 3
    for t in range(stages_of + max(starts)):
        for i in range(n):
            if 0 <= t - starts[i] < stages_of:
                stage(i, t - starts[i])
    for copy in started:
        copy.wait_send()


def scatter_all(grads, plan, mesh):
    nx, ndp = mesh.shape["segment"], mesh.shape["dp"]
    if nx != 2 or ndp != 16:
        return [wide(lax.psum_scatter(g, AXES, scatter_dimension=0, tiled=False)) for g in grads]
    nz, n = ndp // 4, len(grads)

    def scratch(lead):
        return [pltpu.VMEM(lead(o) + g.shape[1:], g.dtype) for (o, _), g in zip(plan, grads)]

    slots = 4 * nz + 2
    return pl.pallas_call(
        functools.partial(scatter_kernel, plan, nz),
        out_shape=[jax.ShapeDtypeStruct(g.shape[1:], jnp.float32) for g in grads],
        in_specs=[pl.BlockSpec(memory_space=pl.ANY)] * n,
        out_specs=[pl.BlockSpec(memory_space=pltpu.VMEM)] * n,
        scratch_shapes=scratch(lambda o: (nz, 2, 2))
        + scratch(lambda o: (2, 2, 2))
        + scratch(lambda o: (nz, 2))
        + scratch(lambda o: (nz - 1, 2) if o[1] == "z" else (nz - 1,))
        + scratch(lambda o: () if o[1] == "z" else (nz,))
        + [
            pltpu.SemaphoreType.DMA((n, slots)),
            pltpu.SemaphoreType.DMA((n, slots)),
            pltpu.SemaphoreType.DMA((n, 2)),
        ],
        compiler_params=pltpu.CompilerParams(
            collective_id=1, has_side_effects=True, vmem_limit_bytes=62 * 2**20
        ),
        name="sum_gradients",
    )(*[g.reshape((2, nz, 2, 2) + g.shape[1:]) for g in grads])


ROWS = 256
GAIN1, BIAS1, VALUE_B, OUT_B, GAIN2, BIAS2, OUTER_B, FIRST_B = range(8)


def chunks(rows, size=ROWS):
    return [slice(at, at + size) for at in range(0, rows, size)]


def norm_parts(rows):
    centre = rows - jnp.mean(rows, axis=-1, keepdims=True)
    inv = lax.rsqrt(jnp.mean(centre * centre, axis=-1, keepdims=True) + EPSILON)
    return centre * inv, inv


def row_loop(rows, body, init):
    return lax.fori_loop(0, rows // 128, lambda j, c: body(pl.ds(pl.multiple_of(j * 128, 128), 128), c), init)


def norm_into(read, write, gain, shift, rows):
    def body(r, carry):
        write[r, :] = half(norm_parts(read(r))[0] * gain + shift)
        return carry

    row_loop(rows, body, 0)


def norm_back(read, grad, gain, rows, done):
    def body(r, carry):
        normal, inv = norm_parts(read(r))
        m_hat = grad(r)
        m = m_hat * gain
        part = inv * (
            m - jnp.mean(m, axis=-1, keepdims=True) - normal * jnp.mean(m * normal, axis=-1, keepdims=True)
        )
        done(r, part)
        return carry[0] + sums(m_hat * normal), carry[1] + sums(m_hat)

    zero = jnp.zeros_like(gain)
    return row_loop(rows, body, (zero, zero))


def sums(value):
    return jnp.sum(wide(value), axis=0, keepdims=True)


def gelu_both(t):
    square = t * t
    s = 0.5 + 0.5 * jnp.tanh(t * (GELU_SCALE + GELU_SCALE * 0.044715 * square))
    value = t * s
    slope = s + value * (1.0 - s) * (2 * GELU_SCALE + 6 * GELU_SCALE * 0.044715 * square)
    return value, slope


def forward_kernel(dense, pairs, parts, length_ref, x_ref, vec_ref, value_ref, out_ref, *refs):
    if dense:
        first_ref, first_b, second_ref, second_b, *refs = refs
        inner_ref, inner_b, outer_ref, y_ref, a_ref, v_ref, probs_ref, c_ref, hid_ref, b_ref, q_ref, slope_ref, *refs = refs
        p_ref, first_slope, acc = refs
    else:
        table_ref, *refs = refs
        inner_ref, inner_b, outer_ref, y_ref, a_ref, v_ref, probs_ref, c_ref, hid_ref, b_ref, q_ref, slope_ref, acc = refs
    i = pl.program_id(0)
    rows, width = x_ref.shape
    head = width // HEADS

    def vec(k):
        return vec_ref[0, k : k + 1, :]

    @pl.when(i == 0)
    def _():
        norm_into(lambda r: wide(x_ref[r, :]), a_ref, vec(GAIN1), vec(BIAS1), rows)
        for r in chunks(rows):
            v_ref[r] = half(mm(a_ref[r], value_ref[0]) + vec(VALUE_B))
            if dense:
                value, slope = gelu_both(mm(a_ref[r], first_ref[...]) + first_b[...])
                p_ref[r] = half(value)
                first_slope[r] = half(slope)

    @pl.when(i < pairs)
    def _():
        at = pl.ds(pl.multiple_of(i * 2 * head, 2 * head), 2 * head)
        v = v_ref[:, at]
        slots = probs_ref.shape[2]
        hidden_keys = lax.broadcasted_iota(jnp.int32, (1, slots), 1) >= length_ref[0]
        shut = jnp.where(hidden_keys, -1e30, 0.0)
        lower = lax.broadcasted_iota(jnp.int32, (1, 2 * head), 1) < head
        for r in chunks(rows):
            mixed = []
            for h in range(2):
                if dense:
                    cols = slice(h * slots, (h + 1) * slots)
                    logits = mm(p_ref[r], second_ref[:, cols]) + jnp.where(hidden_keys, -1e30, second_b[:, cols])
                else:
                    logits = wide(table_ref[h * slots + r.start : h * slots + r.stop, :]) + shut
                expo = jnp.exp(logits - jnp.max(logits, axis=1, keepdims=True))
                probs = half(expo * (1.0 / jnp.sum(expo, axis=1, keepdims=True)))
                probs_ref[h, r] = probs
                mixed.append(mm(probs, v))
            c_ref[r, at] = half(jnp.where(lower, mixed[0], mixed[1]))

    @pl.when(i == pairs - 1)
    def _():
        for r in chunks(rows):
            hid_ref[r] = wide(x_ref[r]) + mm(c_ref[r], out_ref[0]) + vec(OUT_B)
        norm_into(lambda r: hid_ref[r, :], b_ref, vec(GAIN2), vec(BIAS2), rows)

    @pl.when(i >= pairs)
    def _():
        for r in chunks(rows):
            value, slope = gelu_both(mm(b_ref[r], inner_ref[0]) + inner_b[0])
            q = half(value)
            q_ref[r] = q
            slope_ref[r] = half(slope)
            more = mm(q, outer_ref[0])

            @pl.when(i == pairs)
            def _():
                acc[r] = more

            @pl.when(i > pairs)
            def _():
                acc[r] += more

    @pl.when(i == pairs + parts - 1)
    def _():
        for r in chunks(rows):
            y_ref[r] = half(hid_ref[r] + acc[r] + vec(OUTER_B))


def backward_kernel(dense, layer, pairs, parts, *refs):
    g_ref, x_ref, hid_ref, b_ref, c_ref, a_ref, v_ref, q_ref, slope_ref, probs_ref, vec_ref, *refs = refs
    inner_ref, outer_ref, out_ref, value_ref, *refs = refs
    if dense:
        p_ref, first_slope, first_ref, second_ref, *refs = refs
    if layer == 0:
        refs = refs[6:]
    gx_ref, g_outer, g_inner, g_out, g_value, g_vec, g_inner_b, *refs = refs
    if dense:
        g_first, g_second, g_second_b, *refs = refs
    else:
        g_table, *refs = refs
    acc, ghid, gatt, gc_ref, gv_ref, db, *refs = refs
    i = pl.program_id(0)
    rows, width = x_ref.shape
    head = width // HEADS

    def vec(k):
        return vec_ref[0, k : k + 1, :]

    def put(k, value):
        g_vec[0, k : k + 1, :] = value

    @pl.when(i < parts)
    def _():
        gy = g_ref[...]
        for r in chunks(rows):
            gz = half(mm_nt(g_ref[r], outer_ref[0]) * wide(slope_ref[r]))
            db[0, r] = gz
            more = mm_nt(gz, inner_ref[0])

            @pl.when(i == 0)
            def _():
                acc[r] = more

            @pl.when(i > 0)
            def _():
                acc[r] += more

        gz = db[0]
        g_outer[0] = half(mm_tn(q_ref[...], gy))
        g_inner[0] = half(mm_tn(b_ref[...], gz))
        g_inner_b[0] = sums(gz)

    @pl.when(i == parts - 1)
    def _():
        def done(r, part):
            total = wide(g_ref[r, :]) + part
            ghid[r, :] = total
            gatt[r, :] = half(total)

        gain, shift = norm_back(lambda r: hid_ref[r, :], lambda r: acc[r, :], vec(GAIN2), rows, done)
        put(GAIN2, gain)
        put(BIAS2, shift)
        put(OUTER_B, sums(g_ref[...]))
        put(OUT_B, sums(gatt[...]))
        g_out[0] = half(mm_tn(c_ref[...], gatt[...]))
        for r in chunks(rows):
            gc_ref[r] = half(mm_nt(gatt[r], out_ref[0]))

    @pl.when(i >= parts)
    def _():
        at = pl.ds(pl.multiple_of((i - parts) * 2 * head, 2 * head), 2 * head)
        slots = probs_ref.shape[2]
        lower = lax.broadcasted_iota(jnp.int32, (1, 2 * head), 1) < head
        v, gc = v_ref[:, at], gc_ref[:, at]
        values = []
        for h in range(2):
            mine = lower if h == 0 else jnp.logical_not(lower)
            v_own = jnp.where(mine, v, jnp.zeros_like(v))
            cols = slice(h * slots, (h + 1) * slots)
            for r in chunks(rows):
                probs = wide(probs_ref[h, r])
                weighed = probs * mm_nt(gc_ref[r, at], v_own)
                grad = half(weighed - probs * jnp.sum(weighed, axis=1, keepdims=True))
                db[h, r] = grad
                if not dense:
                    g_table[h * slots + r.start : h * slots + r.stop, :] = grad
            values.append(mm_tn(probs_ref[h], gc))
            if dense:
                grad = db[h]
                g_second[:, cols] = half(mm_tn(p_ref[...], grad))
                g_second_b[:, cols] = sums(grad)
                for r in chunks(rows):
                    more = mm_nt(db[h, r], second_ref[:, cols])
                    if h == 0:

                        @pl.when(i == parts)
                        def _():
                            acc[r] = more

                        @pl.when(i > parts)
                        def _():
                            acc[r] += more

                    else:
                        acc[r] += more
        gv_ref[:, at] = half(jnp.where(lower, values[0], values[1]))

    @pl.when(i == pairs + parts - 1)
    def _():
        gv = gv_ref[...]
        put(VALUE_B, sums(gv))
        g_value[0] = half(mm_tn(a_ref[...], gv))
        if dense:
            for r in chunks(rows):
                gatt[r] = half(acc[r] * wide(first_slope[r]))
            gf = gatt[...]
            put(FIRST_B, sums(gf))
            g_first[...] = half(mm_tn(a_ref[...], gf))
        else:
            put(FIRST_B, jnp.zeros((1, width), jnp.float32))
        for r in chunks(rows):
            ga = mm_nt(gv_ref[r], value_ref[0])
            if dense:
                ga = ga + mm_nt(gatt[r], first_ref[...])
            acc[r] = ga

        def done(r, part):
            gx_ref[r, :] = half(ghid[r, :] + part)

        gain, shift = norm_back(lambda r: wide(x_ref[r, :]), lambda r: acc[r, :], vec(GAIN1), rows, done)
        put(GAIN1, gain)
        put(BIAS1, shift)


class Weights(NamedTuple):
    vectors: Any
    value: Any
    out: Any
    inner: Any
    inner_b: Any
    outer: Any
    first: Any
    first_b: Any
    second: Any
    second_b: Any
    table: Any


def whole(shape, *at):
    at = tuple(at)
    block = (1,) * len(at) + tuple(shape[len(at) :])
    return pl.BlockSpec(block, lambda i: at + (0,) * (len(shape) - len(at)), pipeline_mode=pl.Buffered(1))


def whole_out(shape, *at):
    at = tuple(at)
    block = (1,) * len(at) + tuple(shape[len(at) :])
    return pl.BlockSpec(block, lambda i: at + (0,) * (len(shape) - len(at)))


class Saved(NamedTuple):
    a: Any
    v: Any
    probs: Any
    c: Any
    hid: Any
    b: Any
    q: Any
    slope: Any
    p: Any = None
    first_slope: Any = None


def sizes_of(x, w):
    rows, width = x.shape
    parts = w.inner.shape[2] // 512
    return rows, width, HEADS // 2, parts, w.inner.shape[2] // parts


def forward(x, length, w, layer):
    dense = layer == 0
    rows, width, pairs, parts, part = sizes_of(x, w)
    slots = rows

    def pair(i):
        return jnp.minimum(i, pairs - 1)

    def piece(i):
        return jnp.maximum(i - pairs, 0)

    ins = [length, x, w.vectors, w.value, w.out]
    specs = [pl.BlockSpec(memory_space=pltpu.SMEM), whole(x.shape), whole(w.vectors.shape, layer)]
    specs += [whole(w.value.shape, layer), whole(w.out.shape, layer)]
    if dense:
        ins += [w.first, w.first_b, w.second, w.second_b]
        specs += [
            whole(w.first.shape),
            whole(w.first_b.shape),
            pl.BlockSpec((width, 2 * slots), lambda i: (0, pair(i))),
            pl.BlockSpec((1, 2 * slots), lambda i: (0, pair(i))),
        ]
    else:
        ins += [w.table]
        specs += [pl.BlockSpec((2 * slots, slots), lambda i: (pair(i), 0))]
    ins += [w.inner, w.inner_b, w.outer]
    specs += [
        pl.BlockSpec((1, width, part), lambda i: (layer, 0, piece(i))),
        pl.BlockSpec((1, 1, part), lambda i: (layer, 0, piece(i))),
        pl.BlockSpec((1, part, width), lambda i: (layer, piece(i), 0)),
    ]
    wide_half = jax.ShapeDtypeStruct((rows, width), jnp.bfloat16)
    hidden = jax.ShapeDtypeStruct((rows, part * parts), jnp.bfloat16)
    outs = [wide_half] * 3 + [jax.ShapeDtypeStruct((2 * pairs, rows, slots), jnp.bfloat16), wide_half]
    outs += [jax.ShapeDtypeStruct((rows, width), jnp.float32), wide_half, hidden, hidden]
    row_block = whole_out((rows, width))
    hidden_block = pl.BlockSpec((rows, part), lambda i: (0, piece(i)))
    out_specs = [row_block] * 3 + [pl.BlockSpec((2, rows, slots), lambda i: (pair(i), 0, 0))]
    out_specs += [row_block] * 3 + [hidden_block] * 2
    if dense:
        outs += [wide_half] * 2
        out_specs += [row_block] * 2
    y, *saved = pl.pallas_call(
        functools.partial(forward_kernel, dense, pairs, parts),
        grid=(pairs + parts,),
        out_shape=outs,
        in_specs=specs,
        out_specs=out_specs,
        scratch_shapes=[pltpu.VMEM((rows, width), jnp.float32)],
        compiler_params=pltpu.CompilerParams(vmem_limit_bytes=56 * 2**20),
        name=f"forward_{layer}",
    )(*ins)
    return y, Saved(*saved)


def backward(g, x, saved, w, layer, before):
    dense = layer == 0
    rows, width, pairs, parts, part = sizes_of(x, w)
    slots = rows

    def pair(i):
        return jnp.maximum(i - parts, 0)

    def piece(i):
        return jnp.minimum(i, parts - 1)

    hidden_block = pl.BlockSpec((rows, part), lambda i: (0, piece(i)))
    ins = [g, x, saved.hid, saved.b, saved.c, saved.a, saved.v, saved.q, saved.slope, saved.probs, w.vectors]
    specs = [whole((rows, width))] * 7 + [hidden_block] * 2
    specs += [pl.BlockSpec((2, rows, slots), lambda i: (pair(i), 0, 0)), whole(w.vectors.shape, layer)]
    ins += [w.inner, w.outer, w.out, w.value]
    inner_block = pl.BlockSpec((1, width, part), lambda i: (layer, 0, piece(i)))
    outer_block = pl.BlockSpec((1, part, width), lambda i: (layer, piece(i), 0))
    specs += [inner_block, outer_block, whole(w.out.shape, layer), whole(w.value.shape, layer)]
    second_block = pl.BlockSpec((width, 2 * slots), lambda i: (0, pair(i)))
    if dense:
        ins += [saved.p, saved.first_slope, w.first, w.second]
        specs += [whole((rows, width))] * 2 + [whole(w.first.shape), second_block]
    aliases = {}
    if before is not None:
        aliases = {len(ins) + j: 1 + j for j in range(6)}
        ins += list(before)
        specs += [pl.BlockSpec(memory_space=pl.ANY)] * 6

    def like(shape, dtype=jnp.bfloat16):
        return jax.ShapeDtypeStruct(shape, dtype)

    outs = [like((rows, width)), like(w.outer.shape), like(w.inner.shape), like(w.out.shape), like(w.value.shape)]
    outs += [like((2, 8, width), jnp.float32), like(w.inner_b.shape, jnp.float32)]
    out_specs = [whole_out((rows, width)), outer_block, inner_block]
    out_specs += [whole_out(w.out.shape, layer), whole_out(w.value.shape, layer), whole_out((2, 8, width), layer)]
    out_specs += [pl.BlockSpec((1, 1, part), lambda i: (layer, 0, piece(i)))]
    if dense:
        outs += [like(w.first.shape), like(w.second.shape), like(w.second_b.shape, jnp.float32)]
        out_specs += [whole_out(w.first.shape), second_block, pl.BlockSpec((1, 2 * slots), lambda i: (0, pair(i)))]
    else:
        outs += [like(w.table.shape)]
        out_specs += [pl.BlockSpec((2 * slots, slots), lambda i: (pair(i), 0))]
    gx, *grads = pl.pallas_call(
        functools.partial(backward_kernel, dense, layer, pairs, parts),
        grid=(pairs + parts,),
        out_shape=outs,
        in_specs=specs,
        out_specs=out_specs,
        scratch_shapes=[
            pltpu.VMEM((rows, width), jnp.float32),
            pltpu.VMEM((rows, width), jnp.float32),
            pltpu.VMEM((rows, width), jnp.bfloat16),
            pltpu.VMEM((rows, width), jnp.bfloat16),
            pltpu.VMEM((rows, width), jnp.bfloat16),
            pltpu.VMEM((2, rows, slots), jnp.bfloat16),
        ],
        input_output_aliases=aliases,
        compiler_params=pltpu.CompilerParams(vmem_limit_bytes=60 * 2**20),
        name=f"backward_{layer}",
    )(*ins)
    return gx, grads[:6], grads[6:]


ROW_VECTORS = (0, 1, 3, 5, 6, 7, 11)
VECTORS = ROW_VECTORS + (9, 13, 15)
MATRICES = (2, 4, 8, 10, 12, 14, 16)
SMALL = 17
GATHER = (
    (16, "zxy", 0),
    (SMALL, "xzy", 0),
    (8, "zyx", 0),
    (12, "zxy", 0),
    (14, "yzx", 0),
    (2, "zyx", 1),
    (4, "xzy", 1),
    (10, "xzy", 0),
)
SUM = (
    (16, "yzx", 0),
    (8, "xzy", 0),
    (12, "yzx", 0),
    (14, "yxz", 0),
    (SMALL, "xyz", 1),
    (2, "yzx", 2),
    (4, "yzx", 1),
    (10, "xyz", 1),
)


def planned(call, plan, arrays, mesh):
    got = call([arrays[k] for k, _, _ in plan], [entry[1:] for entry in plan], mesh)
    return {k: g for (k, _, _), g in zip(plan, got)}


def per_device(mesh, boundary, lengths, *parts):
    nx, ndp = mesh.shape["segment"], mesh.shape["dp"]
    devices = nx * ndp
    first = lax.axis_index("segment") == 0
    swap = [(0, 1), (1, 0)]
    own = boundary[0, :, 0]
    received = lax.ppermute(jnp.where(first, own[1], own[0]), "segment", swap)
    rows = jnp.where(first, own[0], received)
    cotangent = jnp.where(first, received, own[1])
    length = jnp.where(first, lengths[0], lengths[1])

    flat = jnp.concatenate([parts[k].reshape(-1) for k in VECTORS])
    sizes = [parts[k].size for k in VECTORS]
    lanes = -(-flat.size // 2048) * 16
    packed = half(jnp.pad(flat, (0, lanes * 128 - flat.size)).reshape(lanes, 128))
    shards = {k: half(parts[k].reshape(parts[k].shape[-2:])) for k in MATRICES}
    shards[SMALL] = packed
    full = planned(gather_all, GATHER, shards, mesh)
    for k in MATRICES:
        g = full[k]
        full[k] = g.reshape((nx, ndp * g.shape[1]) + g.shape[2:]) if k < 12 else g.reshape(-1, g.shape[2])
    vec = wide(full[SMALL].reshape(devices, lanes * 128))
    count, size = len(ROW_VECTORS), sizes[0]
    bounds = [count * size]
    for k in VECTORS[count:]:
        bounds.append(bounds[-1] + parts[k].size)
    vectors = vec[:, : bounds[0]].reshape(nx, ndp, count, size).transpose(0, 2, 1, 3).reshape(nx, count, -1)
    inner_b, first_b, second_b = (vec[:, lo:hi] for lo, hi in zip(bounds, bounds[1:]))
    w = Weights(
        vectors,
        full[2],
        full[4],
        full[8],
        inner_b.reshape(nx, 1, -1),
        full[10],
        full[12],
        first_b.reshape(1, -1),
        full[14],
        second_b.reshape(1, -1),
        full[16],
    )

    out0, saved0 = forward(rows, length, w, 0)
    out1, saved1 = forward(out0, length, w, 1)
    gin1, both, synth1 = backward(cotangent, out0, saved1, w, 1, None)
    gin0, both, synth0 = backward(gin1, rows, saved0, w, 0, both)

    def swapped(for_first, for_second):
        got = lax.ppermute(jnp.where(first, for_second, for_first), "segment", swap)
        return jnp.stack([jnp.where(first, for_first, got), jnp.where(first, got, for_second)])[None, :, None]

    layer_outputs = swapped(out0, out1)
    input_grads = swapped(gin0, gin1)

    g_outer, g_inner, g_out, g_value, g_vec, g_inner_b = both
    g_first, g_second, g_second_b = synth0
    matrices = (g_value, g_out, g_inner, g_outer, g_first, g_second, synth1[0])
    grads = {k: g.reshape((devices,) + parts[k].shape[-2:]) for k, g in zip(MATRICES, matrices)}
    vec = [g_vec[:, :count].reshape(nx, count, ndp, size).transpose(0, 2, 1, 3).reshape(devices, count * size)]
    vec += [g.reshape(devices, -1) for g in (g_inner_b, g_vec[0, FIRST_B], g_second_b)]
    vec = jnp.concatenate(vec, axis=1)
    grads[SMALL] = jnp.pad(vec, ((0, 0), (0, lanes * 128 - vec.shape[1]))).reshape(devices, lanes, 128)
    summed = planned(scatter_all, SUM, grads, mesh)
    result = {k: summed[k].reshape(parts[k].shape) for k in MATRICES}
    vec = summed[SMALL].reshape(-1)
    at = 0
    for k, size in zip(VECTORS, sizes):
        result[k] = vec[at : at + size].reshape(parts[k].shape)
        at += size
    return (layer_outputs, input_grads) + tuple(result[k] for k in range(17))


def solution(mesh):
    layer = [P("segment", "dp")] * 12
    layer[2] = layer[4] = layer[8] = layer[10] = P("segment", "dp", None)
    both = P(AXES)
    rows = P(AXES, None)
    boundary = P("segment", None, "dp", None, None)
    weights = tuple(layer) + (rows, both, rows, both, rows)
    return jax.shard_map(
        functools.partial(per_device, mesh),
        mesh=mesh,
        in_specs=(boundary, P(None, "dp")) + weights,
        out_specs=(boundary, boundary) + weights,
        check_vma=False,
    )
```

```python
import functools
import math
from typing import Any, NamedTuple

import jax
import jax.numpy as jnp
from jax import lax
from jax.experimental import pallas as pl
from jax.experimental.pallas import tpu as pltpu
from jax.sharding import PartitionSpec as P

MESH = pl.DeviceIdType.MESH
HEADS = 12
EPSILON = 1e-05
GELU_SCALE = 0.7978845608028654
AXES = ("segment", "dp")


def half(value):
    return value.astype(jnp.bfloat16)


def wide(value):
    return value.astype(jnp.float32)


def mm(left, right):
    return jnp.dot(left, right, preferred_element_type=jnp.float32)


def mm_tn(left, right):
    return lax.dot_general(left, right, (((0,), (0,)), ((), ())), preferred_element_type=jnp.float32)


def mm_nt(left, right):
    return lax.dot_general(left, right, (((1,), (1,)), ((), ())), preferred_element_type=jnp.float32)


class Place:
    def __init__(self, nz):
        self.nz = nz
        self.x = lax.axis_index("segment")
        d = lax.axis_index("dp")
        self.c = d % 2
        self.y = (d // 2) % 2
        self.z = d // 4
        par = self.z % 2
        self.q = par * ((self.z + 1) // 2) + (1 - par) * ((nz - self.z // 2) % nz)

    def z_at(self, q):
        nz = self.nz
        upper = ((q + nz - 1) % nz) // (nz // 2)
        return (1 - upper) * (2 * q - 1) + upper * ((2 * (nz - q)) % (2 * nz))

    def ring_z(self, back):
        return self.z_at((self.q + 2 * self.nz - back) % self.nz)

    def device(self, x=None, z=None, y=None, c=None):
        x = self.x if x is None else x
        z = self.z if z is None else z
        y = self.y if y is None else y
        c = self.c if c is None else c
        return (x, (z * 2 + y) * 2 + c)

    def other(self, axis):
        return self.device(**{axis: 1 - getattr(self, axis)})

    def succ(self):
        return self.device(z=self.z_at((self.q + 1) % self.nz))

    def pred(self):
        return self.device(z=self.ring_z(1))


def greet(place):
    barrier = pltpu.get_barrier_semaphore()
    peers = [place.other("x"), place.other("y"), place.other("c"), place.succ(), place.pred()]
    for peer in peers:
        pl.semaphore_signal(barrier, inc=1, device_id=peer, device_id_type=MESH)
    pl.semaphore_wait(barrier, len(peers))


def block_of(ref, place, c, z, x=None, y=None):
    xs = pl.ds(0, 2) if x is None else x
    ys = pl.ds(0, 2) if y is None else y
    return ref.at[xs, z, ys, c]


def gather_kernel(plan, nz, *refs):
    orders, starts = zip(*plan)
    n = len(orders)
    far, own, outs, pair, refs = refs[:n], refs[n], refs[n + 1 : 2 * n + 1], refs[2 * n + 1], refs[2 * n + 2 :]
    raw, ins, (held, send, recv, local, swap, loads) = refs[:n], refs[n : 2 * n], refs[2 * n :]
    place = Place(nz)
    loading = [pltpu.make_async_copy(src, dst, loads.at[j]) for j, (src, dst) in enumerate(zip(far, raw))]
    loading.append(pltpu.make_async_copy(own.at[place.x], held, loads.at[n]))
    for copy in loading:
        copy.start()
    greet(place)
    stays = pltpu.make_async_copy(held, pair.at[place.x], swap.at[0])
    leaves = pltpu.make_async_remote_copy(
        src_ref=own.at[1 - place.x],
        dst_ref=pair.at[place.x],
        send_sem=swap.at[1],
        recv_sem=swap.at[2],
        device_id=place.other("x"),
        device_id_type=MESH,
    )
    started = []

    def put(i, k, src, dst, device):
        copy = pltpu.make_async_remote_copy(
            src_ref=src,
            dst_ref=dst,
            send_sem=send.at[i, k],
            recv_sem=recv.at[i, k],
            device_id=device,
            device_id_type=MESH,
        )
        copy.start()
        started.append(copy)
        return copy

    copies = [dict() for _ in orders]

    def stage(i, t):
        first, second, third = orders[i]
        out, mine = outs[i], copies[i]

        def shard(z, **at):
            return block_of(out, place, place.c, z, **at)

        def own(axis, z):
            return shard(z, **{axis: getattr(place, axis)})

        one = shard(place.z, x=place.x, y=place.y)
        if t == 0:
            loading[i].wait()
            ins[i][...] = half(raw[i][...])
            mine["own"] = pltpu.make_async_copy(ins[i], one, local.at[i])
            mine["own"].start()
        if second == "z":
            if t == 0:
                mine["p"] = put(i, 0, ins[i], one, place.other(first))
                return
            if t == 1:
                mine["own"].wait()
                mine["p"].wait_recv()
            elif t <= nz:
                mine["z", t - 1].wait_recv()
            if t <= nz:
                z = place.ring_z(t - 1)
                block = own(third, z)
                if t < nz:
                    mine["z", t] = put(i, t, block, block, place.succ())
                mine["l", t] = put(i, nz + t, block, block, place.other(third))
                mine["c", t] = put(i, 2 * nz + t, block, block, place.other("c"))
            if t >= 2:
                mine["l", t - 1].wait_recv()
                z = place.ring_z(t - 2)
                block = shard(z, **{third: 1 - getattr(place, third)})
                mine["d", t - 1] = put(i, 3 * nz + t - 1, block, block, place.other("c"))
        else:
            if t <= nz - 1:
                if t > 0:
                    mine["z", t].wait_recv()
                z = place.ring_z(t)
                src = ins[i] if t == 0 else shard(z, x=place.x, y=place.y)
                dst = shard(z, x=place.x, y=place.y)
                if t < nz - 1:
                    mine["z", t + 1] = put(i, t, src, dst, place.succ())
                mine["p", t + 1] = put(i, nz + t, src, dst, place.other(second))
            if 1 <= t <= nz:
                if t == 1:
                    mine["own"].wait()
                mine["p", t].wait_recv()
                block = own(third, place.ring_z(t - 1))
                mine["l", t] = put(i, 2 * nz + t, block, block, place.other(third))
                mine["c", t] = put(i, 3 * nz + t, block, block, place.other("c"))
            if t >= 2:
                mine["l", t - 1].wait_recv()
                block = shard(place.ring_z(t - 2), **{third: 1 - getattr(place, third)})
                mine["d", t - 1] = put(i, 4 * nz + t - 1, block, block, place.other("c"))

    stages = nz + 2
    for t in range(stages + max(starts)):
        for i in range(n):
            if 0 <= t - starts[i] < stages:
                stage(i, t - starts[i])
        if t == 0:
            leaves.start()
        if t == 1:
            loading[n].wait()
            stays.start()
    for mine in copies:
        for key, copy in mine.items():
            if key[0] in "cd":
                copy.wait_recv()
    for copy in started:
        copy.wait_send()
    stays.wait()
    leaves.wait()


def gather_all(shards, plan, mesh, own):
    nx, ndp = mesh.shape["segment"], mesh.shape["dp"]
    if nx != 2 or ndp != 16:
        first = lax.axis_index("segment") == 0
        other = lax.ppermute(jnp.where(first, own[1], own[0]), "segment", [(0, 1), (1, 0)])
        pair = jnp.where(first, jnp.stack([own[0], other]), jnp.stack([other, own[1]]))
        return [lax.all_gather(half(s), AXES, axis=0) for s in shards], pair
    nz, n = ndp // 4, len(shards)
    slots = 5 * nz + 2
    *outs, pair = pl.pallas_call(
        functools.partial(gather_kernel, plan, nz),
        out_shape=[jax.ShapeDtypeStruct((2, nz, 2, 2) + s.shape, jnp.bfloat16) for s in shards]
        + [jax.ShapeDtypeStruct(own.shape, own.dtype)],
        in_specs=[pl.BlockSpec(memory_space=pl.ANY)] * (n + 1),
        out_specs=[pl.BlockSpec(memory_space=pl.ANY)] * (n + 1),
        scratch_shapes=[pltpu.VMEM(s.shape, s.dtype) for s in shards]
        + [pltpu.VMEM(s.shape, jnp.bfloat16) for s in shards]
        + [
            pltpu.VMEM(own.shape[1:], own.dtype),
            pltpu.SemaphoreType.DMA((n, slots)),
            pltpu.SemaphoreType.DMA((n, slots)),
            pltpu.SemaphoreType.DMA((n,)),
            pltpu.SemaphoreType.DMA((3,)),
            pltpu.SemaphoreType.DMA((n + 1,)),
        ],
        compiler_params=pltpu.CompilerParams(collective_id=0, has_side_effects=True, vmem_limit_bytes=62 * 2**20),
        name="gather_weights",
    )(*shards, own)
    return [o.reshape((nx * ndp,) + s.shape) for o, s in zip(outs, shards)], pair


def add_to(dst, src):
    lead = dst.shape[:-2]

    def one(j, carry):
        at = (j // 2, j % 2) if len(lead) == 2 else (j,)[: len(lead)]
        at = at + (slice(None), slice(None))
        dst[at] = dst[at] + src[at]
        return carry

    if lead:
        lax.fori_loop(0, math.prod(lead), one, 0)
    else:
        dst[...] = dst[...] + src[...]


def scatter_kernel(plan, nz, *refs):
    orders, starts = zip(*plan)
    n = len(orders)
    ins, here, refs = refs[:n], refs[n], refs[n + 1 :]
    outs, there, refs = refs[:n], refs[n], refs[n + 1 :]
    accs, stages, firsts, rings, lasts = (refs[j * n : (j + 1) * n] for j in range(5))
    send, recv, local, swap = refs[5 * n :]
    place = Place(nz)
    greet(place)
    started = []
    swapped = pltpu.make_async_remote_copy(
        src_ref=here.at[1 - place.x],
        dst_ref=there,
        send_sem=swap.at[0],
        recv_sem=swap.at[1],
        device_id=place.other("x"),
        device_id_type=MESH,
    )

    def put(i, k, src, dst, device):
        copy = pltpu.make_async_remote_copy(
            src_ref=src,
            dst_ref=dst,
            send_sem=send.at[i, k],
            recv_sem=recv.at[i, k],
            device_id=device,
            device_id_type=MESH,
        )
        copy.start()
        started.append(copy)
        return copy

    live = [dict() for _ in orders]

    def load(i, k):
        copy = pltpu.make_async_copy(
            block_of(ins[i], place, place.c, place.ring_z(k)), stages[i].at[k % 2], local.at[i, k % 2]
        )
        copy.start()
        live[i]["o", k] = copy

    def stage(i, s):
        first, second, third = orders[i]
        acc, mine = accs[i], live[i]
        early, ring, late = firsts[i], rings[i], lasts[i]

        def part(k, flip=0, flip2=None):
            own = {axis: getattr(place, axis) for axis in "xy"}
            own[first] = own[first] + flip * (1 - 2 * own[first])
            if flip2 is None:
                own["xy".replace(first, "")] = pl.ds(0, 2)
            else:
                other = "xy".replace(first, "")
                own[other] = own[other] + flip2 * (1 - 2 * own[other])
            return acc.at[k - 1, own["x"], own["y"]]

        if s == 0:
            for k in range(1, nz + 1):
                src = block_of(ins[i], place, 1 - place.c, place.ring_z(k))
                mine["c", k] = put(i, k, src, acc.at[k - 1], place.other("c"))
            load(i, 1)
            load(i, 2)
        if 1 <= s <= nz:
            k = s
            mine["c", k].wait_recv()
            mine["o", k].wait()
            add_to(acc.at[k - 1], stages[i].at[k % 2])
            if k + 2 <= nz:
                load(i, k + 2)
            mine["p", k] = put(i, nz + k, part(k, 1), early.at[k - 1], place.other(first))
        if 2 <= s <= nz + 1:
            k = s - 1
            mine["p", k].wait_recv()
            add_to(part(k), early.at[k - 1])
        if second == "z":
            if s == 2:
                mine["z", 1] = put(i, 2 * nz + 1, part(1), ring.at[0], place.succ())
            if 3 <= s <= nz + 1:
                t = s - 2
                mine["z", t].wait_recv()
                add_to(ring.at[t - 1], part(t + 1))
                if t < nz - 1:
                    mine["z", t + 1] = put(i, 2 * nz + t + 1, ring.at[t - 1], ring.at[t], place.succ())
                else:
                    there = 1 - getattr(place, third)
                    mine["l"] = put(i, 3 * nz + 1, ring.at[t - 1, there], late, place.other(third))
            if s == nz + 2:
                mine["l"].wait_recv()
                outs[i][...] = wide(ring[nz - 2, getattr(place, third)]) + wide(late[...])
        else:
            if 2 <= s <= nz + 1:
                k = s - 1
                mine["l", k] = put(i, 3 * nz + k, part(k, 0, 1), late.at[k - 1], place.other(second))
            if 3 <= s <= nz + 2:
                k = s - 2
                mine["l", k].wait_recv()
                add_to(part(k, 0, 0), late.at[k - 1])
                if k == 1:
                    mine["z", 1] = put(i, 2 * nz + 1, part(1, 0, 0), ring.at[0], place.succ())
                else:
                    t = k - 1
                    mine["z", t].wait_recv()
                    if t < nz - 1:
                        add_to(ring.at[t - 1], part(t + 1, 0, 0))
                        mine["z", t + 1] = put(i, 2 * nz + t + 1, ring.at[t - 1], ring.at[t], place.succ())
                    else:
                        outs[i][...] = wide(ring[t - 1]) + wide(part(nz, 0, 0)[...])

    stages_of = nz + 3
    for t in range(stages_of + max(starts)):
        for i in range(n):
            if 0 <= t - starts[i] < stages_of:
                stage(i, t - starts[i])
        if t == 0:
            swapped.start()
    for copy in started:
        copy.wait_send()
    swapped.wait()


def finish_kernel(count, *refs):
    n = (len(refs) - 7 - count) // 3
    here, other, ins, packed, refs = refs[:2], refs[2:4], refs[4 : 4 + n], refs[4 + n], refs[5 + n :]
    outs, vectors, held, (rows, sem) = refs[: 2 + n], refs[2 + n : 2 + n + count], refs[2 + n + count : -2], refs[-2:]
    x = lax.axis_index("segment")
    moves = []
    for j in range(2):
        moves.append((here[j].at[x], rows.at[j, 0], outs[j].at[x]))
        moves.append((other[j], rows.at[j, 1], outs[j].at[1 - x]))
    moves += list(zip(ins, held, outs[2:]))
    steps = []
    for j, (src, via, dst) in enumerate(moves):
        steps.append((pltpu.make_async_copy(src, via, sem.at[j, 0]), pltpu.make_async_copy(via, dst, sem.at[j, 1])))
        steps[-1][0].start()
    row = 0
    for dst in vectors:
        size, at = dst.shape[1], 0
        while at < size:
            more = min(128, size - at)
            dst[:, at : at + more] = packed[row : row + 1, :more]
            at, row = at + more, row + 1
    for load, store in steps:
        load.wait()
        store.start()
    for load, store in steps:
        store.wait()


def finish(rows, others, arrays, packed, sizes):
    like = [jax.ShapeDtypeStruct(a.shape, a.dtype) for a in list(rows) + list(arrays)]
    vectors = [jax.ShapeDtypeStruct((1, size), jnp.float32) for size in sizes]
    far, near = pl.BlockSpec(memory_space=pl.ANY), pl.BlockSpec(memory_space=pltpu.VMEM)
    got = pl.pallas_call(
        functools.partial(finish_kernel, len(sizes)),
        out_shape=like + vectors,
        in_specs=[far] * (4 + len(arrays)) + [near],
        out_specs=[far] * len(like) + [near] * len(sizes),
        scratch_shapes=[pltpu.VMEM(a.shape, a.dtype) for a in arrays]
        + [pltpu.VMEM((2,) + rows[0].shape, rows[0].dtype), pltpu.SemaphoreType.DMA((4 + len(arrays), 2))],
        compiler_params=pltpu.CompilerParams(vmem_limit_bytes=62 * 2**20),
        name="finish",
    )(*rows, *others, *arrays, packed)
    return got[: len(like)], got[len(like) :]


def from_other(rows):
    return lax.ppermute(rows[1 - lax.axis_index("segment")], "segment", [(0, 1), (1, 0)])


def scatter_all(grads, plan, mesh, rows):
    nx, ndp = mesh.shape["segment"], mesh.shape["dp"]
    if nx != 2 or ndp != 16:
        return [wide(lax.psum_scatter(g, AXES, scatter_dimension=0, tiled=False)) for g in grads], from_other(rows)
    nz, n = ndp // 4, len(grads)

    def scratch(lead):
        return [pltpu.VMEM(lead(o) + g.shape[1:], g.dtype) for (o, _), g in zip(plan, grads)]

    slots = 4 * nz + 2
    far, near = pl.BlockSpec(memory_space=pl.ANY), pl.BlockSpec(memory_space=pltpu.VMEM)
    got = pl.pallas_call(
        functools.partial(scatter_kernel, plan, nz),
        out_shape=[jax.ShapeDtypeStruct(g.shape[1:], jnp.float32) for g in grads]
        + [jax.ShapeDtypeStruct(rows.shape[1:], rows.dtype)],
        in_specs=[far] * (n + 1),
        out_specs=[near] * n + [far],
        scratch_shapes=scratch(lambda o: (nz, 2, 2))
        + scratch(lambda o: (2, 2, 2))
        + scratch(lambda o: (nz, 2))
        + scratch(lambda o: (nz - 1, 2) if o[1] == "z" else (nz - 1,))
        + scratch(lambda o: () if o[1] == "z" else (nz,))
        + [
            pltpu.SemaphoreType.DMA((n, slots)),
            pltpu.SemaphoreType.DMA((n, slots)),
            pltpu.SemaphoreType.DMA((n, 2)),
            pltpu.SemaphoreType.DMA((2,)),
        ],
        compiler_params=pltpu.CompilerParams(
            collective_id=1, has_side_effects=True, vmem_limit_bytes=62 * 2**20
        ),
        name="sum_gradients",
    )(*[g.reshape((2, nz, 2, 2) + g.shape[1:]) for g in grads], rows)
    return got[:n], got[n]


ROWS = 512
HIDDEN = 768
GAIN1, BIAS1, VALUE_B, OUT_B, GAIN2, BIAS2, OUTER_B, FIRST_B = range(8)


def chunks(rows, size=ROWS):
    return [slice(at, at + size) for at in range(0, rows, size)]


def norm_parts(rows):
    centre = rows - jnp.mean(rows, axis=-1, keepdims=True)
    inv = lax.rsqrt(jnp.mean(centre * centre, axis=-1, keepdims=True) + EPSILON)
    return centre * inv, inv


def row_loop(rows, body, init):
    return lax.fori_loop(0, rows // 128, lambda j, c: body(pl.ds(pl.multiple_of(j * 128, 128), 128), c), init)


def norm_into(read, write, gain, shift, rows):
    def body(r, carry):
        write[r, :] = half(norm_parts(read(r))[0] * gain + shift)
        return carry

    row_loop(rows, body, 0)


def norm_back(read, grad, gain, rows, done):
    def body(r, carry):
        normal, inv = norm_parts(read(r))
        m_hat = grad(r)
        m = m_hat * gain
        part = inv * (
            m - jnp.mean(m, axis=-1, keepdims=True) - normal * jnp.mean(m * normal, axis=-1, keepdims=True)
        )
        done(r, part)
        return carry[0] + sums(m_hat * normal), carry[1] + sums(m_hat)

    zero = jnp.zeros_like(gain)
    return row_loop(rows, body, (zero, zero))


def sums(value):
    return jnp.sum(wide(value), axis=0, keepdims=True)


def gelu_both(t):
    square = t * t
    s = 0.5 + 0.5 * jnp.tanh(t * (GELU_SCALE + GELU_SCALE * 0.044715 * square))
    value = t * s
    slope = s + value * (1.0 - s) * (2 * GELU_SCALE + 6 * GELU_SCALE * 0.044715 * square)
    return value, slope


def masked_pair(head):
    return lax.broadcasted_iota(jnp.int32, (1, 2 * head), 1) < head


def add_up(fresh, ref, at, value):
    @pl.when(fresh)
    def _():
        ref[at] = value

    @pl.when(jnp.logical_not(fresh))
    def _():
        ref[at] += value


def forward_start(read, vec, value_ref, a_ref, v_ref, first=None):
    rows = a_ref.shape[0]
    norm_into(read, a_ref, vec(GAIN1), vec(BIAS1), rows)
    for r in chunks(rows):
        v_ref[r] = half(mm(a_ref[r], value_ref[...]) + vec(VALUE_B))
        if first is not None:
            first_ref, first_b, p_ref, slope_ref = first
            value, slope = gelu_both(mm(a_ref[r], first_ref[...]) + first_b[...])
            p_ref[r] = half(value)
            slope_ref[r] = half(slope)


def both_heads(pair, head):
    lower = masked_pair(head)
    zero = jnp.zeros_like(pair)
    return jnp.concatenate([jnp.where(lower, pair, zero), jnp.where(lower, zero, pair)], axis=0)


def forward_heads(pair, length, v_ref, c_ref, probs_ref, logits_of):
    rows, width = v_ref.shape
    slots = probs_ref.shape[1] // 2
    head = width // HEADS
    at = pl.ds(pl.multiple_of(pair * 2 * head, 2 * head), 2 * head)
    shut = jnp.where(lax.broadcasted_iota(jnp.int32, (1, slots), 1) >= length, -1e30, 0.0)
    both = logits_of(shut)
    for h in range(2):
        logits = both[h]
        expo = jnp.exp(logits - jnp.max(logits, axis=1, keepdims=True))
        probs_ref[:, h * slots : (h + 1) * slots] = half(expo * (1.0 / jnp.sum(expo, axis=1, keepdims=True)))
    c_ref[:, at] = half(mm(probs_ref[...], both_heads(v_ref[:, at], head)))


def forward_middle(read, vec, out_ref, c_ref, hid_ref, b_ref):
    rows = c_ref.shape[0]
    for r in chunks(rows):
        hid_ref[r] = read(r) + mm(c_ref[r], out_ref[...]) + vec(OUT_B)
    norm_into(lambda r: hid_ref[r, :], b_ref, vec(GAIN2), vec(BIAS2), rows)


def forward_hidden(fresh, b_ref, inner_ref, inner_b, outer_ref, q_ref, slope_ref, acc):
    for r in chunks(b_ref.shape[0]):
        value, slope = gelu_both(mm(b_ref[r], inner_ref[...]) + inner_b)
        q = half(value)
        q_ref[r] = q
        slope_ref[r] = half(slope)
        add_up(fresh, acc, r, mm(q, outer_ref[...]))


def forward_end(vec, hid_ref, acc, y_ref):
    for r in chunks(acc.shape[0]):
        y_ref[r] = half(hid_ref[r] + acc[r] + vec(OUTER_B))


def backward_hidden(fresh, g_ref, b_ref, q_ref, slope_ref, inner_ref, outer_ref, gz_ref, acc, g_outer, g_inner, g_inner_b):
    for r in chunks(g_ref.shape[0]):
        gz = half(mm_nt(g_ref[r], outer_ref[...]) * wide(slope_ref[r]))
        gz_ref[r] = gz
        add_up(fresh, acc, r, mm_nt(gz, inner_ref[...]))
    gz = gz_ref[...]
    g_outer[...] = half(mm_tn(q_ref[...], g_ref[...]))
    g_inner[...] = half(mm_tn(b_ref[...], gz))
    g_inner_b[...] = sums(gz)


def backward_middle(vec, put, g_ref, hid_ref, c_ref, out_ref, acc, ghid, gatt, gc_ref, g_out):
    rows = g_ref.shape[0]

    def done(r, part):
        total = wide(g_ref[r, :]) + part
        ghid[r, :] = total
        gatt[r, :] = half(total)

    gain, shift = norm_back(lambda r: hid_ref[r, :], lambda r: acc[r, :], vec(GAIN2), rows, done)
    put(GAIN2, gain)
    put(BIAS2, shift)
    put(OUTER_B, sums(g_ref[...]))
    put(OUT_B, sums(gatt[...]))
    g_out[...] = half(mm_tn(c_ref[...], gatt[...]))
    for r in chunks(rows):
        gc_ref[r] = half(mm_nt(gatt[r], out_ref[...]))


def backward_heads(pair, v_ref, gc_ref, gv_ref, probs_ref, db):
    rows, width = v_ref.shape
    slots = probs_ref.shape[1] // 2
    head = width // HEADS
    at = pl.ds(pl.multiple_of(pair * 2 * head, 2 * head), 2 * head)
    both = mm_nt(gc_ref[:, at], both_heads(v_ref[:, at], head))
    for h in range(2):
        cols = slice(h * slots, (h + 1) * slots)
        probs = wide(probs_ref[:, cols])
        weighed = probs * both[:, cols]
        db[:, cols] = half(weighed - probs * jnp.sum(weighed, axis=1, keepdims=True))
    values = mm_tn(probs_ref[...], gc_ref[:, at])
    gv_ref[:, at] = half(jnp.where(masked_pair(head), values[:slots], values[slots:]))


def backward_end(vec, put, read, gv_ref, value_ref, a_ref, acc, ghid, g_value, gx_ref, first=None):
    rows = gv_ref.shape[0]
    put(VALUE_B, sums(gv_ref[...]))
    g_value[...] = half(mm_tn(a_ref[...], gv_ref[...]))
    if first is not None:
        first_ref, slope_ref, gf_ref, g_first = first
        for r in chunks(rows):
            gf_ref[r] = half(acc[r] * wide(slope_ref[r]))
        put(FIRST_B, sums(gf_ref[...]))
        g_first[...] = half(mm_tn(a_ref[...], gf_ref[...]))
    else:
        put(FIRST_B, jnp.zeros((1, acc.shape[1]), jnp.float32))
    for r in chunks(rows):
        ga = mm_nt(gv_ref[r], value_ref[...])
        if first is not None:
            ga = ga + mm_nt(gf_ref[r], first_ref[...])
        acc[r] = ga

    def done(r, part):
        gx_ref[r, :] = half(ghid[r, :] + part)

    gain, shift = norm_back(read, lambda r: acc[r, :], vec(GAIN1), rows, done)
    put(GAIN1, gain)
    put(BIAS1, shift)


def forward_kernel(pairs, parts, length_ref, x_ref, vec_ref, value_ref, out_ref, first_ref, first_b, second_ref, second_b, inner_ref, inner_b, outer_ref, y_ref, *refs):
    kept, probs_ref, q_ref, slope_ref = refs[:7], refs[7], refs[8], refs[9]
    a_ref, v_ref, p_ref, first_slope, c_ref, b_ref, hid_ref, acc, sem = refs[10:]
    held = (a_ref, v_ref, p_ref, first_slope, c_ref, b_ref, hid_ref)
    copies = [pltpu.make_async_copy(src, dst, sem.at[j]) for j, (src, dst) in enumerate(zip(held, kept))]
    i = pl.program_id(0)
    slots = probs_ref.shape[2] // 2

    def vec(k):
        return vec_ref[0, k : k + 1, :]

    x_ref, y_ref = x_ref.at[0], y_ref.at[0]

    def read(r):
        return wide(x_ref[r, :])

    @pl.when(i == 0)
    def _():
        forward_start(read, vec, value_ref.at[0], a_ref, v_ref, (first_ref, first_b, p_ref, first_slope))
        for copy in copies[:4]:
            copy.start()

    @pl.when(i < pairs)
    def _():
        def logits_of(shut):
            logits = mm(p_ref[...], second_ref[...]) + (second_b[...] + jnp.concatenate([shut, shut], axis=1))
            return logits[:, :slots], logits[:, slots:]

        forward_heads(i, length_ref[0], v_ref, c_ref, probs_ref.at[0], logits_of)

    @pl.when(i == pairs - 1)
    def _():
        forward_middle(read, vec, out_ref.at[0], c_ref, hid_ref, b_ref)
        for copy in copies[4:]:
            copy.start()

    @pl.when(i >= pairs)
    def _():
        forward_hidden(i == pairs, b_ref, inner_ref.at[0], inner_b[0], outer_ref.at[0], q_ref, slope_ref, acc)

    @pl.when(i == pairs + parts - 1)
    def _():
        forward_end(vec, hid_ref, acc, y_ref)
        for copy in copies:
            copy.wait()


def backward_kernel(pairs, parts, g_ref, b_ref, vec_ref, q_ref, slope_ref, probs_ref, inner_ref, outer_ref, second_ref, *refs):
    far, refs = refs[:10], refs[16:]
    gx_ref, g_outer, g_inner, g_out, g_value, g_vec, g_inner_b, g_first, g_second, g_second_b = refs[:10]
    near, refs = refs[10:20], refs[20:]
    acc, ghid, gatt, gc_ref, gv_ref, db, gz_ref, sem = refs
    far = [ref.at[0] if len(ref.shape) == 3 else ref for ref in far]
    copies = [pltpu.make_async_copy(src, dst, sem.at[j]) for j, (src, dst) in enumerate(zip(far, near))]
    hid_ref, c_ref, out_ref, v_ref, p_ref, a_ref, value_ref, first_ref, first_slope, x_ref = near
    g_ref, gx_ref = g_ref.at[0], gx_ref.at[0]
    i = pl.program_id(0)
    slots = probs_ref.shape[2] // 2

    def vec(k):
        return vec_ref[0, k : k + 1, :]

    def put(k, value):
        g_vec[0, k : k + 1, :] = value

    @pl.when(i == 0)
    def _():
        for copy in copies:
            copy.start()

    @pl.when(i < parts)
    def _():
        backward_hidden(i == 0, g_ref, b_ref, q_ref, slope_ref, inner_ref.at[0], outer_ref.at[0], gz_ref, acc, g_outer.at[0], g_inner.at[0], g_inner_b.at[0])

    @pl.when(i == parts - 1)
    def _():
        for copy in copies[:3]:
            copy.wait()
        backward_middle(vec, put, g_ref, hid_ref, c_ref, out_ref, acc, ghid, gatt, gc_ref, g_out.at[0])
        for copy in copies[3:5]:
            copy.wait()

    @pl.when(i >= parts)
    def _():
        backward_heads(i - parts, v_ref, gc_ref, gv_ref, probs_ref.at[0], db)
        g_second[...] = half(mm_tn(p_ref[...], db[...]))
        g_second_b[...] = sums(db[...])
        add_up(i == parts, acc, slice(None), mm_nt(db[...], second_ref[...]))

    @pl.when(i == pairs + parts - 1)
    def _():
        for copy in copies[5:]:
            copy.wait()
        backward_end(
            vec, put, lambda r: wide(x_ref[r, :]), gv_ref, value_ref, a_ref, acc, ghid, g_value.at[0], gx_ref,
            (first_ref, first_slope, gatt, g_first),
        )


def both_kernel(pairs, parts, length_ref, x_ref, g_ref, vec_ref, value_ref, out_ref, table_ref, inner_ref, inner_b, outer_ref, *refs):
    y_ref, gx_ref, g_outer, g_inner, g_out, g_value, g_vec, g_inner_b, g_table = refs[:9]
    acc, hid_ref, ghid, a_ref, v_ref, c_ref, b_ref, gatt, gc_ref, gv_ref, probs_ref, q_ref, slope_ref, db, gz_ref = refs[9:]
    i = pl.program_id(0)
    slots = probs_ref.shape[2] // 2
    j = i - pairs
    k = j - parts
    n = k - parts

    def vec(k):
        return vec_ref[0, k : k + 1, :]

    def put(k, value):
        g_vec[0, k : k + 1, :] = value

    x_ref, g_ref, y_ref, gx_ref = (ref.at[0] for ref in (x_ref, g_ref, y_ref, gx_ref))

    def read(r):
        return wide(x_ref[r, :])

    @pl.when(i == 0)
    def _():
        forward_start(read, vec, value_ref.at[0], a_ref, v_ref)

    @pl.when(i < pairs)
    def _():
        def logits_of(shut):
            return wide(table_ref[:slots, :]) + shut, wide(table_ref[slots:, :]) + shut

        forward_heads(i, length_ref[0], v_ref, c_ref, probs_ref.at[i], logits_of)

    @pl.when(i == pairs - 1)
    def _():
        forward_middle(read, vec, out_ref.at[0], c_ref, hid_ref, b_ref)

    @pl.when((j >= 0) & (j < parts))
    def _():
        forward_hidden(j == 0, b_ref, inner_ref.at[0], inner_b[0], outer_ref.at[0], q_ref.at[j], slope_ref.at[j], acc)

    @pl.when(j == parts - 1)
    def _():
        forward_end(vec, hid_ref, acc, y_ref)

    @pl.when((k >= 0) & (k < parts))
    def _():
        at = parts - 1 - k
        backward_hidden(k == 0, g_ref, b_ref, q_ref.at[at], slope_ref.at[at], inner_ref.at[0], outer_ref.at[0], gz_ref, acc, g_outer.at[0], g_inner.at[0], g_inner_b.at[0])

    @pl.when(k == parts - 1)
    def _():
        backward_middle(vec, put, g_ref, hid_ref, c_ref, out_ref.at[0], acc, ghid, gatt, gc_ref, g_out.at[0])

    @pl.when(n >= 0)
    def _():
        backward_heads(n, v_ref, gc_ref, gv_ref, probs_ref.at[n], db)
        g_table[:slots, :] = db[:, :slots]
        g_table[slots:, :] = db[:, slots:]

    @pl.when(n == pairs - 1)
    def _():
        backward_end(vec, put, read, gv_ref, value_ref.at[0], a_ref, acc, ghid, g_value.at[0], gx_ref)


class Weights(NamedTuple):
    vectors: Any
    value: Any
    out: Any
    inner: Any
    inner_b: Any
    outer: Any
    first: Any
    first_b: Any
    second: Any
    second_b: Any
    table: Any


def whole(shape, *at):
    at = tuple(at)
    block = (1,) * len(at) + tuple(shape[len(at) :])
    return pl.BlockSpec(block, lambda i: at + (0,) * (len(shape) - len(at)), pipeline_mode=pl.Buffered(1))


def whole_out(shape, *at):
    at = tuple(at)
    block = (1,) * len(at) + tuple(shape[len(at) :])
    return pl.BlockSpec(block, lambda i: at + (0,) * (len(shape) - len(at)))


def like(shape, dtype=jnp.bfloat16):
    return jax.ShapeDtypeStruct(shape, dtype)


FAR = pl.BlockSpec(memory_space=pl.ANY)


def sizes_of(x, w):
    rows, width = x.shape[-2:]
    parts = w.inner.shape[2] // HIDDEN
    return rows, width, HEADS // 2, parts, w.inner.shape[2] // parts


def forward(x, length, w):
    rows, width, pairs, parts, part = sizes_of(x, w)
    slots = rows

    def pair(i):
        return jnp.minimum(i, pairs - 1)

    def piece(i):
        return jnp.maximum(i - pairs, 0)

    ins = [length, x, w.vectors, w.value, w.out, w.first, w.first_b, w.second, w.second_b, w.inner, w.inner_b, w.outer]
    specs = [
        pl.BlockSpec(memory_space=pltpu.SMEM),
        whole(x.shape, 0),
        whole(w.vectors.shape, 0),
        whole(w.value.shape, 0),
        whole(w.out.shape, 0),
        whole(w.first.shape),
        whole(w.first_b.shape),
        pl.BlockSpec((width, 2 * slots), lambda i: (0, pair(i))),
        pl.BlockSpec((1, 2 * slots), lambda i: (0, pair(i))),
        pl.BlockSpec((1, width, part), lambda i: (0, 0, piece(i))),
        pl.BlockSpec((1, 1, part), lambda i: (0, 0, piece(i))),
        pl.BlockSpec((1, part, width), lambda i: (0, piece(i), 0)),
    ]
    half_rows = like((rows, width))
    kept = [half_rows] * 6 + [like((rows, width), jnp.float32)]
    hidden_block = pl.BlockSpec((rows, part), lambda i: (0, piece(i)))
    y, *saved = pl.pallas_call(
        functools.partial(forward_kernel, pairs, parts),
        grid=(pairs + parts,),
        out_shape=[like(x.shape)] + kept + [like((pairs, rows, 2 * slots))] + [like((rows, part * parts))] * 2,
        in_specs=specs,
        out_specs=[whole_out(x.shape, 0)]
        + [FAR] * 7
        + [pl.BlockSpec((1, rows, 2 * slots), lambda i: (pair(i), 0, 0))]
        + [hidden_block] * 2,
        scratch_shapes=[pltpu.VMEM(k.shape, k.dtype) for k in kept]
        + [pltpu.VMEM((rows, width), jnp.float32), pltpu.SemaphoreType.DMA((7,))],
        compiler_params=pltpu.CompilerParams(vmem_limit_bytes=62 * 2**20),
        name="forward_0",
    )(*ins)
    return y, saved


def backward(g, x, saved, w, before):
    rows, width, pairs, parts, part = sizes_of(x, w)
    slots = rows
    a, v, p, first_slope, c, b, hid, probs, q, slope = saved

    def pair(i):
        return jnp.maximum(i - parts, 0)

    def piece(i):
        return jnp.minimum(i, parts - 1)

    hidden_block = pl.BlockSpec((rows, part), lambda i: (0, piece(i)))
    inner_block = pl.BlockSpec((1, width, part), lambda i: (0, 0, piece(i)))
    outer_block = pl.BlockSpec((1, part, width), lambda i: (0, piece(i), 0))
    second_block = pl.BlockSpec((width, 2 * slots), lambda i: (0, pair(i)))
    far = [hid, c, w.out, v, p, a, w.value, w.first, first_slope, x]
    ins = [g, b, w.vectors, q, slope, probs, w.inner, w.outer, w.second] + far
    specs = [whole(g.shape, 1), whole((rows, width)), whole(w.vectors.shape, 0)] + [hidden_block] * 2
    specs += [pl.BlockSpec((1, rows, 2 * slots), lambda i: (pair(i), 0, 0)), inner_block, outer_block, second_block]
    specs += [FAR] * 10
    aliases = {len(ins) + j: 1 + j for j in range(6)}
    aliases[0] = 0
    ins += list(before)
    specs += [FAR] * 6
    outs = [like(g.shape)] + [like(k.shape, k.dtype) for k in before]
    out_specs = [whole_out(g.shape, 0), outer_block, inner_block]
    out_specs += [whole_out(w.out.shape, 0), whole_out(w.value.shape, 0), whole_out((2, 8, width), 0)]
    out_specs += [pl.BlockSpec((1, 1, part), lambda i: (0, 0, piece(i)))]
    outs += [like(w.first.shape), like(w.second.shape), like(w.second_b.shape, jnp.float32)]
    out_specs += [whole_out(w.first.shape), second_block, pl.BlockSpec((1, 2 * slots), lambda i: (0, pair(i)))]
    gx, *grads = pl.pallas_call(
        functools.partial(backward_kernel, pairs, parts),
        grid=(pairs + parts,),
        out_shape=outs,
        in_specs=specs,
        out_specs=out_specs,
        scratch_shapes=[pltpu.VMEM(k.shape[-2:], k.dtype) for k in far]
        + [pltpu.VMEM((rows, width), jnp.float32)] * 2
        + [pltpu.VMEM((rows, width), jnp.bfloat16)] * 3
        + [pltpu.VMEM((rows, 2 * slots), jnp.bfloat16), pltpu.VMEM((rows, part), jnp.bfloat16), pltpu.SemaphoreType.DMA((10,))],
        input_output_aliases=aliases,
        compiler_params=pltpu.CompilerParams(vmem_limit_bytes=62 * 2**20),
        name="backward_0",
    )(*ins)
    return gx, grads[:6], grads[6:]


def both_ways(x, g, length, w):
    rows, width, pairs, parts, part = sizes_of(x, w)
    slots = rows

    def there(i):
        return jnp.minimum(i, pairs - 1)

    def back(i):
        return jnp.maximum(i - pairs - 2 * parts, 0)

    def piece(i):
        j = jnp.clip(i - pairs, 0, 2 * parts - 1)
        return jnp.minimum(j, 2 * parts - 1 - j)

    def late(i):
        return parts - 1 - jnp.clip(i - pairs - parts, 0, parts - 1)

    ins = [length, x, g, w.vectors, w.value, w.out, w.table, w.inner, w.inner_b, w.outer]
    specs = [pl.BlockSpec(memory_space=pltpu.SMEM), whole(x.shape, 0), whole(g.shape, 1)]
    specs += [whole(w.vectors.shape, 1), whole(w.value.shape, 1), whole(w.out.shape, 1)]
    specs += [
        pl.BlockSpec((2 * slots, slots), lambda i: (there(i), 0)),
        pl.BlockSpec((1, width, part), lambda i: (1, 0, piece(i))),
        pl.BlockSpec((1, 1, part), lambda i: (1, 0, piece(i))),
        pl.BlockSpec((1, part, width), lambda i: (1, piece(i), 0)),
    ]
    grads = [like(w.outer.shape), like(w.inner.shape), like(w.out.shape), like(w.value.shape)]
    grads += [like((2, 8, width), jnp.float32), like(w.inner_b.shape, jnp.float32), like(w.table.shape)]
    grad_specs = [
        pl.BlockSpec((1, part, width), lambda i: (1, late(i), 0)),
        pl.BlockSpec((1, width, part), lambda i: (1, 0, late(i))),
        whole_out(w.out.shape, 1),
        whole_out(w.value.shape, 1),
        whole_out((2, 8, width), 1),
        pl.BlockSpec((1, 1, part), lambda i: (1, 0, late(i))),
        pl.BlockSpec((2 * slots, slots), lambda i: (back(i), 0)),
    ]
    y, gx, *grads = pl.pallas_call(
        functools.partial(both_kernel, pairs, parts),
        grid=(2 * pairs + 2 * parts,),
        out_shape=[like(x.shape)] * 2 + grads,
        in_specs=specs,
        out_specs=[whole_out(x.shape, 1)] * 2 + grad_specs,
        scratch_shapes=[pltpu.VMEM((rows, width), jnp.float32)] * 3
        + [pltpu.VMEM((rows, width), jnp.bfloat16)] * 7
        + [pltpu.VMEM((pairs, rows, 2 * slots), jnp.bfloat16)]
        + [pltpu.VMEM((parts, rows, part), jnp.bfloat16)] * 2
        + [pltpu.VMEM((rows, 2 * slots), jnp.bfloat16), pltpu.VMEM((rows, part), jnp.bfloat16)],
        input_output_aliases={1: 0},
        compiler_params=pltpu.CompilerParams(vmem_limit_bytes=62 * 2**20),
        name="forward_backward_1",
    )(*ins)
    return y, gx, grads[:6], grads[6]


ROW_VECTORS = (0, 1, 3, 5, 6, 7, 11)
VECTORS = ROW_VECTORS + (9, 13, 15)
MATRICES = (2, 4, 8, 10, 12, 14, 16)
SMALL = 17
GATHER = (
    (8, "zyx", 1),
    (10, "yzx", 1),
    (16, "xzy", 0),
    (14, "xzy", 1),
    (SMALL, "xzy", 0),
    (12, "zyx", 0),
    (4, "zxy", 0),
    (2, "zxy", 0),
)
SUM = (
    (12, "yzx", 2),
    (8, "xzy", 2),
    (16, "xzy", 4),
    (4, "yzx", 0),
    (SMALL, "yzx", 1),
    (2, "yzx", 0),
    (14, "yxz", 4),
    (10, "yxz", 2),
)


def planned(call, plan, arrays, mesh, rows):
    got, rows = call([arrays[k] for k, _, _ in plan], [entry[1:] for entry in plan], mesh, rows)
    return {k: g for (k, _, _), g in zip(plan, got)}, rows


def lanes(array):
    n, size = array.shape
    rows = -(-size // 128)
    return jnp.pad(array, ((0, 0), (0, rows * 128 - size))).reshape(n, rows, 128)


def per_device(mesh, boundary, lengths, *parts):
    nx, ndp = mesh.shape["segment"], mesh.shape["dp"]
    devices = nx * ndp
    first = lax.axis_index("segment") == 0
    length = jnp.where(first, lengths[0], lengths[1])
    sizes = [parts[k].size for k in VECTORS]

    shards = {k: parts[k].reshape(parts[k].shape[-2:]) for k in MATRICES}
    flat = jnp.concatenate([parts[k].reshape(-1) for k in VECTORS])
    rows = -(-flat.size // 2048) * 16
    shards[SMALL] = jnp.pad(flat, (0, rows * 128 - flat.size)).reshape(rows, 128)
    full, pair = planned(gather_all, GATHER, shards, mesh, boundary[0, :, 0])
    for k in MATRICES:
        g = full[k]
        full[k] = g.reshape((nx, ndp * g.shape[1]) + g.shape[2:]) if k < 12 else g.reshape(-1, g.shape[2])
    vec = wide(full[SMALL].reshape(devices, rows * 128))
    count, size = len(ROW_VECTORS), sizes[0]
    bounds = [count * size]
    for k in VECTORS[count:]:
        bounds.append(bounds[-1] + parts[k].size)
    vectors = vec[:, : bounds[0]].reshape(nx, ndp, count, size).transpose(0, 2, 1, 3).reshape(nx, count, -1)
    inner_b, first_b, second_b = (vec[:, lo:hi] for lo, hi in zip(bounds, bounds[1:]))
    w = Weights(
        vectors,
        full[2],
        full[4],
        full[8],
        inner_b.reshape(nx, 1, -1),
        full[10],
        full[12],
        first_b.reshape(1, -1),
        full[14],
        second_b.reshape(1, -1),
        full[16],
    )

    outs, saved = forward(pair, length, w)
    outs, gins, both, g_table = both_ways(outs, pair, length, w)
    other_outs = from_other(outs)
    gins, both, synth = backward(gins, pair, saved, w, both)

    g_outer, g_inner, g_out, g_value, g_vec, g_inner_b = both
    g_first, g_second, g_second_b = synth
    matrices = (g_value, g_out, g_inner, g_outer, g_first, g_second, g_table)
    grads = {k: g.reshape((devices,) + parts[k].shape[-2:]) for k, g in zip(MATRICES, matrices)}
    vec = g_vec[:, :count].reshape(nx, count, ndp, size).transpose(0, 2, 1, 3).reshape(devices * count, size)
    vec = [lanes(vec).reshape(devices, -1, 128)]
    vec += [lanes(g.reshape(devices, -1)) for g in (g_inner_b, g_vec[0, FIRST_B], g_second_b)]
    vec = jnp.concatenate(vec, axis=1)
    grads[SMALL] = jnp.pad(vec, ((0, 0), (0, -vec.shape[1] % 16), (0, 0)))
    summed, other_gins = planned(scatter_all, SUM, grads, mesh, gins)
    arrays, vectors = finish([outs, gins], [other_outs, other_gins], [summed[k] for k in MATRICES], summed[SMALL], sizes)
    result = {k: g.reshape(parts[k].shape) for k, g in zip(MATRICES, arrays[2:])}
    for k, g in zip(VECTORS, vectors):
        result[k] = g.reshape(parts[k].shape)
    return tuple(a.reshape(boundary.shape) for a in arrays[:2]) + tuple(result[k] for k in range(17))


def solution(mesh):
    layer = [P("segment", "dp")] * 12
    layer[2] = layer[4] = layer[8] = layer[10] = P("segment", "dp", None)
    both = P(AXES)
    rows = P(AXES, None)
    boundary = P("segment", None, "dp", None, None)
    weights = tuple(layer) + (rows, both, rows, both, rows)
    return jax.shard_map(
        functools.partial(per_device, mesh),
        mesh=mesh,
        in_specs=(boundary, P(None, "dp")) + weights,
        out_specs=(boundary, boundary) + weights,
        check_vma=False,
    )
```

```python
import functools
import math
from typing import Any, NamedTuple

import jax
import jax.numpy as jnp
from jax import lax
from jax.experimental import pallas as pl
from jax.experimental.pallas import tpu as pltpu
from jax.sharding import PartitionSpec as P

MESH = pl.DeviceIdType.MESH
HEADS = 12
EPSILON = 1e-05
GELU_SCALE = 0.7978845608028654
AXES = ("segment", "dp")


def half(value):
    return value.astype(jnp.bfloat16)


def wide(value):
    return value.astype(jnp.float32)


def mm(left, right):
    return jnp.dot(left, right, preferred_element_type=jnp.float32)


def mm_tn(left, right):
    return lax.dot_general(left, right, (((0,), (0,)), ((), ())), preferred_element_type=jnp.float32)


def mm_nt(left, right):
    return lax.dot_general(left, right, (((1,), (1,)), ((), ())), preferred_element_type=jnp.float32)


class Place:
    def __init__(self, nz):
        self.nz = nz
        self.x = lax.axis_index("segment")
        d = lax.axis_index("dp")
        self.c = d % 2
        self.y = (d // 2) % 2
        self.z = d // 4
        par = self.z % 2
        self.q = par * ((self.z + 1) // 2) + (1 - par) * ((nz - self.z // 2) % nz)

    def z_at(self, q):
        nz = self.nz
        upper = ((q + nz - 1) % nz) // (nz // 2)
        return (1 - upper) * (2 * q - 1) + upper * ((2 * (nz - q)) % (2 * nz))

    def ring_z(self, back):
        return self.z_at((self.q + 2 * self.nz - back) % self.nz)

    def device(self, x=None, z=None, y=None, c=None):
        x = self.x if x is None else x
        z = self.z if z is None else z
        y = self.y if y is None else y
        c = self.c if c is None else c
        return (x, (z * 2 + y) * 2 + c)

    def other(self, axis):
        return self.device(**{axis: 1 - getattr(self, axis)})

    def succ(self):
        return self.device(z=self.z_at((self.q + 1) % self.nz))

    def pred(self):
        return self.device(z=self.ring_z(1))


def greet(place):
    barrier = pltpu.get_barrier_semaphore()
    peers = [place.other("x"), place.other("y"), place.other("c"), place.succ(), place.pred()]
    for peer in peers:
        pl.semaphore_signal(barrier, inc=1, device_id=peer, device_id_type=MESH)
    pl.semaphore_wait(barrier, len(peers))


def part_of(shape, part):
    rows, cols = shape
    if part is None:
        return (slice(0, rows), slice(0, cols))
    if rows % 32 == 0:
        return (slice(part * rows // 2, (part + 1) * rows // 2), slice(0, cols))
    return (slice(0, rows), slice(part * cols // 2, (part + 1) * cols // 2))


def part_shape(shape, part):
    return tuple(cut.stop - cut.start for cut in part_of(shape, part))


def block_of(ref, cut, c, z, x=None, y=None):
    xs = pl.ds(0, 2) if x is None else x
    ys = pl.ds(0, 2) if y is None else y
    return ref.at[(xs, z, ys, c) + cut]


def gather_kernel(plan, nz, small_at, count, *refs):
    which, parts, orders, starts = zip(*plan)
    n = max(which) + 1
    far, vectors, own, refs = refs[: n - 1], refs[n - 1 : n - 1 + count], refs[n - 1 + count], refs[n + count :]
    whole_outs, pair, raw, whole_ins, refs = refs[:n], refs[n], refs[n + 1 : 2 * n + 1], refs[2 * n + 1 : 3 * n + 1], refs[3 * n + 1 :]
    near, (held, send, recv, local, swap, loads) = refs[:count], refs[count:]
    cuts = [part_of(raw[k].shape, part) for k, part in zip(which, parts)]
    ins = [whole_ins[k].at[cut] for k, cut in zip(which, cuts)]
    outs = [whole_outs[k] for k in which]
    ready = set()
    place = Place(nz)
    moves = list(zip(vectors, near))
    moves += list(zip(far, [ref for k, ref in enumerate(raw) if k != small_at])) + [(own.at[place.x], held)]
    loading = [pltpu.make_async_copy(src, dst, loads.at[j]) for j, (src, dst) in enumerate(moves)]
    for copy in loading:
        copy.start()
    packing, loading = loading[:count], loading[count:]
    loading.insert(small_at, None)
    greet(place)
    stays = pltpu.make_async_copy(held, pair.at[place.x], swap.at[0])
    leaves = pltpu.make_async_remote_copy(
        src_ref=own.at[1 - place.x],
        dst_ref=pair.at[place.x],
        send_sem=swap.at[1],
        recv_sem=swap.at[2],
        device_id=place.other("x"),
        device_id_type=MESH,
    )
    started = []

    def put(i, k, src, dst, device):
        copy = pltpu.make_async_remote_copy(
            src_ref=src,
            dst_ref=dst,
            send_sem=send.at[i, k],
            recv_sem=recv.at[i, k],
            device_id=device,
            device_id_type=MESH,
        )
        copy.start()
        started.append(copy)
        return copy

    copies = [dict() for _ in orders]

    def stage(i, t):
        first, second, third = orders[i]
        out, mine = outs[i], copies[i]

        def shard(z, **at):
            return block_of(out, cuts[i], place.c, z, **at)

        def own(axis, z):
            return shard(z, **{axis: getattr(place, axis)})

        one = shard(place.z, x=place.x, y=place.y)
        if t == 0:
            k = which[i]
            if k not in ready:
                if k == small_at:
                    raw[k][...] = jnp.zeros_like(raw[k])
                    row = 0
                    for copy, vector in zip(packing, near):
                        copy.wait()
                        for r, lo, many in pieces_of(vector.shape[1], row):
                            raw[k][r : r + 1, :many] = vector[:, lo : lo + many]
                        row += rows_for(vector.shape[1])
                else:
                    loading[k].wait()
                whole_ins[k][...] = half(raw[k][...])
                ready.add(k)
            mine["own"] = pltpu.make_async_copy(ins[i], one, local.at[i])
            mine["own"].start()
        if second == "z":
            if t == 0:
                mine["p"] = put(i, 0, ins[i], one, place.other(first))
                return
            if t == 1:
                mine["own"].wait()
                mine["p"].wait_recv()
            elif t <= nz:
                mine["z", t - 1].wait_recv()
            if t <= nz:
                z = place.ring_z(t - 1)
                block = own(third, z)
                if t < nz:
                    mine["z", t] = put(i, t, block, block, place.succ())
                mine["l", t] = put(i, nz + t, block, block, place.other(third))
                mine["c", t] = put(i, 2 * nz + t, block, block, place.other("c"))
            if t >= 2:
                mine["l", t - 1].wait_recv()
                z = place.ring_z(t - 2)
                block = shard(z, **{third: 1 - getattr(place, third)})
                mine["d", t - 1] = put(i, 3 * nz + t - 1, block, block, place.other("c"))
        else:
            if t <= nz - 1:
                if t > 0:
                    mine["z", t].wait_recv()
                z = place.ring_z(t)
                src = ins[i] if t == 0 else shard(z, x=place.x, y=place.y)
                dst = shard(z, x=place.x, y=place.y)
                if t < nz - 1:
                    mine["z", t + 1] = put(i, t, src, dst, place.succ())
                mine["p", t + 1] = put(i, nz + t, src, dst, place.other(second))
            if 1 <= t <= nz:
                if t == 1:
                    mine["own"].wait()
                mine["p", t].wait_recv()
                block = own(third, place.ring_z(t - 1))
                mine["l", t] = put(i, 2 * nz + t, block, block, place.other(third))
                mine["c", t] = put(i, 3 * nz + t, block, block, place.other("c"))
            if t >= 2:
                mine["l", t - 1].wait_recv()
                block = shard(place.ring_z(t - 2), **{third: 1 - getattr(place, third)})
                mine["d", t - 1] = put(i, 4 * nz + t - 1, block, block, place.other("c"))

    stages = nz + 2
    for t in range(stages + max(starts)):
        for i in range(len(plan)):
            if 0 <= t - starts[i] < stages:
                stage(i, t - starts[i])
        if t == 0:
            leaves.start()
        if t == 1:
            loading[-1].wait()
            stays.start()
    for mine in copies:
        for key, copy in mine.items():
            if key[0] in "cd":
                copy.wait_recv()
    for copy in started:
        copy.wait_send()
    stays.wait()
    leaves.wait()


def gather_all(shards, plan, mesh, rows):
    nx, ndp = mesh.shape["segment"], mesh.shape["dp"]
    small_at = [isinstance(s, list) for s in shards].index(True)
    vectors = shards[small_at]
    if nx != 2 or ndp != 16:
        first = lax.axis_index("segment") == 0
        other = lax.ppermute(jnp.where(first, rows[1], rows[0]), "segment", [(0, 1), (1, 0)])
        pair = jnp.where(first, jnp.stack([rows[0], other]), jnp.stack([other, rows[1]]))
        packed = sixteens(jnp.concatenate([lanes(v) for v in vectors]))
        shards = [packed if j == small_at else s for j, s in enumerate(shards)]
        return [lax.all_gather(half(s), AXES, axis=0) for s in shards], pair
    nz, n, count = ndp // 4, len(shards), len(vectors)
    height = sum(rows_for(v.size) for v in vectors)
    shapes = [(height + -height % 16, 128) if j == small_at else s.shape for j, s in enumerate(shards)]
    far = [s for j, s in enumerate(shards) if j != small_at]
    slots = 5 * nz + 2
    *outs, pair = pl.pallas_call(
        functools.partial(gather_kernel, plan, nz, small_at, count),
        out_shape=[jax.ShapeDtypeStruct((2, nz, 2, 2) + s, jnp.bfloat16) for s in shapes]
        + [jax.ShapeDtypeStruct(rows.shape, rows.dtype)],
        in_specs=[pl.BlockSpec(memory_space=pl.ANY)] * (n + count),
        out_specs=[pl.BlockSpec(memory_space=pl.ANY)] * (n + 1),
        scratch_shapes=[pltpu.VMEM(s, jnp.float32) for s in shapes]
        + [pltpu.VMEM(s, jnp.bfloat16) for s in shapes]
        + [pltpu.VMEM(v.shape, v.dtype) for v in vectors]
        + [
            pltpu.VMEM(rows.shape[1:], rows.dtype),
            pltpu.SemaphoreType.DMA((len(plan), slots)),
            pltpu.SemaphoreType.DMA((len(plan), slots)),
            pltpu.SemaphoreType.DMA((len(plan),)),
            pltpu.SemaphoreType.DMA((3,)),
            pltpu.SemaphoreType.DMA((n + count,)),
        ],
        compiler_params=pltpu.CompilerParams(collective_id=0, has_side_effects=True, vmem_limit_bytes=62 * 2**20),
        name="gather_weights",
    )(*far, *vectors, rows)
    return [o.reshape((nx * ndp,) + s) for o, s in zip(outs, shapes)], pair


def add_to(dst, src):
    lead = dst.shape[:-2]

    def one(j, carry):
        at = (j // 2, j % 2) if len(lead) == 2 else (j,)[: len(lead)]
        at = at + (slice(None), slice(None))
        dst[at] = dst[at] + src[at]
        return carry

    if lead:
        lax.fori_loop(0, math.prod(lead), one, 0)
    else:
        dst[...] = dst[...] + src[...]


def scatter_kernel(plan, nz, *refs):
    which, parts, orders, starts = zip(*plan)
    n = max(which) + 1
    ins, here, refs = refs[:n], refs[n], refs[n + 1 :]
    outs, there, refs = refs[:n], refs[n], refs[n + 1 :]
    cuts = [part_of(outs[k].shape, part) for k, part in zip(which, parts)]
    ins = [ins[k] for k in which]
    outs = [outs[k].at[cut] for k, cut in zip(which, cuts)]
    n = len(plan)
    accs, stages, firsts, rings, lasts = (refs[j * n : (j + 1) * n] for j in range(5))
    send, recv, local, swap = refs[5 * n :]
    place = Place(nz)
    greet(place)
    started = []
    swapped = pltpu.make_async_remote_copy(
        src_ref=here.at[1 - place.x],
        dst_ref=there,
        send_sem=swap.at[0],
        recv_sem=swap.at[1],
        device_id=place.other("x"),
        device_id_type=MESH,
    )

    def put(i, k, src, dst, device):
        copy = pltpu.make_async_remote_copy(
            src_ref=src,
            dst_ref=dst,
            send_sem=send.at[i, k],
            recv_sem=recv.at[i, k],
            device_id=device,
            device_id_type=MESH,
        )
        copy.start()
        started.append(copy)
        return copy

    live = [dict() for _ in orders]

    def load(i, k):
        copy = pltpu.make_async_copy(
            block_of(ins[i], cuts[i], place.c, place.ring_z(k)), stages[i].at[k % 2], local.at[i, k % 2]
        )
        copy.start()
        live[i]["o", k] = copy

    def stage(i, s):
        first, second, third = orders[i]
        acc, mine = accs[i], live[i]
        early, ring, late = firsts[i], rings[i], lasts[i]

        def part(k, flip=0, flip2=None):
            own = {axis: getattr(place, axis) for axis in "xy"}
            own[first] = own[first] + flip * (1 - 2 * own[first])
            if flip2 is None:
                own["xy".replace(first, "")] = pl.ds(0, 2)
            else:
                other = "xy".replace(first, "")
                own[other] = own[other] + flip2 * (1 - 2 * own[other])
            return acc.at[k - 1, own["x"], own["y"]]

        if s == 0:
            for k in range(1, nz + 1):
                src = block_of(ins[i], cuts[i], 1 - place.c, place.ring_z(k))
                mine["c", k] = put(i, k, src, acc.at[k - 1], place.other("c"))
            load(i, 1)
            load(i, 2)
        if 1 <= s <= nz:
            k = s
            mine["c", k].wait_recv()
            mine["o", k].wait()
            add_to(acc.at[k - 1], stages[i].at[k % 2])
            if k + 2 <= nz:
                load(i, k + 2)
            mine["p", k] = put(i, nz + k, part(k, 1), early.at[k - 1], place.other(first))
        if 2 <= s <= nz + 1:
            k = s - 1
            mine["p", k].wait_recv()
            add_to(part(k), early.at[k - 1])
        if second == "z":
            if s == 2:
                mine["z", 1] = put(i, 2 * nz + 1, part(1), ring.at[0], place.succ())
            if 3 <= s <= nz + 1:
                t = s - 2
                mine["z", t].wait_recv()
                add_to(ring.at[t - 1], part(t + 1))
                if t < nz - 1:
                    mine["z", t + 1] = put(i, 2 * nz + t + 1, ring.at[t - 1], ring.at[t], place.succ())
                else:
                    there = 1 - getattr(place, third)
                    mine["l"] = put(i, 3 * nz + 1, ring.at[t - 1, there], late, place.other(third))
            if s == nz + 2:
                mine["l"].wait_recv()
                outs[i][...] = wide(ring[nz - 2, getattr(place, third)]) + wide(late[...])
        else:
            if 2 <= s <= nz + 1:
                k = s - 1
                mine["l", k] = put(i, 3 * nz + k, part(k, 0, 1), late.at[k - 1], place.other(second))
            if 3 <= s <= nz + 2:
                k = s - 2
                mine["l", k].wait_recv()
                add_to(part(k, 0, 0), late.at[k - 1])
                if k == 1:
                    mine["z", 1] = put(i, 2 * nz + 1, part(1, 0, 0), ring.at[0], place.succ())
                else:
                    t = k - 1
                    mine["z", t].wait_recv()
                    if t < nz - 1:
                        add_to(ring.at[t - 1], part(t + 1, 0, 0))
                        mine["z", t + 1] = put(i, 2 * nz + t + 1, ring.at[t - 1], ring.at[t], place.succ())
                    else:
                        outs[i][...] = wide(ring[t - 1]) + wide(part(nz, 0, 0)[...])

    stages_of = nz + 3
    for t in range(stages_of + max(starts)):
        for i in range(n):
            if 0 <= t - starts[i] < stages_of:
                stage(i, t - starts[i])
        if t == 0:
            swapped.start()
    for copy in started:
        copy.wait_send()
    swapped.wait()


def finish_kernel(count, *refs):
    n = (len(refs) - 7 - count) // 3
    here, other, ins, packed, refs = refs[:2], refs[2:4], refs[4 : 4 + n], refs[4 + n], refs[5 + n :]
    outs, vectors, held, (rows, sem) = refs[: 2 + n], refs[2 + n : 2 + n + count], refs[2 + n + count : -2], refs[-2:]
    x = lax.axis_index("segment")
    moves = []
    for j in range(2):
        moves.append((here[j].at[x], rows.at[j, 0], outs[j].at[x]))
        moves.append((other[j], rows.at[j, 1], outs[j].at[1 - x]))
    moves += list(zip(ins, held, outs[2:]))
    steps = []
    for j, (src, via, dst) in enumerate(moves):
        steps.append((pltpu.make_async_copy(src, via, sem.at[j, 0]), pltpu.make_async_copy(via, dst, sem.at[j, 1])))
        steps[-1][0].start()
    row = 0
    for dst in vectors:
        size, at = dst.shape[1], 0
        while at < size:
            more = min(128, size - at)
            dst[:, at : at + more] = packed[row : row + 1, :more]
            at, row = at + more, row + 1
    for load, store in steps:
        load.wait()
        store.start()
    for load, store in steps:
        store.wait()


def finish(rows, others, arrays, packed, sizes):
    like = [jax.ShapeDtypeStruct(a.shape, a.dtype) for a in list(rows) + list(arrays)]
    vectors = [jax.ShapeDtypeStruct((1, size), jnp.float32) for size in sizes]
    far, near = pl.BlockSpec(memory_space=pl.ANY), pl.BlockSpec(memory_space=pltpu.VMEM)
    got = pl.pallas_call(
        functools.partial(finish_kernel, len(sizes)),
        out_shape=like + vectors,
        in_specs=[far] * (4 + len(arrays)) + [near],
        out_specs=[far] * len(like) + [near] * len(sizes),
        scratch_shapes=[pltpu.VMEM(a.shape, a.dtype) for a in arrays]
        + [pltpu.VMEM((2,) + rows[0].shape, rows[0].dtype), pltpu.SemaphoreType.DMA((4 + len(arrays), 2))],
        compiler_params=pltpu.CompilerParams(vmem_limit_bytes=62 * 2**20),
        name="finish",
    )(*rows, *others, *arrays, packed)
    return got[: len(like)], got[len(like) :]


def from_other(rows):
    return lax.ppermute(rows[1 - lax.axis_index("segment")], "segment", [(0, 1), (1, 0)])


def scatter_all(grads, plan, mesh, rows):
    nx, ndp = mesh.shape["segment"], mesh.shape["dp"]
    if nx != 2 or ndp != 16:
        return [wide(lax.psum_scatter(g, AXES, scatter_dimension=0, tiled=False)) for g in grads], from_other(rows)
    nz, n = ndp // 4, len(grads)

    def scratch(lead):
        return [
            pltpu.VMEM(lead(order) + part_shape(grads[k].shape[1:], part), grads[k].dtype)
            for k, part, order, _ in plan
        ]

    slots = 4 * nz + 2
    far, near = pl.BlockSpec(memory_space=pl.ANY), pl.BlockSpec(memory_space=pltpu.VMEM)
    got = pl.pallas_call(
        functools.partial(scatter_kernel, plan, nz),
        out_shape=[jax.ShapeDtypeStruct(g.shape[1:], jnp.float32) for g in grads]
        + [jax.ShapeDtypeStruct(rows.shape[1:], rows.dtype)],
        in_specs=[far] * (n + 1),
        out_specs=[near] * n + [far],
        scratch_shapes=scratch(lambda o: (nz, 2, 2))
        + scratch(lambda o: (2, 2, 2))
        + scratch(lambda o: (nz, 2))
        + scratch(lambda o: (nz - 1, 2) if o[1] == "z" else (nz - 1,))
        + scratch(lambda o: () if o[1] == "z" else (nz,))
        + [
            pltpu.SemaphoreType.DMA((len(plan), slots)),
            pltpu.SemaphoreType.DMA((len(plan), slots)),
            pltpu.SemaphoreType.DMA((len(plan), 2)),
            pltpu.SemaphoreType.DMA((2,)),
        ],
        compiler_params=pltpu.CompilerParams(
            collective_id=1, has_side_effects=True, vmem_limit_bytes=62 * 2**20
        ),
        name="sum_gradients",
    )(*[g.reshape((2, nz, 2, 2) + g.shape[1:]) for g in grads], rows)
    return got[:n], got[n]


ROWS = 512
HIDDEN = 768
GAIN1, BIAS1, VALUE_B, OUT_B, GAIN2, BIAS2, OUTER_B, FIRST_B = range(8)
VECTOR_ROWS = 7


def rows_for(size):
    return -(-size // 128)


def pieces_of(size, row):
    return [(row + j, j * 128, min(128, size - j * 128)) for j in range(rows_for(size))]


def unpack_rows(small, at, ndp, row, ref):
    size = ref.shape[1] // ndp
    for d in range(ndp):
        for r, lo, n in pieces_of(size, row):
            ref[:, d * size + lo : d * size + lo + n] = wide(small[at + d])[r : r + 1, :n]


def unpack_vectors(small, at, ndp, ref):
    size = ref.shape[1] // ndp
    for d in range(ndp):
        ref[:, d * size : (d + 1) * size] = wide(small[at + d])[: ref.shape[0], :size]


def pack_rows(ref, ndp, row, small, at):
    size = ref.shape[1] // ndp
    for d in range(ndp):
        for r, lo, n in pieces_of(size, row):
            small[at + d, r : r + 1, :n] = ref[:, d * size + lo : d * size + lo + n]


def pack_vectors(ref, ndp, small, at):
    size = ref.shape[1] // ndp
    for d in range(ndp):
        small[at + d, :VECTOR_ROWS, :size] = ref[:VECTOR_ROWS, d * size : (d + 1) * size]


def chunks(rows, size=ROWS):
    return [slice(at, at + size) for at in range(0, rows, size)]


def norm_parts(rows):
    centre = rows - jnp.mean(rows, axis=-1, keepdims=True)
    inv = lax.rsqrt(jnp.mean(centre * centre, axis=-1, keepdims=True) + EPSILON)
    return centre * inv, inv


def row_loop(rows, body, init):
    return lax.fori_loop(0, rows // 128, lambda j, c: body(pl.ds(pl.multiple_of(j * 128, 128), 128), c), init)


def norm_into(read, write, gain, shift, rows):
    def body(r, carry):
        write[r, :] = half(norm_parts(read(r))[0] * gain + shift)
        return carry

    row_loop(rows, body, 0)


def norm_back(read, grad, gain, rows, done):
    def body(r, carry):
        normal, inv = norm_parts(read(r))
        m_hat = grad(r)
        m = m_hat * gain
        part = inv * (
            m - jnp.mean(m, axis=-1, keepdims=True) - normal * jnp.mean(m * normal, axis=-1, keepdims=True)
        )
        done(r, part)
        return carry[0] + sums(m_hat * normal), carry[1] + sums(m_hat)

    zero = jnp.zeros_like(gain)
    return row_loop(rows, body, (zero, zero))


def sums(value):
    return jnp.sum(wide(value), axis=0, keepdims=True)


def gelu_both(t):
    square = t * t
    s = 0.5 + 0.5 * jnp.tanh(t * (GELU_SCALE + GELU_SCALE * 0.044715 * square))
    value = t * s
    slope = s + value * (1.0 - s) * (2 * GELU_SCALE + 6 * GELU_SCALE * 0.044715 * square)
    return value, slope


def masked_pair(head):
    return lax.broadcasted_iota(jnp.int32, (1, 2 * head), 1) < head


def add_up(fresh, ref, at, value):
    @pl.when(fresh)
    def _():
        ref[at] = value

    @pl.when(jnp.logical_not(fresh))
    def _():
        ref[at] += value


def forward_start(read, vec, value_ref, a_ref, v_ref, first=None):
    rows = a_ref.shape[0]
    norm_into(read, a_ref, vec(GAIN1), vec(BIAS1), rows)
    for r in chunks(rows):
        v_ref[r] = half(mm(a_ref[r], value_ref[...]) + vec(VALUE_B))
        if first is not None:
            first_ref, first_b, p_ref, slope_ref = first
            value, slope = gelu_both(mm(a_ref[r], first_ref[...]) + first_b[...])
            p_ref[r] = half(value)
            slope_ref[r] = half(slope)


def both_heads(pair, head):
    lower = masked_pair(head)
    zero = jnp.zeros_like(pair)
    return jnp.concatenate([jnp.where(lower, pair, zero), jnp.where(lower, zero, pair)], axis=0)


def forward_heads(pair, length, v_ref, c_ref, probs_ref, logits_of, bounded=False):
    rows, width = v_ref.shape
    slots = probs_ref.shape[1] // 2
    head = width // HEADS
    at = pl.ds(pl.multiple_of(pair * 2 * head, 2 * head), 2 * head)
    shut = jnp.where(lax.broadcasted_iota(jnp.int32, (1, slots), 1) >= length, -1e30, 0.0)
    both = logits_of(shut)
    for h in range(2):
        logits = both[h]
        expo = jnp.exp(logits if bounded else logits - jnp.max(logits, axis=1, keepdims=True))
        probs_ref[:, h * slots : (h + 1) * slots] = half(expo * (1.0 / jnp.sum(expo, axis=1, keepdims=True)))
    c_ref[:, at] = half(mm(probs_ref[...], both_heads(v_ref[:, at], head)))


def forward_middle(read, vec, out_ref, c_ref, hid_ref, b_ref):
    rows = c_ref.shape[0]
    for r in chunks(rows):
        hid_ref[r] = read(r) + mm(c_ref[r], out_ref[...]) + vec(OUT_B)
    norm_into(lambda r: hid_ref[r, :], b_ref, vec(GAIN2), vec(BIAS2), rows)


def forward_hidden(fresh, b_ref, inner_ref, inner_b, outer_ref, q_ref, slope_ref, acc):
    for r in chunks(b_ref.shape[0]):
        value, slope = gelu_both(mm(b_ref[r], inner_ref[...]) + inner_b)
        q = half(value)
        q_ref[r] = q
        slope_ref[r] = half(slope)
        add_up(fresh, acc, r, mm(q, outer_ref[...]))


def forward_end(vec, hid_ref, acc, y_ref):
    for r in chunks(acc.shape[0]):
        y_ref[r] = half(hid_ref[r] + acc[r] + vec(OUTER_B))


def backward_hidden(fresh, g_ref, b_ref, q_ref, slope_ref, inner_ref, outer_ref, gz_ref, acc, g_outer, g_inner, g_inner_b):
    for r in chunks(g_ref.shape[0]):
        gz = half(mm_nt(g_ref[r], outer_ref[...]) * wide(slope_ref[r]))
        gz_ref[r] = gz
        add_up(fresh, acc, r, mm_nt(gz, inner_ref[...]))
    gz = gz_ref[...]
    g_outer[...] = half(mm_tn(q_ref[...], g_ref[...]))
    g_inner[...] = half(mm_tn(b_ref[...], gz))
    g_inner_b[...] = sums(gz)


def backward_middle(vec, put, g_ref, hid_ref, c_ref, out_ref, acc, ghid, gatt, gc_ref, g_out):
    rows = g_ref.shape[0]

    def done(r, part):
        total = wide(g_ref[r, :]) + part
        ghid[r, :] = total
        gatt[r, :] = half(total)

    gain, shift = norm_back(lambda r: hid_ref[r, :], lambda r: acc[r, :], vec(GAIN2), rows, done)
    put(GAIN2, gain)
    put(BIAS2, shift)
    put(OUTER_B, sums(g_ref[...]))
    put(OUT_B, sums(gatt[...]))
    g_out[...] = half(mm_tn(c_ref[...], gatt[...]))
    for r in chunks(rows):
        gc_ref[r] = half(mm_nt(gatt[r], out_ref[...]))


def backward_heads(pair, v_ref, c_ref, gc_ref, gv_ref, probs_ref, db):
    rows, width = v_ref.shape
    slots = probs_ref.shape[1] // 2
    head = width // HEADS
    at = pl.ds(pl.multiple_of(pair * 2 * head, 2 * head), 2 * head)
    both = mm_nt(gc_ref[:, at], both_heads(v_ref[:, at], head))
    along = wide(gc_ref[:, at]) * wide(c_ref[:, at])
    lower = masked_pair(head)
    for h in range(2):
        cols = slice(h * slots, (h + 1) * slots)
        mean = jnp.sum(jnp.where(lower if h == 0 else jnp.logical_not(lower), along, 0.0), axis=1, keepdims=True)
        db[:, cols] = half(wide(probs_ref[:, cols]) * (both[:, cols] - mean))
    values = mm_tn(probs_ref[...], gc_ref[:, at])
    gv_ref[:, at] = half(jnp.where(masked_pair(head), values[:slots], values[slots:]))


def backward_end(vec, put, read, gv_ref, value_ref, a_ref, acc, ghid, g_value, gx_ref, first=None):
    rows = gv_ref.shape[0]
    put(VALUE_B, sums(gv_ref[...]))
    g_value[...] = half(mm_tn(a_ref[...], gv_ref[...]))
    if first is not None:
        first_ref, slope_ref, gf_ref, g_first = first
        for r in chunks(rows):
            gf_ref[r] = half(acc[r] * wide(slope_ref[r]))
        put(FIRST_B, sums(gf_ref[...]))
        g_first[...] = half(mm_tn(a_ref[...], gf_ref[...]))
    else:
        put(FIRST_B, jnp.zeros((1, acc.shape[1]), jnp.float32))
    for r in chunks(rows):
        ga = mm_nt(gv_ref[r], value_ref[...])
        if first is not None:
            ga = ga + mm_nt(gf_ref[r], first_ref[...])
        acc[r] = ga

    def done(r, part):
        gx_ref[r, :] = half(ghid[r, :] + part)

    gain, shift = norm_back(read, lambda r: acc[r, :], vec(GAIN1), rows, done)
    put(GAIN1, gain)
    put(BIAS1, shift)


def forward_kernel(pairs, parts, length_ref, x_ref, small, value_ref, out_ref, first_ref, second_ref, inner_ref, outer_ref, y_ref, *refs):
    kept, probs_ref, q_ref, slope_ref = refs[:7], refs[7], refs[8], refs[9]
    a_ref, v_ref, p_ref, first_slope, c_ref, b_ref, hid_ref, acc, vectors, inner_b, first_b, second_b, sem = refs[10:]
    held = (a_ref, v_ref, p_ref, first_slope, c_ref, b_ref, hid_ref)
    copies = [pltpu.make_async_copy(src, dst, sem.at[j]) for j, (src, dst) in enumerate(zip(held, kept))]
    i = pl.program_id(0)
    slots = probs_ref.shape[2] // 2
    ndp, part = small.shape[0] // 2, q_ref.shape[1]

    def vec(k):
        return vectors[k : k + 1, :]

    x_ref, y_ref = x_ref.at[0], y_ref.at[0]

    def read(r):
        return wide(x_ref[r, :])

    @pl.when(i == 0)
    def _():
        unpack_vectors(small, 0, ndp, vectors)
        unpack_rows(small, 0, ndp, VECTOR_ROWS, inner_b)
        row = VECTOR_ROWS + rows_for(inner_b.shape[1] // ndp)
        unpack_rows(small, 0, 2 * ndp, row, first_b)
        unpack_rows(small, 0, 2 * ndp, row + rows_for(first_b.shape[1] // (2 * ndp)), second_b)
        forward_start(read, vec, value_ref.at[0], a_ref, v_ref, (first_ref, first_b, p_ref, first_slope))
        for copy in copies[:4]:
            copy.start()

    @pl.when(i < pairs)
    def _():
        def logits_of(shut):
            bias = second_b[:, pl.ds(pl.multiple_of(i * 2 * slots, 2 * slots), 2 * slots)]
            logits = mm(p_ref[...], second_ref[...]) + (bias + jnp.concatenate([shut, shut], axis=1))
            return logits[:, :slots], logits[:, slots:]

        forward_heads(i, length_ref[0], v_ref, c_ref, probs_ref.at[0], logits_of)

    @pl.when(i == pairs - 1)
    def _():
        forward_middle(read, vec, out_ref.at[0], c_ref, hid_ref, b_ref)
        for copy in copies[4:]:
            copy.start()

    @pl.when(i >= pairs)
    def _():
        bias = inner_b[:, pl.ds(pl.multiple_of((i - pairs) * part, part), part)]
        forward_hidden(i == pairs, b_ref, inner_ref.at[0], bias, outer_ref.at[0], q_ref, slope_ref, acc)

    @pl.when(i == pairs + parts - 1)
    def _():
        forward_end(vec, hid_ref, acc, y_ref)
        for copy in copies:
            copy.wait()


def backward_kernel(pairs, parts, g_ref, b_ref, small, g_small1, q_ref, slope_ref, probs_ref, inner_ref, outer_ref, second_ref, *refs):
    far, refs = refs[:10], refs[14:]
    gx_ref, g_outer, g_inner, g_out, g_value, g_small, g_first, g_second = refs[:8]
    near, refs = refs[8:18], refs[18:]
    acc, ghid, gatt, gc_ref, gv_ref, db, gz_ref, vectors, g_vec, g_inner_b, g_second_b, sem = refs
    far = [ref.at[0] if len(ref.shape) == 3 else ref for ref in far]
    copies = [pltpu.make_async_copy(src, dst, sem.at[j]) for j, (src, dst) in enumerate(zip(far, near))]
    hid_ref, c_ref, out_ref, v_ref, p_ref, a_ref, value_ref, first_ref, first_slope, x_ref = near
    g_ref, gx_ref = g_ref.at[0], gx_ref.at[0]
    i = pl.program_id(0)
    slots = probs_ref.shape[2] // 2
    ndp, part = small.shape[0] // 2, q_ref.shape[1]

    def vec(k):
        return vectors[k : k + 1, :]

    def put(k, value):
        g_vec[k : k + 1, :] = value

    @pl.when(i == 0)
    def _():
        for copy in copies:
            copy.start()
        unpack_vectors(small, 0, ndp, vectors)

    @pl.when(i < parts)
    def _():
        bias = g_inner_b.at[:, pl.ds(pl.multiple_of(i * part, part), part)]
        backward_hidden(i == 0, g_ref, b_ref, q_ref, slope_ref, inner_ref.at[0], outer_ref.at[0], gz_ref, acc, g_outer.at[0], g_inner.at[0], bias)

    @pl.when(i == parts - 1)
    def _():
        for copy in copies[:3]:
            copy.wait()
        backward_middle(vec, put, g_ref, hid_ref, c_ref, out_ref, acc, ghid, gatt, gc_ref, g_out.at[0])
        for copy in copies[3:5]:
            copy.wait()

    @pl.when(i >= parts)
    def _():
        backward_heads(i - parts, v_ref, c_ref, gc_ref, gv_ref, probs_ref.at[0], db)
        g_second[...] = half(mm_tn(p_ref[...], db[...]))
        g_second_b[:, pl.ds(pl.multiple_of((i - parts) * 2 * slots, 2 * slots), 2 * slots)] = sums(db[...])
        add_up(i == parts, acc, slice(None), mm_nt(db[...], second_ref[...]))

    @pl.when(i == pairs + parts - 1)
    def _():
        for copy in copies[5:]:
            copy.wait()
        backward_end(
            vec, put, lambda r: wide(x_ref[r, :]), gv_ref, value_ref, a_ref, acc, ghid, g_value.at[0], gx_ref,
            (first_ref, first_slope, gatt, g_first),
        )
        g_small[:ndp] = jnp.zeros_like(g_small1)
        g_small[ndp:] = g_small1[...]
        pack_vectors(g_vec, ndp, g_small, 0)
        pack_rows(g_inner_b, ndp, VECTOR_ROWS, g_small, 0)
        row = VECTOR_ROWS + rows_for(g_inner_b.shape[1] // ndp)
        pack_rows(g_vec.at[FIRST_B : FIRST_B + 1, :], 2 * ndp, row, g_small, 0)
        row += rows_for(g_vec.shape[1] // (2 * ndp))
        pack_rows(g_second_b, 2 * ndp, row, g_small, 0)


def both_kernel(pairs, parts, length_ref, x_ref, g_ref, small, value_ref, out_ref, table_ref, inner_ref, outer_ref, *refs):
    y_ref, gx_ref, g_outer, g_inner, g_out, g_value, g_small, g_table = refs[:8]
    acc, hid_ref, ghid, a_ref, v_ref, c_ref, b_ref, gatt, gc_ref, gv_ref, probs_ref, q_ref, slope_ref, db, gz_ref, *refs = refs[8:]
    vectors, inner_b, g_vec, g_inner_b = refs
    i = pl.program_id(0)
    slots = probs_ref.shape[2] // 2
    j = i - pairs
    k = j - parts
    n = k - parts

    ndp, part = small.shape[0] // 2, q_ref.shape[2]

    def vec(k):
        return vectors[k : k + 1, :]

    def put(k, value):
        g_vec[k : k + 1, :] = value

    def hidden(ref, k):
        return ref.at[:, pl.ds(pl.multiple_of(k * part, part), part)]

    x_ref, g_ref, y_ref, gx_ref = (ref.at[0] for ref in (x_ref, g_ref, y_ref, gx_ref))

    def read(r):
        return wide(x_ref[r, :])

    @pl.when(i == 0)
    def _():
        unpack_vectors(small, ndp, ndp, vectors)
        unpack_rows(small, ndp, ndp, VECTOR_ROWS, inner_b)
        forward_start(read, vec, value_ref.at[0], a_ref, v_ref)

    @pl.when(i < pairs)
    def _():
        def logits_of(shut):
            return wide(table_ref[:slots, :]) + shut, wide(table_ref[slots:, :]) + shut

        forward_heads(i, length_ref[0], v_ref, c_ref, probs_ref.at[i], logits_of, True)

    @pl.when(i == pairs - 1)
    def _():
        forward_middle(read, vec, out_ref.at[0], c_ref, hid_ref, b_ref)

    @pl.when((j >= 0) & (j < parts))
    def _():
        forward_hidden(j == 0, b_ref, inner_ref.at[0], hidden(inner_b, j)[...], outer_ref.at[0], q_ref.at[j], slope_ref.at[j], acc)

    @pl.when(j == parts - 1)
    def _():
        forward_end(vec, hid_ref, acc, y_ref)

    @pl.when((k >= 0) & (k < parts))
    def _():
        at = parts - 1 - k
        backward_hidden(k == 0, g_ref, b_ref, q_ref.at[at], slope_ref.at[at], inner_ref.at[0], outer_ref.at[0], gz_ref, acc, g_outer.at[0], g_inner.at[0], hidden(g_inner_b, at))

    @pl.when(k == parts - 1)
    def _():
        backward_middle(vec, put, g_ref, hid_ref, c_ref, out_ref.at[0], acc, ghid, gatt, gc_ref, g_out.at[0])

    @pl.when(n >= 0)
    def _():
        backward_heads(n, v_ref, c_ref, gc_ref, gv_ref, probs_ref.at[n], db)
        g_table[:slots, :] = db[:, :slots]
        g_table[slots:, :] = db[:, slots:]

    @pl.when(n == pairs - 1)
    def _():
        backward_end(vec, put, read, gv_ref, value_ref.at[0], a_ref, acc, ghid, g_value.at[0], gx_ref)
        g_small[...] = jnp.zeros_like(g_small)
        pack_vectors(g_vec, ndp, g_small, 0)
        pack_rows(g_inner_b, ndp, VECTOR_ROWS, g_small, 0)


class Weights(NamedTuple):
    small: Any
    value: Any
    out: Any
    inner: Any
    outer: Any
    first: Any
    second: Any
    table: Any


def whole(shape, *at):
    at = tuple(at)
    block = (1,) * len(at) + tuple(shape[len(at) :])
    return pl.BlockSpec(block, lambda i: at + (0,) * (len(shape) - len(at)), pipeline_mode=pl.Buffered(1))


def whole_out(shape, *at):
    at = tuple(at)
    block = (1,) * len(at) + tuple(shape[len(at) :])
    return pl.BlockSpec(block, lambda i: at + (0,) * (len(shape) - len(at)))


def like(shape, dtype=jnp.bfloat16):
    return jax.ShapeDtypeStruct(shape, dtype)


FAR = pl.BlockSpec(memory_space=pl.ANY)


def sizes_of(x, w):
    rows, width = x.shape[-2:]
    parts = w.inner.shape[2] // HIDDEN
    return rows, width, HEADS // 2, parts, w.inner.shape[2] // parts


def forward(x, length, w):
    rows, width, pairs, parts, part = sizes_of(x, w)
    slots = rows

    def pair(i):
        return jnp.minimum(i, pairs - 1)

    def piece(i):
        return jnp.maximum(i - pairs, 0)

    ins = [length, x, w.small, w.value, w.out, w.first, w.second, w.inner, w.outer]
    specs = [
        pl.BlockSpec(memory_space=pltpu.SMEM),
        whole(x.shape, 0),
        whole(w.small.shape),
        whole(w.value.shape, 0),
        whole(w.out.shape, 0),
        whole(w.first.shape),
        pl.BlockSpec((width, 2 * slots), lambda i: (0, pair(i))),
        pl.BlockSpec((1, width, part), lambda i: (0, 0, piece(i))),
        pl.BlockSpec((1, part, width), lambda i: (0, piece(i), 0)),
    ]
    half_rows = like((rows, width))
    kept = [half_rows] * 6 + [like((rows, width), jnp.float32)]
    hidden_block = pl.BlockSpec((rows, part), lambda i: (0, piece(i)))
    y, *saved = pl.pallas_call(
        functools.partial(forward_kernel, pairs, parts),
        grid=(pairs + parts,),
        out_shape=[like(x.shape)] + kept + [like((pairs, rows, 2 * slots))] + [like((rows, part * parts))] * 2,
        in_specs=specs,
        out_specs=[whole_out(x.shape, 0)]
        + [FAR] * 7
        + [pl.BlockSpec((1, rows, 2 * slots), lambda i: (pair(i), 0, 0))]
        + [hidden_block] * 2,
        scratch_shapes=[pltpu.VMEM(k.shape, k.dtype) for k in kept]
        + [
            pltpu.VMEM((rows, width), jnp.float32),
            pltpu.VMEM((8, width), jnp.float32),
            pltpu.VMEM((1, part * parts), jnp.float32),
            pltpu.VMEM((1, width), jnp.float32),
            pltpu.VMEM((1, w.second.shape[1]), jnp.float32),
            pltpu.SemaphoreType.DMA((7,)),
        ],
        compiler_params=pltpu.CompilerParams(vmem_limit_bytes=62 * 2**20),
        name="forward_0",
    )(*ins)
    return y, saved


def backward(g, x, saved, w, before, small1):
    rows, width, pairs, parts, part = sizes_of(x, w)
    slots = rows
    a, v, p, first_slope, c, b, hid, probs, q, slope = saved

    def pair(i):
        return jnp.maximum(i - parts, 0)

    def piece(i):
        return jnp.minimum(i, parts - 1)

    hidden_block = pl.BlockSpec((rows, part), lambda i: (0, piece(i)))
    inner_block = pl.BlockSpec((1, width, part), lambda i: (0, 0, piece(i)))
    outer_block = pl.BlockSpec((1, part, width), lambda i: (0, piece(i), 0))
    second_block = pl.BlockSpec((width, 2 * slots), lambda i: (0, pair(i)))
    far = [hid, c, w.out, v, p, a, w.value, w.first, first_slope, x]
    ins = [g, b, w.small, small1, q, slope, probs, w.inner, w.outer, w.second] + far
    specs = [whole(g.shape, 1), whole((rows, width)), whole(w.small.shape), whole(small1.shape)] + [hidden_block] * 2
    specs += [pl.BlockSpec((1, rows, 2 * slots), lambda i: (pair(i), 0, 0)), inner_block, outer_block, second_block]
    specs += [FAR] * 10
    aliases = {len(ins) + j: 1 + j for j in range(4)}
    aliases[0] = 0
    ins += list(before)
    specs += [FAR] * 4
    outs = [like(g.shape)] + [like(k.shape, k.dtype) for k in before]
    out_specs = [whole_out(g.shape, 0), outer_block, inner_block]
    out_specs += [whole_out(w.out.shape, 0), whole_out(w.value.shape, 0)]
    outs += [like(w.small.shape, jnp.float32), like(w.first.shape), like(w.second.shape)]
    out_specs += [whole_out(w.small.shape), whole_out(w.first.shape), second_block]
    gx, *grads = pl.pallas_call(
        functools.partial(backward_kernel, pairs, parts),
        grid=(pairs + parts,),
        out_shape=outs,
        in_specs=specs,
        out_specs=out_specs,
        scratch_shapes=[pltpu.VMEM(k.shape[-2:], k.dtype) for k in far]
        + [pltpu.VMEM((rows, width), jnp.float32)] * 2
        + [pltpu.VMEM((rows, width), jnp.bfloat16)] * 3
        + [pltpu.VMEM((rows, 2 * slots), jnp.bfloat16), pltpu.VMEM((rows, part), jnp.bfloat16)]
        + [pltpu.VMEM((8, width), jnp.float32)] * 2
        + [pltpu.VMEM((1, part * parts), jnp.float32), pltpu.VMEM((1, w.second.shape[1]), jnp.float32)]
        + [pltpu.SemaphoreType.DMA((10,))],
        input_output_aliases=aliases,
        compiler_params=pltpu.CompilerParams(vmem_limit_bytes=62 * 2**20),
        name="backward_0",
    )(*ins)
    return gx, grads[:4], grads[4:]


def both_ways(x, g, length, w):
    rows, width, pairs, parts, part = sizes_of(x, w)
    slots = rows

    def there(i):
        return jnp.minimum(i, pairs - 1)

    def back(i):
        return jnp.maximum(i - pairs - 2 * parts, 0)

    def piece(i):
        j = jnp.clip(i - pairs, 0, 2 * parts - 1)
        return jnp.minimum(j, 2 * parts - 1 - j)

    def late(i):
        return parts - 1 - jnp.clip(i - pairs - parts, 0, parts - 1)

    ins = [length, x, g, w.small, w.value, w.out, w.table, w.inner, w.outer]
    specs = [pl.BlockSpec(memory_space=pltpu.SMEM), whole(x.shape, 0), whole(g.shape, 1)]
    specs += [whole(w.small.shape), whole(w.value.shape, 1), whole(w.out.shape, 1)]
    specs += [
        pl.BlockSpec((2 * slots, slots), lambda i: (there(i), 0)),
        pl.BlockSpec((1, width, part), lambda i: (1, 0, piece(i))),
        pl.BlockSpec((1, part, width), lambda i: (1, piece(i), 0)),
    ]
    grads = [like(w.outer.shape), like(w.inner.shape), like(w.out.shape), like(w.value.shape)]
    small = (w.small.shape[0] // 2,) + w.small.shape[1:]
    grads += [like(small, jnp.float32), like(w.table.shape)]
    grad_specs = [
        pl.BlockSpec((1, part, width), lambda i: (1, late(i), 0)),
        pl.BlockSpec((1, width, part), lambda i: (1, 0, late(i))),
        whole_out(w.out.shape, 1),
        whole_out(w.value.shape, 1),
        whole_out(small),
        pl.BlockSpec((2 * slots, slots), lambda i: (back(i), 0)),
    ]
    y, gx, *grads = pl.pallas_call(
        functools.partial(both_kernel, pairs, parts),
        grid=(2 * pairs + 2 * parts,),
        out_shape=[like(x.shape)] * 2 + grads,
        in_specs=specs,
        out_specs=[whole_out(x.shape, 1)] * 2 + grad_specs,
        scratch_shapes=[pltpu.VMEM((rows, width), jnp.float32)] * 3
        + [pltpu.VMEM((rows, width), jnp.bfloat16)] * 7
        + [pltpu.VMEM((pairs, rows, 2 * slots), jnp.bfloat16)]
        + [pltpu.VMEM((parts, rows, part), jnp.bfloat16)] * 2
        + [pltpu.VMEM((rows, 2 * slots), jnp.bfloat16), pltpu.VMEM((rows, part), jnp.bfloat16)]
        + [pltpu.VMEM((8, width), jnp.float32), pltpu.VMEM((1, part * parts), jnp.float32)] * 2,
        input_output_aliases={1: 0},
        compiler_params=pltpu.CompilerParams(vmem_limit_bytes=62 * 2**20),
        name="forward_backward_1",
    )(*ins)
    return y, gx, grads[:4], grads[4], grads[5]


ROW_VECTORS = (0, 1, 3, 5, 6, 7, 11)
VECTORS = ROW_VECTORS + (9, 13, 15)
MATRICES = (2, 4, 8, 10, 12, 14, 16)
SMALL = 17
GATHER = (
    (8, 0, "xzy", 2),
    (SMALL, None, "xzy", 3),
    (10, 1, "zyx", 1),
    (2, None, "zyx", 0),
    (16, 0, "zxy", 1),
    (10, 0, "yzx", 2),
    (12, None, "zyx", 0),
    (16, 1, "xzy", 0),
    (8, 1, "yzx", 2),
    (4, None, "zyx", 0),
    (14, 0, "xzy", 2),
    (14, 1, "xzy", 0),
)
SUM = (
    (8, 1, "yzx", 3),
    (8, 0, "xzy", 4),
    (4, None, "yzx", 1),
    (14, 1, "yxz", 4),
    (16, 0, "xzy", 3),
    (12, None, "yzx", 0),
    (10, 1, "yxz", 4),
    (2, None, "yzx", 1),
    (SMALL, None, "xzy", 4),
    (16, 1, "xzy", 1),
    (14, 0, "yxz", 4),
    (10, 0, "xzy", 3),
)


def planned(call, plan, arrays, mesh, rows):
    names = list(dict.fromkeys(entry[0] for entry in plan))
    plan = [(names.index(entry[0]),) + entry[1:] for entry in plan]
    got, rows = call([arrays[k] for k in names], plan, mesh, rows)
    return dict(zip(names, got)), rows


def lanes(vector):
    rows = rows_for(vector.size)
    return jnp.pad(vector.reshape(-1), (0, rows * 128 - vector.size)).reshape(rows, 128)


def sixteens(rows):
    return jnp.pad(rows, ((0, -rows.shape[0] % 16), (0, 0)))


def per_device(mesh, boundary, lengths, *parts):
    nx, ndp = mesh.shape["segment"], mesh.shape["dp"]
    devices = nx * ndp
    first = lax.axis_index("segment") == 0
    length = jnp.where(first, lengths[0], lengths[1])
    sizes = [parts[k].size for k in VECTORS]

    shards = {k: parts[k].reshape(parts[k].shape[-2:]) for k in MATRICES}
    shards[SMALL] = [parts[k].reshape(1, -1) for k in VECTORS]
    full, pair = planned(gather_all, GATHER, shards, mesh, boundary[0, :, 0])
    for k in MATRICES:
        g = full[k]
        full[k] = g.reshape((nx, ndp * g.shape[1]) + g.shape[2:]) if k < 12 else g.reshape(-1, g.shape[2])
    w = Weights(full[SMALL], full[2], full[4], full[8], full[10], full[12], full[14], full[16])

    outs, saved = forward(pair, length, w)
    outs, gins, both, g_small, g_table = both_ways(outs, pair, length, w)
    other_outs = from_other(outs)
    gins, both, synth = backward(gins, pair, saved, w, both, g_small)

    g_outer, g_inner, g_out, g_value = both
    g_small, g_first, g_second = synth
    matrices = (g_value, g_out, g_inner, g_outer, g_first, g_second, g_table)
    grads = {k: g.reshape((devices,) + parts[k].shape[-2:]) for k, g in zip(MATRICES, matrices)}
    grads[SMALL] = g_small
    summed, other_gins = planned(scatter_all, SUM, grads, mesh, gins)
    arrays, vectors = finish([outs, gins], [other_outs, other_gins], [summed[k] for k in MATRICES], summed[SMALL], sizes)
    result = {k: g.reshape(parts[k].shape) for k, g in zip(MATRICES, arrays[2:])}
    for k, g in zip(VECTORS, vectors):
        result[k] = g.reshape(parts[k].shape)
    return tuple(a.reshape(boundary.shape) for a in arrays[:2]) + tuple(result[k] for k in range(17))


def solution(mesh):
    layer = [P("segment", "dp")] * 12
    layer[2] = layer[4] = layer[8] = layer[10] = P("segment", "dp", None)
    both = P(AXES)
    rows = P(AXES, None)
    boundary = P("segment", None, "dp", None, None)
    weights = tuple(layer) + (rows, both, rows, both, rows)
    return jax.shard_map(
        functools.partial(per_device, mesh),
        mesh=mesh,
        in_specs=(boundary, P(None, "dp")) + weights,
        out_specs=(boundary, boundary) + weights,
        check_vma=False,
    )
```

```python
import functools
import math
from typing import Any, NamedTuple

import jax
import jax.numpy as jnp
from jax import lax
from jax.experimental import pallas as pl
from jax.experimental.pallas import tpu as pltpu
from jax.sharding import PartitionSpec as P

MESH = pl.DeviceIdType.MESH
HEADS = 12
EPSILON = 1e-05
GELU_SCALE = 0.7978845608028654
AXES = ("segment", "dp")


def half(value):
    return value.astype(jnp.bfloat16)


def wide(value):
    return value.astype(jnp.float32)


def mm(left, right):
    return jnp.dot(left, right, preferred_element_type=jnp.float32)


def mm_tn(left, right):
    return lax.dot_general(left, right, (((0,), (0,)), ((), ())), preferred_element_type=jnp.float32)


def mm_nt(left, right):
    return lax.dot_general(left, right, (((1,), (1,)), ((), ())), preferred_element_type=jnp.float32)


class Place:
    def __init__(self, nz):
        self.nz = nz
        self.x = lax.axis_index("segment")
        d = lax.axis_index("dp")
        self.c = d % 2
        self.y = (d // 2) % 2
        self.z = d // 4
        par = self.z % 2
        self.q = par * ((self.z + 1) // 2) + (1 - par) * ((nz - self.z // 2) % nz)
        self.places = [self.z_at((self.q + 2 * nz - back) % nz) for back in range(nz + 1)]

    def z_at(self, q):
        nz = self.nz
        upper = ((q + nz - 1) % nz) // (nz // 2)
        return (1 - upper) * (2 * q - 1) + upper * ((2 * (nz - q)) % (2 * nz))

    def ring_z(self, back):
        return self.places[back]

    def device(self, x=None, z=None, y=None, c=None):
        x = self.x if x is None else x
        z = self.z if z is None else z
        y = self.y if y is None else y
        c = self.c if c is None else c
        return (x, (z * 2 + y) * 2 + c)

    def other(self, axis):
        return self.device(**{axis: 1 - getattr(self, axis)})

    def succ(self):
        return self.device(z=self.z_at((self.q + 1) % self.nz))

    def pred(self):
        return self.device(z=self.ring_z(1))


def greet(place):
    barrier = pltpu.get_barrier_semaphore()
    peers = [place.other("x"), place.other("y"), place.other("c"), place.succ(), place.pred()]
    for peer in peers:
        pl.semaphore_signal(barrier, inc=1, device_id=peer, device_id_type=MESH)
    pl.semaphore_wait(barrier, len(peers))


def part_of(shape, part):
    rows, cols = shape
    if part is None:
        return (slice(0, rows), slice(0, cols))
    if rows % 32 == 0:
        return (slice(part * rows // 2, (part + 1) * rows // 2), slice(0, cols))
    return (slice(0, rows), slice(part * cols // 2, (part + 1) * cols // 2))


def part_shape(shape, part):
    return tuple(cut.stop - cut.start for cut in part_of(shape, part))


def block_of(ref, cut, c, z, x=None, y=None):
    xs = pl.ds(0, 2) if x is None else x
    ys = pl.ds(0, 2) if y is None else y
    return ref.at[(xs, z, ys, c) + cut]


def gather_kernel(plan, nz, small_at, count, *refs):
    which, parts, orders, starts = zip(*plan)
    n = max(which) + 1
    far, vectors, own, refs = refs[: n - 1], refs[n - 1 : n - 1 + count], refs[n - 1 + count], refs[n + count :]
    whole_outs, pair, raw, whole_ins, refs = refs[:n], refs[n], refs[n + 1 : 2 * n + 1], refs[2 * n + 1 : 3 * n + 1], refs[3 * n + 1 :]
    near, (held, send, recv, local, swap, loads) = refs[:count], refs[count:]
    cuts = [part_of(raw[k].shape, part) for k, part in zip(which, parts)]
    ins = [whole_ins[k].at[cut] for k, cut in zip(which, cuts)]
    outs = [whole_outs[k] for k in which]
    ready = set()
    place = Place(nz)
    moves = list(zip(vectors, near))
    moves += list(zip(far, [ref for k, ref in enumerate(raw) if k != small_at])) + [(own.at[place.x], held)]
    loading = [pltpu.make_async_copy(src, dst, loads.at[j]) for j, (src, dst) in enumerate(moves)]
    for copy in loading:
        copy.start()
    packing, loading = loading[:count], loading[count:]
    loading.insert(small_at, None)
    greet(place)
    stays = pltpu.make_async_copy(held, pair.at[place.x], swap.at[0])
    leaves = pltpu.make_async_remote_copy(
        src_ref=own.at[1 - place.x],
        dst_ref=pair.at[place.x],
        send_sem=swap.at[1],
        recv_sem=swap.at[2],
        device_id=place.other("x"),
        device_id_type=MESH,
    )
    started = []

    def put(i, k, src, dst, device):
        copy = pltpu.make_async_remote_copy(
            src_ref=src,
            dst_ref=dst,
            send_sem=send.at[i, k],
            recv_sem=recv.at[i, k],
            device_id=device,
            device_id_type=MESH,
        )
        copy.start()
        started.append(copy)
        return copy

    copies = [dict() for _ in orders]

    def stage(i, t):
        first, second, third = orders[i]
        out, mine = outs[i], copies[i]

        def shard(z, **at):
            return block_of(out, cuts[i], place.c, z, **at)

        def own(axis, z):
            return shard(z, **{axis: getattr(place, axis)})

        one = shard(place.z, x=place.x, y=place.y)
        if t == 0:
            k = which[i]
            if k not in ready:
                if k == small_at:
                    raw[k][...] = jnp.zeros_like(raw[k])
                    row = 0
                    for copy, vector in zip(packing, near):
                        copy.wait()
                        for r, lo, many in pieces_of(vector.shape[1], row):
                            raw[k][r : r + 1, :many] = vector[:, lo : lo + many]
                        row += rows_for(vector.shape[1])
                else:
                    loading[k].wait()
                whole_ins[k][...] = half(raw[k][...])
                ready.add(k)
            mine["own"] = pltpu.make_async_copy(ins[i], one, local.at[i])
            mine["own"].start()
        if second == "z":
            if t == 0:
                mine["p"] = put(i, 0, ins[i], one, place.other(first))
                return
            if t == 1:
                mine["own"].wait()
                mine["p"].wait_recv()
            elif t <= nz:
                mine["z", t - 1].wait_recv()
            if t <= nz:
                z = place.ring_z(t - 1)
                block = own(third, z)
                if t < nz:
                    mine["z", t] = put(i, t, block, block, place.succ())
                mine["l", t] = put(i, nz + t, block, block, place.other(third))
                mine["c", t] = put(i, 2 * nz + t, block, block, place.other("c"))
            if t >= 2:
                mine["l", t - 1].wait_recv()
                z = place.ring_z(t - 2)
                block = shard(z, **{third: 1 - getattr(place, third)})
                mine["d", t - 1] = put(i, 3 * nz + t - 1, block, block, place.other("c"))
        else:
            if t <= nz - 1:
                if t > 0:
                    mine["z", t].wait_recv()
                z = place.ring_z(t)
                src = ins[i] if t == 0 else shard(z, x=place.x, y=place.y)
                dst = shard(z, x=place.x, y=place.y)
                if t < nz - 1:
                    mine["z", t + 1] = put(i, t, src, dst, place.succ())
                mine["p", t + 1] = put(i, nz + t, src, dst, place.other(second))
            if 1 <= t <= nz:
                if t == 1:
                    mine["own"].wait()
                mine["p", t].wait_recv()
                block = own(third, place.ring_z(t - 1))
                mine["l", t] = put(i, 2 * nz + t, block, block, place.other(third))
                mine["c", t] = put(i, 3 * nz + t, block, block, place.other("c"))
            if t >= 2:
                mine["l", t - 1].wait_recv()
                block = shard(place.ring_z(t - 2), **{third: 1 - getattr(place, third)})
                mine["d", t - 1] = put(i, 4 * nz + t - 1, block, block, place.other("c"))

    stages = nz + 2
    for t in range(stages + max(starts)):
        for i in range(len(plan)):
            if 0 <= t - starts[i] < stages:
                stage(i, t - starts[i])
        if t == 0:
            leaves.start()
        if t == 1:
            loading[-1].wait()
            stays.start()
    for mine in copies:
        for key, copy in mine.items():
            if key[0] in "cd":
                copy.wait_recv()
    for copy in started:
        copy.wait_send()
    stays.wait()
    leaves.wait()


def gather_all(shards, plan, mesh, rows):
    nx, ndp = mesh.shape["segment"], mesh.shape["dp"]
    small_at = [isinstance(s, list) for s in shards].index(True)
    vectors = shards[small_at]
    if nx != 2 or ndp != 16:
        first = lax.axis_index("segment") == 0
        other = lax.ppermute(jnp.where(first, rows[1], rows[0]), "segment", [(0, 1), (1, 0)])
        pair = jnp.where(first, jnp.stack([rows[0], other]), jnp.stack([other, rows[1]]))
        packed = sixteens(jnp.concatenate([lanes(v) for v in vectors]))
        shards = [packed if j == small_at else s for j, s in enumerate(shards)]
        return [lax.all_gather(half(s), AXES, axis=0) for s in shards], pair
    nz, n, count = ndp // 4, len(shards), len(vectors)
    height = sum(rows_for(v.size) for v in vectors)
    shapes = [(height + -height % 16, 128) if j == small_at else s.shape for j, s in enumerate(shards)]
    far = [s for j, s in enumerate(shards) if j != small_at]
    slots = 5 * nz + 2
    *outs, pair = pl.pallas_call(
        functools.partial(gather_kernel, plan, nz, small_at, count),
        out_shape=[jax.ShapeDtypeStruct((2, nz, 2, 2) + s, jnp.bfloat16) for s in shapes]
        + [jax.ShapeDtypeStruct(rows.shape, rows.dtype)],
        in_specs=[pl.BlockSpec(memory_space=pl.ANY)] * (n + count),
        out_specs=[pl.BlockSpec(memory_space=pl.ANY)] * (n + 1),
        scratch_shapes=[pltpu.VMEM(s, jnp.float32) for s in shapes]
        + [pltpu.VMEM(s, jnp.bfloat16) for s in shapes]
        + [pltpu.VMEM(v.shape, v.dtype) for v in vectors]
        + [
            pltpu.VMEM(rows.shape[1:], rows.dtype),
            pltpu.SemaphoreType.DMA((len(plan), slots)),
            pltpu.SemaphoreType.DMA((len(plan), slots)),
            pltpu.SemaphoreType.DMA((len(plan),)),
            pltpu.SemaphoreType.DMA((3,)),
            pltpu.SemaphoreType.DMA((n + count,)),
        ],
        compiler_params=pltpu.CompilerParams(collective_id=0, has_side_effects=True, vmem_limit_bytes=62 * 2**20),
        name="gather_weights",
    )(*far, *vectors, rows)
    return [o.reshape((nx * ndp,) + s) for o, s in zip(outs, shapes)], pair


def add_to(dst, src):
    lead = dst.shape[:-2]

    def one(j, carry):
        at = (j // 2, j % 2) if len(lead) == 2 else (j,)[: len(lead)]
        at = at + (slice(None), slice(None))
        dst[at] = dst[at] + src[at]
        return carry

    if lead:
        lax.fori_loop(0, math.prod(lead), one, 0)
    else:
        dst[...] = dst[...] + src[...]


def sum_rounds(plan, place, nz, ins, outs, refs):
    which, parts, orders, starts, only = zip(*plan)
    cuts = [part_of(outs[k].shape, part) for k, part in zip(which, parts)]
    ins = [ins[k] for k in which]
    outs = [outs[k].at[cut] for k, cut in zip(which, cuts)]
    n = len(plan)
    accs, stages, firsts, rings, lasts = (refs[j * n : (j + 1) * n] for j in range(5))
    send, recv, local = refs[5 * n :]
    sent = []

    def put(do, i, k, src, dst, device):
        copy = pltpu.make_async_remote_copy(
            src_ref=src,
            dst_ref=dst,
            send_sem=send.at[i, k],
            recv_sem=recv.at[i, k],
            device_id=device,
            device_id_type=MESH,
        )
        do(copy.start)
        sent.append(copy.wait_send)
        return copy

    live = [dict() for _ in plan]

    def source(i, c, z):
        if only[i] is None:
            return block_of(ins[i], cuts[i], c, z)
        return ins[i].at[(z, pl.ds(0, 2), c) + cuts[i]]

    def load(do, i, k):
        copy = pltpu.make_async_copy(source(i, place.c, place.ring_z(k)), stages[i].at[k % 2], local.at[i, k % 2])
        do(copy.start)
        live[i]["o", k] = copy

    def stage(i, s, do):
        first, second, third = orders[i]
        acc, mine = accs[i], live[i]
        early, ring, late = firsts[i], rings[i], lasts[i]

        def part(k, **own):
            at = (own.get("y", pl.ds(0, 2)),)
            if only[i] is None:
                at = (own.get("x", pl.ds(0, 2)),) + at
            return acc.at[(k - 1,) + at]

        here = {axis: getattr(place, axis) for axis in "xy"}
        one = {first: here[first]}

        def there(axis, **own):
            own[axis] = 1 - here[axis]
            return own

        def step(dst, src):
            do(lambda: add_to(dst(), src()))

        def write(left, right):
            def out():
                outs[i][...] = wide(left()[...]) + wide(right()[...])

            do(out)

        if s == 0:
            for k in range(1, nz + 1):
                mine["c", k] = put(do, i, k, source(i, 1 - place.c, place.ring_z(k)), acc.at[k - 1], place.other("c"))
            load(do, i, 1)
            load(do, i, 2)
        if 1 <= s <= nz:
            k = s
            do(mine["c", k].wait_recv)
            do(mine["o", k].wait)
            step(lambda: acc.at[k - 1], lambda: stages[i].at[k % 2])
            if k + 2 <= nz:
                load(do, i, k + 2)
            mine["p", k] = put(do, i, nz + k, part(k, **there(first)), early.at[k - 1], place.other(first))
        if 2 <= s <= nz + 1:
            j = s - 1
            do(mine["p", j].wait_recv)
            step(lambda: part(j, **one), lambda: early.at[j - 1])
        if second == "z":
            if s == 2:
                mine["z", 1] = put(do, i, 2 * nz + 1, part(1, **one), ring.at[0], place.succ())
            if 3 <= s <= nz + 1:
                t = s - 2
                do(mine["z", t].wait_recv)
                step(lambda: ring.at[t - 1], lambda: part(t + 1, **one))
                if t < nz - 1:
                    mine["z", t + 1] = put(do, i, 2 * nz + t + 1, ring.at[t - 1], ring.at[t], place.succ())
                else:
                    src = ring.at[t - 1] if only[i] is not None else ring.at[t - 1, 1 - here[third]]
                    mine["l"] = put(do, i, 3 * nz + 1, src, late, place.other(third))
            if s == nz + 2:
                do(mine["l"].wait_recv)
                write(lambda: ring.at[nz - 2] if only[i] is not None else ring.at[nz - 2, here[third]], lambda: late)
        else:
            if 2 <= s <= nz + 1:
                j = s - 1
                src = part(j, **there(second, **one))
                mine["l", j] = put(do, i, 3 * nz + j, src, late.at[j - 1], place.other(second))
            if 3 <= s <= nz + 2:
                h = s - 2
                do(mine["l", h].wait_recv)
                step(lambda: part(h, **here), lambda: late.at[h - 1])
                if h == 1:
                    mine["z", 1] = put(do, i, 2 * nz + 1, part(1, **here), ring.at[0], place.succ())
                else:
                    t = h - 1
                    do(mine["z", t].wait_recv)
                    if t < nz - 1:
                        step(lambda: ring.at[t - 1], lambda: part(t + 1, **here))
                        mine["z", t + 1] = put(do, i, 2 * nz + t + 1, ring.at[t - 1], ring.at[t], place.succ())
                    else:
                        write(lambda: ring.at[t - 1], lambda: part(nz, **here))

    rounds = []
    for t in range(nz + 3 + max(starts)):
        rounds.append([])
        for i in range(n):
            if 0 <= t - starts[i] < nz + 3:
                stage(i, t - starts[i], rounds[-1].append)
    return rounds, sent


def sum_scratch(plan, grads, nz):
    def scratch(lead):
        return [
            pltpu.VMEM(lead(order, () if only is not None else (2,)) + part_shape(grads[k].shape[-2:], part), grads[k].dtype)
            for k, part, order, _, only in plan
        ]

    return (
        scratch(lambda o, x: (nz,) + x + (2,))
        + scratch(lambda o, x: (2,) + x + (2,))
        + scratch(lambda o, x: (nz,) + x)
        + scratch(lambda o, x: (nz - 1,) + x if o[1] == "z" else (nz - 1,))
        + scratch(lambda o, x: () if o[1] == "z" else (nz,))
        + [
            pltpu.SemaphoreType.DMA((len(plan), 4 * nz + 2)),
            pltpu.SemaphoreType.DMA((len(plan), 4 * nz + 2)),
            pltpu.SemaphoreType.DMA((len(plan), 2)),
        ]
    )


def by_chip(grads, plan, nz):
    only = dict((k, entry) for k, _, _, _, entry in plan)
    return [
        g.reshape(((2,) if only[k] is None else ()) + (nz, 2, 2) + g.shape[1:]) for k, g in enumerate(grads)
    ]


def scatter_kernel(plan, nz, *refs):
    n = max(entry[0] for entry in plan) + 1
    ins, here, refs = refs[:n], refs[n : n + 2], refs[n + 2 :]
    outs, there, refs, swap = refs[:n], refs[n], refs[n + 1 : -1], refs[-1]
    place = Place(nz)
    greet(place)
    rounds, sent = sum_rounds(plan, place, nz, ins, outs, refs)
    swaps = [
        pltpu.make_async_remote_copy(
            src_ref=ref,
            dst_ref=there,
            send_sem=swap.at[0],
            recv_sem=swap.at[1],
            device_id=place.other("x"),
            device_id_type=MESH,
        )
        for ref in here
    ]
    for t, acts in enumerate(rounds):
        for act in acts:
            act()
        if t == 0:
            pl.when(place.x == 0)(swaps[1].start)
            pl.when(place.x == 1)(swaps[0].start)
    for act in sent:
        act()
    swaps[0].wait()


def finish_kernel(count, chosen, *refs):
    n = len(chosen)
    ys, other_ys, gin0, gin1, other_gins, refs = refs[:5] + (refs[5:],)
    ins = []
    for two in chosen:
        ins.append(refs[: 1 + two])
        refs = refs[1 + two :]
    packed, outs, refs = refs[0], refs[1 : 3 + n], refs[3 + n :]
    vectors, held, (rows, sem) = refs[:count], refs[count:-2], refs[-2:]
    x = lax.axis_index("segment")
    moves = [((ys.at[x],), rows.at[0, 0], outs[0].at[x]), ((other_ys,), rows.at[0, 1], outs[0].at[1 - x])]
    moves += [((gin0, gin1), rows.at[1, 0], outs[1].at[x]), ((other_gins,), rows.at[1, 1], outs[1].at[1 - x])]
    moves += list(zip(ins, held, outs[2:]))
    steps = []
    for j, (sources, via, dst) in enumerate(moves):
        loads = [pltpu.make_async_copy(src, via, sem.at[j, 0]) for src in sources]
        if len(loads) == 1:
            loads[0].start()
        else:
            pl.when(x == 0)(loads[0].start)
            pl.when(x == 1)(loads[1].start)
        steps.append((loads[0], pltpu.make_async_copy(via, dst, sem.at[j, 1])))
    row = 0
    for dst in vectors:
        for r, lo, many in pieces_of(dst.shape[1], row):
            dst[:, lo : lo + many] = packed[r : r + 1, :many]
        row += rows_for(dst.shape[1])
    for load, store in steps:
        load.wait()
        store.start()
    for load, store in steps:
        store.wait()


def finish(ys, other_ys, gins, other_gins, arrays, packed, sizes):
    chosen = [isinstance(a, tuple) for a in arrays]
    flat = [part for a in arrays for part in (a if isinstance(a, tuple) else (a,))]
    first = [a[0] if isinstance(a, tuple) else a for a in arrays]
    like = [jax.ShapeDtypeStruct(a.shape, a.dtype) for a in [ys, ys] + first]
    vectors = [jax.ShapeDtypeStruct((1, size), jnp.float32) for size in sizes]
    far, near = pl.BlockSpec(memory_space=pl.ANY), pl.BlockSpec(memory_space=pltpu.VMEM)
    got = pl.pallas_call(
        functools.partial(finish_kernel, len(sizes), chosen),
        out_shape=like + vectors,
        in_specs=[far] * (5 + len(flat)) + [near],
        out_specs=[far] * len(like) + [near] * len(sizes),
        scratch_shapes=[pltpu.VMEM(a.shape, a.dtype) for a in first]
        + [pltpu.VMEM((2,) + ys.shape, ys.dtype), pltpu.SemaphoreType.DMA((4 + len(arrays), 2))],
        compiler_params=pltpu.CompilerParams(vmem_limit_bytes=62 * 2**20),
        name="finish",
    )(ys, other_ys, *gins, other_gins, *flat, packed)
    return got[: len(like)], got[len(like) :]


def from_other(first_rows, second_rows):
    payload = jnp.where(lax.axis_index("segment") == 0, second_rows, first_rows)
    return lax.ppermute(payload, "segment", [(0, 1), (1, 0)])


def plain_sums(grads, plan):
    only = dict((k, entry) for k, _, _, _, entry in plan)
    got = []
    for k, g in enumerate(grads):
        if only[k] is None:
            got.append(wide(lax.psum_scatter(g, AXES, scatter_dimension=0, tiled=False)))
        else:
            got.append(wide(lax.psum_scatter(lax.psum(g, "segment"), "dp", scatter_dimension=0, tiled=False)))
    return got


def scatter_all(grads, plan, mesh, rows):
    nx, ndp = mesh.shape["segment"], mesh.shape["dp"]
    if nx != 2 or ndp != 16:
        return plain_sums(grads, plan), from_other(*rows)
    nz, n = ndp // 4, len(grads)
    far, near = pl.BlockSpec(memory_space=pl.ANY), pl.BlockSpec(memory_space=pltpu.VMEM)
    got = pl.pallas_call(
        functools.partial(scatter_kernel, plan, nz),
        out_shape=[jax.ShapeDtypeStruct(g.shape[1:], jnp.float32) for g in grads]
        + [jax.ShapeDtypeStruct(rows[0].shape, rows[0].dtype)],
        in_specs=[far] * (n + 2),
        out_specs=[near] * n + [far],
        scratch_shapes=sum_scratch(plan, grads, nz) + [pltpu.SemaphoreType.DMA((2,))],
        compiler_params=pltpu.CompilerParams(
            collective_id=1, has_side_effects=True, vmem_limit_bytes=62 * 2**20
        ),
        name="sum_gradients",
    )(*by_chip(grads, plan, nz), *rows)
    return got[:n], got[n]


ROWS = 512
HIDDEN = 768
GAIN1, BIAS1, VALUE_B, OUT_B, GAIN2, BIAS2, OUTER_B, FIRST_B = range(8)
VECTOR_ROWS = 7


def rows_for(size):
    return -(-size // 128)


def pieces_of(size, row):
    return [(row + j, j * 128, min(128, size - j * 128)) for j in range(rows_for(size))]


def unpack_rows(small, at, ndp, row, ref):
    size = ref.shape[1] // ndp
    for d in range(ndp):
        for r, lo, n in pieces_of(size, row):
            ref[:, d * size + lo : d * size + lo + n] = wide(small[at + d])[r : r + 1, :n]


def unpack_vectors(small, at, ndp, ref):
    size = ref.shape[1] // ndp
    for d in range(ndp):
        ref[:, d * size : (d + 1) * size] = wide(small[at + d])[: ref.shape[0], :size]


def pack_rows(ref, ndp, row, small, at):
    size = ref.shape[1] // ndp
    for d in range(ndp):
        for r, lo, n in pieces_of(size, row):
            small[at + d, r : r + 1, :n] = ref[:, d * size + lo : d * size + lo + n]


def pack_vectors(ref, ndp, small, at):
    size = ref.shape[1] // ndp
    for d in range(ndp):
        small[at + d, :VECTOR_ROWS, :size] = ref[:VECTOR_ROWS, d * size : (d + 1) * size]


def chunks(rows, size=ROWS):
    return [slice(at, at + size) for at in range(0, rows, size)]


def norm_parts(rows):
    centre = rows - jnp.mean(rows, axis=-1, keepdims=True)
    inv = lax.rsqrt(jnp.mean(centre * centre, axis=-1, keepdims=True) + EPSILON)
    return centre * inv, inv


def row_loop(rows, body, init):
    return lax.fori_loop(0, rows // 128, lambda j, c: body(pl.ds(pl.multiple_of(j * 128, 128), 128), c), init)


def norm_into(read, write, gain, shift, rows):
    def body(r, carry):
        write[r, :] = half(norm_parts(read(r))[0] * gain + shift)
        return carry

    row_loop(rows, body, 0)


def norm_back(read, grad, gain, rows, done):
    def body(r, carry):
        normal, inv = norm_parts(read(r))
        m_hat = grad(r)
        m = m_hat * gain
        part = inv * (
            m - jnp.mean(m, axis=-1, keepdims=True) - normal * jnp.mean(m * normal, axis=-1, keepdims=True)
        )
        done(r, part)
        return carry[0] + sums(m_hat * normal), carry[1] + sums(m_hat)

    zero = jnp.zeros_like(gain)
    return row_loop(rows, body, (zero, zero))


def sums(value):
    return jnp.sum(wide(value), axis=0, keepdims=True)


def gelu_both(t):
    square = t * t
    s = 0.5 + 0.5 * jnp.tanh(t * (GELU_SCALE + GELU_SCALE * 0.044715 * square))
    value = t * s
    slope = s + value * (1.0 - s) * (2 * GELU_SCALE + 6 * GELU_SCALE * 0.044715 * square)
    return value, slope


def masked_pair(head):
    return lax.broadcasted_iota(jnp.int32, (1, 2 * head), 1) < head


def add_up(fresh, ref, at, value):
    @pl.when(fresh)
    def _():
        ref[at] = value

    @pl.when(jnp.logical_not(fresh))
    def _():
        ref[at] += value


def forward_start(read, vec, value_ref, a_ref, v_ref, first=None):
    rows = a_ref.shape[0]
    norm_into(read, a_ref, vec(GAIN1), vec(BIAS1), rows)
    for r in chunks(rows):
        v_ref[r] = half(mm(a_ref[r], value_ref[...]) + vec(VALUE_B))
        if first is not None:
            first_ref, first_b, p_ref, slope_ref = first
            value, slope = gelu_both(mm(a_ref[r], first_ref[...]) + first_b[...])
            p_ref[r] = half(value)
            slope_ref[r] = half(slope)


def both_heads(pair, head):
    lower = masked_pair(head)
    zero = jnp.zeros_like(pair)
    return jnp.concatenate([jnp.where(lower, pair, zero), jnp.where(lower, zero, pair)], axis=0)


def forward_heads(pair, length, v_ref, c_ref, probs_ref, logits_of, bounded=False):
    rows, width = v_ref.shape
    slots = probs_ref.shape[1] // 2
    head = width // HEADS
    at = pl.ds(pl.multiple_of(pair * 2 * head, 2 * head), 2 * head)
    shut = jnp.where(lax.broadcasted_iota(jnp.int32, (1, slots), 1) >= length, -1e30, 0.0)
    both = logits_of(shut)
    for h in range(2):
        logits = both[h]
        expo = jnp.exp(logits if bounded else logits - jnp.max(logits, axis=1, keepdims=True))
        probs_ref[:, h * slots : (h + 1) * slots] = half(expo * (1.0 / jnp.sum(expo, axis=1, keepdims=True)))
    c_ref[:, at] = half(mm(probs_ref[...], both_heads(v_ref[:, at], head)))


def forward_middle(read, vec, out_ref, c_ref, hid_ref, b_ref):
    rows = c_ref.shape[0]
    for r in chunks(rows):
        hid_ref[r] = read(r) + mm(c_ref[r], out_ref[...]) + vec(OUT_B)
    norm_into(lambda r: hid_ref[r, :], b_ref, vec(GAIN2), vec(BIAS2), rows)


def forward_hidden(fresh, b_ref, inner_ref, inner_b, outer_ref, q_ref, slope_ref, acc):
    for r in chunks(b_ref.shape[0]):
        value, slope = gelu_both(mm(b_ref[r], inner_ref[...]) + inner_b)
        q = half(value)
        q_ref[r] = q
        slope_ref[r] = half(slope)
        add_up(fresh, acc, r, mm(q, outer_ref[...]))


def forward_end(vec, hid_ref, acc, y_ref):
    for r in chunks(acc.shape[0]):
        y_ref[r] = half(hid_ref[r] + acc[r] + vec(OUTER_B))


def backward_hidden(fresh, g_ref, b_ref, q_ref, slope_ref, inner_ref, outer_ref, gz_ref, acc, g_outer, g_inner, g_inner_b):
    for r in chunks(g_ref.shape[0]):
        gz = half(mm_nt(g_ref[r], outer_ref[...]) * wide(slope_ref[r]))
        gz_ref[r] = gz
        add_up(fresh, acc, r, mm_nt(gz, inner_ref[...]))
    gz = gz_ref[...]
    g_outer[...] = half(mm_tn(q_ref[...], g_ref[...]))
    g_inner[...] = half(mm_tn(b_ref[...], gz))
    g_inner_b[...] = sums(gz)


def backward_middle(vec, put, g_ref, hid_ref, c_ref, out_ref, acc, ghid, gatt, gc_ref, g_out):
    rows = g_ref.shape[0]

    def done(r, part):
        total = wide(g_ref[r, :]) + part
        ghid[r, :] = total
        gatt[r, :] = half(total)

    gain, shift = norm_back(lambda r: hid_ref[r, :], lambda r: acc[r, :], vec(GAIN2), rows, done)
    put(GAIN2, gain)
    put(BIAS2, shift)
    put(OUTER_B, sums(g_ref[...]))
    put(OUT_B, sums(gatt[...]))
    g_out[...] = half(mm_tn(c_ref[...], gatt[...]))
    for r in chunks(rows):
        gc_ref[r] = half(mm_nt(gatt[r], out_ref[...]))


def backward_heads(pair, v_ref, c_ref, gc_ref, gv_ref, probs_ref, db):
    rows, width = v_ref.shape
    slots = probs_ref.shape[1] // 2
    head = width // HEADS
    at = pl.ds(pl.multiple_of(pair * 2 * head, 2 * head), 2 * head)
    both = mm_nt(gc_ref[:, at], both_heads(v_ref[:, at], head))
    along = wide(gc_ref[:, at]) * wide(c_ref[:, at])
    lower = masked_pair(head)
    for h in range(2):
        cols = slice(h * slots, (h + 1) * slots)
        mean = jnp.sum(jnp.where(lower if h == 0 else jnp.logical_not(lower), along, 0.0), axis=1, keepdims=True)
        db[:, cols] = half(wide(probs_ref[:, cols]) * (both[:, cols] - mean))
    values = mm_tn(probs_ref[...], gc_ref[:, at])
    gv_ref[:, at] = half(jnp.where(masked_pair(head), values[:slots], values[slots:]))


def backward_end(vec, put, read, gv_ref, value_ref, a_ref, acc, ghid, g_value, gx_ref, first=None):
    rows = gv_ref.shape[0]
    put(VALUE_B, sums(gv_ref[...]))
    g_value[...] = half(mm_tn(a_ref[...], gv_ref[...]))
    if first is not None:
        first_ref, slope_ref, gf_ref, g_first = first
        for r in chunks(rows):
            gf_ref[r] = half(acc[r] * wide(slope_ref[r]))
        put(FIRST_B, sums(gf_ref[...]))
        g_first[...] = half(mm_tn(a_ref[...], gf_ref[...]))
    else:
        put(FIRST_B, jnp.zeros((1, acc.shape[1]), jnp.float32))
    for r in chunks(rows):
        ga = mm_nt(gv_ref[r], value_ref[...])
        if first is not None:
            ga = ga + mm_nt(gf_ref[r], first_ref[...])
        acc[r] = ga

    def done(r, part):
        gx_ref[r, :] = half(ghid[r, :] + part)

    gain, shift = norm_back(read, lambda r: acc[r, :], vec(GAIN1), rows, done)
    put(GAIN1, gain)
    put(BIAS1, shift)


def forward_kernel(pairs, parts, length_ref, x_ref, small, value_ref, out_ref, first_ref, second_ref, inner_ref, outer_ref, y_ref, *refs):
    kept, probs_ref, q_ref, slope_ref = refs[:7], refs[7], refs[8], refs[9]
    a_ref, v_ref, p_ref, first_slope, c_ref, b_ref, hid_ref, acc, vectors, inner_b, first_b, second_b, sem = refs[10:]
    held = (a_ref, v_ref, p_ref, first_slope, c_ref, b_ref, hid_ref)
    copies = [pltpu.make_async_copy(src, dst, sem.at[j]) for j, (src, dst) in enumerate(zip(held, kept))]
    i = pl.program_id(0)
    slots = probs_ref.shape[2] // 2
    ndp, part = small.shape[0] // 2, q_ref.shape[1]

    def vec(k):
        return vectors[k : k + 1, :]

    x_ref, y_ref = x_ref.at[0], y_ref.at[0]

    def read(r):
        return wide(x_ref[r, :])

    @pl.when(i == 0)
    def _():
        unpack_vectors(small, 0, ndp, vectors)
        unpack_rows(small, 0, ndp, VECTOR_ROWS, inner_b)
        row = VECTOR_ROWS + rows_for(inner_b.shape[1] // ndp)
        unpack_rows(small, 0, 2 * ndp, row, first_b)
        unpack_rows(small, 0, 2 * ndp, row + rows_for(first_b.shape[1] // (2 * ndp)), second_b)
        forward_start(read, vec, value_ref.at[0], a_ref, v_ref, (first_ref, first_b, p_ref, first_slope))
        for copy in copies[:4]:
            copy.start()

    @pl.when(i < pairs)
    def _():
        def logits_of(shut):
            bias = second_b[:, pl.ds(pl.multiple_of(i * 2 * slots, 2 * slots), 2 * slots)]
            logits = mm(p_ref[...], second_ref[...]) + (bias + jnp.concatenate([shut, shut], axis=1))
            return logits[:, :slots], logits[:, slots:]

        forward_heads(i, length_ref[0], v_ref, c_ref, probs_ref.at[0], logits_of)

    @pl.when(i == pairs - 1)
    def _():
        forward_middle(read, vec, out_ref.at[0], c_ref, hid_ref, b_ref)
        for copy in copies[4:]:
            copy.start()

    @pl.when(i >= pairs)
    def _():
        bias = inner_b[:, pl.ds(pl.multiple_of((i - pairs) * part, part), part)]
        forward_hidden(i == pairs, b_ref, inner_ref.at[0], bias, outer_ref.at[0], q_ref, slope_ref, acc)

    @pl.when(i == pairs + parts - 1)
    def _():
        forward_end(vec, hid_ref, acc, y_ref)
        for copy in copies:
            copy.wait()


def backward_kernel(pairs, parts, host, g_ref, b_ref, small, g_small1, q_ref, slope_ref, probs_ref, inner_ref, outer_ref, second_ref, *refs):
    far, refs = refs[:10], refs[13:]
    n = max(entry[0] for entry in host[0]) + 1 if host else 0
    sum_ins, refs = refs[:n], refs[n:]
    gx_ref, g_outer, g_inner, g_out, g_value, g_small, g_first, g_second = refs[:8]
    sum_outs, refs = refs[8 : 8 + n], refs[8 + n :]
    near, refs = refs[:10], refs[10:]
    acc, ghid, gatt, gc_ref, gv_ref, db, gz_ref, vectors, g_vec, g_inner_b, g_second_b, sem, *refs = refs
    far = [ref.at[0] if len(ref.shape) == 3 else ref for ref in far]
    copies = [pltpu.make_async_copy(src, dst, sem.at[j]) for j, (src, dst) in enumerate(zip(far, near))]
    hid_ref, c_ref, out_ref, v_ref, p_ref, a_ref, value_ref, first_ref, first_slope, x_ref = near
    i = pl.program_id(0)
    rounds, sent = [], []
    if host:
        place = Place(host[1])
        pl.when(i == 0)(lambda: greet(place))
        rounds, sent = sum_rounds(host[0], place, host[1], sum_ins, sum_outs, refs)
    slots = probs_ref.shape[2] // 2
    ndp, part = small.shape[0] // 2, q_ref.shape[1]

    def vec(k):
        return vectors[k : k + 1, :]

    def put(k, value):
        g_vec[k : k + 1, :] = value

    @pl.when(i == 0)
    def _():
        for copy in copies:
            copy.start()
        unpack_vectors(small, 0, ndp, vectors)

    for at, acts in zip(BESIDE, rounds):

        @pl.when(i == at)
        def _(acts=acts):
            for act in acts:
                act()

    @pl.when(i < parts)
    def _():
        bias = g_inner_b.at[:, pl.ds(pl.multiple_of(i * part, part), part)]
        backward_hidden(i == 0, g_ref, b_ref, q_ref, slope_ref, inner_ref.at[0], outer_ref.at[0], gz_ref, acc, g_outer, g_inner.at[0], bias)

    @pl.when(i == parts - 1)
    def _():
        for copy in copies[:3]:
            copy.wait()
        backward_middle(vec, put, g_ref, hid_ref, c_ref, out_ref, acc, ghid, gatt, gc_ref, g_out.at[0])
        for copy in copies[3:5]:
            copy.wait()

    @pl.when(i >= parts)
    def _():
        backward_heads(i - parts, v_ref, c_ref, gc_ref, gv_ref, probs_ref.at[0], db)
        g_second[...] = half(mm_tn(p_ref[...], db[...]))
        g_second_b[:, pl.ds(pl.multiple_of((i - parts) * 2 * slots, 2 * slots), 2 * slots)] = sums(db[...])
        add_up(i == parts, acc, slice(None), mm_nt(db[...], second_ref[...]))

    @pl.when(i == pairs + parts - 1)
    def _():
        for copy in copies[5:]:
            copy.wait()
        backward_end(
            vec, put, lambda r: wide(x_ref[r, :]), gv_ref, value_ref, a_ref, acc, ghid, g_value.at[0], gx_ref,
            (first_ref, first_slope, gatt, g_first),
        )
        g_small[:ndp] = jnp.zeros_like(g_small1)
        g_small[ndp:] = g_small1[...]
        pack_vectors(g_vec, ndp, g_small, 0)
        pack_rows(g_inner_b, ndp, VECTOR_ROWS, g_small, 0)
        row = VECTOR_ROWS + rows_for(g_inner_b.shape[1] // ndp)
        pack_rows(g_vec.at[FIRST_B : FIRST_B + 1, :], 2 * ndp, row, g_small, 0)
        row += rows_for(g_vec.shape[1] // (2 * ndp))
        pack_rows(g_second_b, 2 * ndp, row, g_small, 0)
        for acts in rounds[len(BESIDE) :] + [sent]:
            for act in acts:
                act()


def both_kernel(pairs, parts, length_ref, x_ref, g_ref, small, value_ref, out_ref, table_ref, inner_ref, outer_ref, *refs):
    y_ref, gx_ref, g_outer, g_inner, g_out, g_value, g_small, g_table = refs[:8]
    acc, hid_ref, ghid, a_ref, v_ref, c_ref, b_ref, gatt, gc_ref, gv_ref, probs_ref, q_ref, slope_ref, db, gz_ref, *refs = refs[8:]
    vectors, inner_b, g_vec, g_inner_b = refs
    i = pl.program_id(0)
    slots = probs_ref.shape[2] // 2
    j = i - pairs
    k = j - parts
    n = k - parts

    ndp, part = small.shape[0] // 2, q_ref.shape[2]

    def vec(k):
        return vectors[k : k + 1, :]

    def put(k, value):
        g_vec[k : k + 1, :] = value

    def hidden(ref, k):
        return ref.at[:, pl.ds(pl.multiple_of(k * part, part), part)]

    x_ref, g_ref, y_ref = (ref.at[0] for ref in (x_ref, g_ref, y_ref))

    def read(r):
        return wide(x_ref[r, :])

    @pl.when(i == 0)
    def _():
        unpack_vectors(small, ndp, ndp, vectors)
        unpack_rows(small, ndp, ndp, VECTOR_ROWS, inner_b)
        forward_start(read, vec, value_ref.at[0], a_ref, v_ref)

    @pl.when(i < pairs)
    def _():
        def logits_of(shut):
            return wide(table_ref[:slots, :]) + shut, wide(table_ref[slots:, :]) + shut

        forward_heads(i, length_ref[0], v_ref, c_ref, probs_ref.at[i], logits_of, True)

    @pl.when(i == pairs - 1)
    def _():
        forward_middle(read, vec, out_ref.at[0], c_ref, hid_ref, b_ref)

    @pl.when((j >= 0) & (j < parts))
    def _():
        forward_hidden(j == 0, b_ref, inner_ref.at[0], hidden(inner_b, j)[...], outer_ref.at[0], q_ref.at[j], slope_ref.at[j], acc)

    @pl.when(j == parts - 1)
    def _():
        forward_end(vec, hid_ref, acc, y_ref)

    @pl.when((k >= 0) & (k < parts))
    def _():
        at = parts - 1 - k
        backward_hidden(k == 0, g_ref, b_ref, q_ref.at[at], slope_ref.at[at], inner_ref.at[0], outer_ref.at[0], gz_ref, acc, g_outer, g_inner.at[0], hidden(g_inner_b, at))

    @pl.when(k == parts - 1)
    def _():
        backward_middle(vec, put, g_ref, hid_ref, c_ref, out_ref.at[0], acc, ghid, gatt, gc_ref, g_out.at[0])

    @pl.when(n >= 0)
    def _():
        backward_heads(n, v_ref, c_ref, gc_ref, gv_ref, probs_ref.at[n], db)
        g_table[:slots, :] = db[:, :slots]
        g_table[slots:, :] = db[:, slots:]

    @pl.when(n == pairs - 1)
    def _():
        backward_end(vec, put, read, gv_ref, value_ref.at[0], a_ref, acc, ghid, g_value.at[0], gx_ref)
        g_small[...] = jnp.zeros_like(g_small)
        pack_vectors(g_vec, ndp, g_small, 0)
        pack_rows(g_inner_b, ndp, VECTOR_ROWS, g_small, 0)


class Weights(NamedTuple):
    small: Any
    value: Any
    out: Any
    inner: Any
    outer: Any
    first: Any
    second: Any
    table: Any


def whole(shape, *at):
    at = tuple(at)
    block = (1,) * len(at) + tuple(shape[len(at) :])
    return pl.BlockSpec(block, lambda i: at + (0,) * (len(shape) - len(at)), pipeline_mode=pl.Buffered(1))


def whole_out(shape, *at):
    at = tuple(at)
    block = (1,) * len(at) + tuple(shape[len(at) :])
    return pl.BlockSpec(block, lambda i: at + (0,) * (len(shape) - len(at)))


def like(shape, dtype=jnp.bfloat16):
    return jax.ShapeDtypeStruct(shape, dtype)


FAR = pl.BlockSpec(memory_space=pl.ANY)


def sizes_of(x, w):
    rows, width = x.shape[-2:]
    parts = w.inner.shape[2] // HIDDEN
    return rows, width, HEADS // 2, parts, w.inner.shape[2] // parts


def forward(x, length, w):
    rows, width, pairs, parts, part = sizes_of(x, w)
    slots = rows

    def pair(i):
        return jnp.minimum(i, pairs - 1)

    def piece(i):
        return jnp.maximum(i - pairs, 0)

    ins = [length, x, w.small, w.value, w.out, w.first, w.second, w.inner, w.outer]
    specs = [
        pl.BlockSpec(memory_space=pltpu.SMEM),
        whole(x.shape, 0),
        whole(w.small.shape),
        whole(w.value.shape, 0),
        whole(w.out.shape, 0),
        whole(w.first.shape),
        pl.BlockSpec((width, 2 * slots), lambda i: (0, pair(i))),
        pl.BlockSpec((1, width, part), lambda i: (0, 0, piece(i))),
        pl.BlockSpec((1, part, width), lambda i: (0, piece(i), 0)),
    ]
    half_rows = like((rows, width))
    kept = [half_rows] * 6 + [like((rows, width), jnp.float32)]
    hidden_block = pl.BlockSpec((rows, part), lambda i: (0, piece(i)))
    y, *saved = pl.pallas_call(
        functools.partial(forward_kernel, pairs, parts),
        grid=(pairs + parts,),
        out_shape=[like(x.shape)] + kept + [like((pairs, rows, 2 * slots))] + [like((rows, part * parts))] * 2,
        in_specs=specs,
        out_specs=[whole_out(x.shape, 0)]
        + [FAR] * 7
        + [pl.BlockSpec((1, rows, 2 * slots), lambda i: (pair(i), 0, 0))]
        + [hidden_block] * 2,
        scratch_shapes=[pltpu.VMEM(k.shape, k.dtype) for k in kept]
        + [
            pltpu.VMEM((rows, width), jnp.float32),
            pltpu.VMEM((8, width), jnp.float32),
            pltpu.VMEM((1, part * parts), jnp.float32),
            pltpu.VMEM((1, width), jnp.float32),
            pltpu.VMEM((1, w.second.shape[1]), jnp.float32),
            pltpu.SemaphoreType.DMA((7,)),
        ],
        compiler_params=pltpu.CompilerParams(vmem_limit_bytes=62 * 2**20),
        name="forward_0",
    )(*ins)
    return y, saved


def backward(g, x, saved, w, before, small1, host=None, early=()):
    rows, width, pairs, parts, part = sizes_of(x, w)
    slots = rows
    a, v, p, first_slope, c, b, hid, probs, q, slope = saved

    def pair(i):
        return jnp.maximum(i - parts, 0)

    def piece(i):
        return jnp.minimum(i, parts - 1)

    hidden_block = pl.BlockSpec((rows, part), lambda i: (0, piece(i)))
    inner_block = pl.BlockSpec((1, width, part), lambda i: (0, 0, piece(i)))
    outer_block = pl.BlockSpec((1, part, width), lambda i: (0, piece(i), 0))
    second_block = pl.BlockSpec((width, 2 * slots), lambda i: (0, pair(i)))
    far = [hid, c, w.out, v, p, a, w.value, w.first, first_slope, x]
    ins = [g, b, w.small, small1, q, slope, probs, w.inner, w.outer, w.second] + far
    specs = [whole((rows, width))] * 2 + [whole(w.small.shape), whole(small1.shape)] + [hidden_block] * 2
    specs += [pl.BlockSpec((1, rows, 2 * slots), lambda i: (pair(i), 0, 0)), inner_block, outer_block, second_block]
    specs += [FAR] * 10
    aliases = {len(ins) + j: 2 + j for j in range(3)}
    ins += list(before) + list(early)
    specs += [FAR] * (3 + len(early))
    outs = [like((rows, width)), like(w.outer.shape[1:])] + [like(k.shape, k.dtype) for k in before]
    out_specs = [whole_out((rows, width)), pl.BlockSpec((part, width), lambda i: (piece(i), 0)), inner_block]
    out_specs += [whole_out(w.out.shape, 0), whole_out(w.value.shape, 0)]
    outs += [like(w.small.shape, jnp.float32), like(w.first.shape), like(w.second.shape)]
    out_specs += [whole_out(w.small.shape), whole_out(w.first.shape), second_block]
    sums_of = [like(e.shape[-2:], jnp.float32) for e in early]
    gx, *grads = pl.pallas_call(
        functools.partial(backward_kernel, pairs, parts, host),
        grid=(pairs + parts,),
        out_shape=outs + sums_of,
        in_specs=specs,
        out_specs=out_specs + [whole_out(e.shape) for e in sums_of],
        scratch_shapes=[pltpu.VMEM(k.shape[-2:], k.dtype) for k in far]
        + [pltpu.VMEM((rows, width), jnp.float32)] * 2
        + [pltpu.VMEM((rows, width), jnp.bfloat16)] * 3
        + [pltpu.VMEM((rows, 2 * slots), jnp.bfloat16), pltpu.VMEM((rows, part), jnp.bfloat16)]
        + [pltpu.VMEM((8, width), jnp.float32)] * 2
        + [pltpu.VMEM((1, part * parts), jnp.float32), pltpu.VMEM((1, w.second.shape[1]), jnp.float32)]
        + [pltpu.SemaphoreType.DMA((10,))]
        + (sum_scratch(host[0], early, host[1]) if host else []),
        input_output_aliases=aliases,
        compiler_params=pltpu.CompilerParams(
            vmem_limit_bytes=63 * 2**20, **(dict(collective_id=2, has_side_effects=True) if host else {})
        ),
        name="backward_0",
    )(*ins)
    return gx, grads[:7], grads[7:]


def both_ways(x, g, length, w):
    rows, width, pairs, parts, part = sizes_of(x, w)
    slots = rows

    def there(i):
        return jnp.minimum(i, pairs - 1)

    def back(i):
        return jnp.maximum(i - pairs - 2 * parts, 0)

    def piece(i):
        j = jnp.clip(i - pairs, 0, 2 * parts - 1)
        return jnp.minimum(j, 2 * parts - 1 - j)

    def late(i):
        return parts - 1 - jnp.clip(i - pairs - parts, 0, parts - 1)

    ins = [length, x, g, w.small, w.value, w.out, w.table, w.inner, w.outer]
    specs = [pl.BlockSpec(memory_space=pltpu.SMEM), whole(x.shape, 0), whole(g.shape, 1)]
    specs += [whole(w.small.shape), whole(w.value.shape, 1), whole(w.out.shape, 1)]
    specs += [
        pl.BlockSpec((2 * slots, slots), lambda i: (there(i), 0)),
        pl.BlockSpec((1, width, part), lambda i: (1, 0, piece(i))),
        pl.BlockSpec((1, part, width), lambda i: (1, piece(i), 0)),
    ]
    grads = [like(w.outer.shape[1:]), like(w.inner.shape), like(w.out.shape), like(w.value.shape)]
    small = (w.small.shape[0] // 2,) + w.small.shape[1:]
    grads += [like(small, jnp.float32), like(w.table.shape)]
    grad_specs = [
        pl.BlockSpec((part, width), lambda i: (late(i), 0)),
        pl.BlockSpec((1, width, part), lambda i: (1, 0, late(i))),
        whole_out(w.out.shape, 1),
        whole_out(w.value.shape, 1),
        whole_out(small),
        pl.BlockSpec((2 * slots, slots), lambda i: (back(i), 0)),
    ]
    y, gx, *grads = pl.pallas_call(
        functools.partial(both_kernel, pairs, parts),
        grid=(2 * pairs + 2 * parts,),
        out_shape=[like(x.shape), like((rows, width))] + grads,
        in_specs=specs,
        out_specs=[whole_out(x.shape, 1), whole_out((rows, width))] + grad_specs,
        scratch_shapes=[pltpu.VMEM((rows, width), jnp.float32)] * 3
        + [pltpu.VMEM((rows, width), jnp.bfloat16)] * 7
        + [pltpu.VMEM((pairs, rows, 2 * slots), jnp.bfloat16)]
        + [pltpu.VMEM((parts, rows, part), jnp.bfloat16)] * 2
        + [pltpu.VMEM((rows, 2 * slots), jnp.bfloat16), pltpu.VMEM((rows, part), jnp.bfloat16)]
        + [pltpu.VMEM((8, width), jnp.float32), pltpu.VMEM((1, part * parts), jnp.float32)] * 2,
        input_output_aliases={1: 0},
        compiler_params=pltpu.CompilerParams(vmem_limit_bytes=62 * 2**20),
        name="forward_backward_1",
    )(*ins)
    return y, gx, grads


ROW_VECTORS = (0, 1, 3, 5, 6, 7, 11)
VECTORS = ROW_VECTORS + (9, 13, 15)
MATRICES = (2, 4, 8, 10, 12, 14, 16)
SMALL = 17
GATHER = (
    (8, 0, "xzy", 2),
    (SMALL, None, "xzy", 3),
    (10, 1, "zyx", 1),
    (2, None, "zyx", 0),
    (16, 0, "zxy", 1),
    (10, 0, "yzx", 2),
    (12, None, "zyx", 0),
    (16, 1, "xzy", 0),
    (8, 1, "yzx", 2),
    (4, None, "zyx", 0),
    (14, 0, "xzy", 2),
    (14, 1, "xzy", 0),
)
EARLY = ((10, 1, "yzx", 1, 1), (10, 0, "yzx", 0, 1), (16, 1, "yxz", 1, None), (16, 0, "xzy", 1, None))
BESIDE = (0, 0, 1, 3, 4, 7, 9)
SUM = (
    (8, 1, "yzx", 4, None),
    (14, 1, "yxz", 5, None),
    (10, 1, "yzx", 2, 0),
    (12, None, "xzy", 2, None),
    (8, 0, "xyz", 3, None),
    (4, None, "yzx", 0, None),
    (10, 0, "yzx", 2, 0),
    (2, None, "xzy", 2, None),
    (SMALL, None, "xyz", 5, None),
    (14, 0, "xzy", 4, None),
)


def numbered(plan):
    names = list(dict.fromkeys(entry[0] for entry in plan))
    return names, [(names.index(entry[0]),) + entry[1:] for entry in plan]


def planned(call, plan, arrays, mesh, rows):
    names, plan = numbered(plan)
    got, rows = call([arrays[k] for k in names], plan, mesh, rows)
    return dict(zip(names, got)), rows


def lanes(vector):
    rows = rows_for(vector.size)
    return jnp.pad(vector.reshape(-1), (0, rows * 128 - vector.size)).reshape(rows, 128)


def sixteens(rows):
    return jnp.pad(rows, ((0, -rows.shape[0] % 16), (0, 0)))


def per_device(mesh, boundary, lengths, *parts):
    nx, ndp = mesh.shape["segment"], mesh.shape["dp"]
    devices = nx * ndp
    first = lax.axis_index("segment") == 0
    length = jnp.where(first, lengths[0], lengths[1])
    sizes = [parts[k].size for k in VECTORS]

    shards = {k: parts[k].reshape(parts[k].shape[-2:]) for k in MATRICES}
    shards[SMALL] = [parts[k].reshape(1, -1) for k in VECTORS]
    full, pair = planned(gather_all, GATHER, shards, mesh, boundary[0, :, 0])
    for k in MATRICES:
        g = full[k]
        full[k] = g.reshape((nx, ndp * g.shape[1]) + g.shape[2:]) if k < 12 else g.reshape(-1, g.shape[2])
    w = Weights(full[SMALL], full[2], full[4], full[8], full[10], full[12], full[14], full[16])

    outs, saved = forward(pair, length, w)
    outs, gin1, (g_outer1, *both, g_small, g_table) = both_ways(outs, pair, length, w)
    other_outs = from_other(outs[0], outs[1])
    early = {16: g_table.reshape((devices,) + parts[16].shape), 10: g_outer1.reshape((ndp,) + parts[10].shape[1:])}
    names, plan = numbered(EARLY)
    early = [early[k] for k in names]
    if nx == 2 and ndp == 16:
        host, hosted = (plan, ndp // 4), by_chip(early, plan, ndp // 4)
        gin0, grads, sums_early = backward(gin1, pair, saved, w, both, g_small, host, hosted)
    else:
        gin0, grads, _ = backward(gin1, pair, saved, w, both, g_small)
        sums_early = plain_sums(early, plan)
    sums_early = dict(zip(names, sums_early))

    g_outer0, g_inner, g_out, g_value, g_small, g_first, g_second = grads
    grads = {2: g_value, 4: g_out, 8: g_inner, 12: g_first, 14: g_second}
    grads = {k: g.reshape((devices,) + parts[k].shape[-2:]) for k, g in grads.items()}
    grads[10] = g_outer0.reshape((ndp,) + parts[10].shape[1:])
    grads[SMALL] = g_small
    summed, other_gins = planned(scatter_all, SUM, grads, mesh, [gin0, gin1])
    summed[16] = sums_early[16]
    summed[10] = (summed[10], sums_early[10])
    matrices = [summed[k] for k in MATRICES]
    arrays, vectors = finish(outs, other_outs, [gin0, gin1], other_gins, matrices, summed[SMALL], sizes)
    result = {k: g.reshape(parts[k].shape) for k, g in zip(MATRICES, arrays[2:])}
    for k, g in zip(VECTORS, vectors):
        result[k] = g.reshape(parts[k].shape)
    return tuple(a.reshape(boundary.shape) for a in arrays[:2]) + tuple(result[k] for k in range(17))


def solution(mesh):
    layer = [P("segment", "dp")] * 12
    layer[2] = layer[4] = layer[8] = layer[10] = P("segment", "dp", None)
    both = P(AXES)
    rows = P(AXES, None)
    boundary = P("segment", None, "dp", None, None)
    weights = tuple(layer) + (rows, both, rows, both, rows)
    return jax.shard_map(
        functools.partial(per_device, mesh),
        mesh=mesh,
        in_specs=(boundary, P(None, "dp")) + weights,
        out_specs=(boundary, boundary) + weights,
        check_vma=False,
    )
```

```python
import functools
import math
from typing import Any, NamedTuple

import jax
import jax.numpy as jnp
from jax import lax
from jax.experimental import pallas as pl
from jax.experimental.pallas import tpu as pltpu
from jax.sharding import PartitionSpec as P

MESH = pl.DeviceIdType.MESH
HEADS = 12
EPSILON = 1e-05
GELU_SCALE = 0.7978845608028654
AXES = ("segment", "dp")


def half(value):
    return value.astype(jnp.bfloat16)


def wide(value):
    return value.astype(jnp.float32)


def mm(left, right):
    return jnp.dot(left, right, preferred_element_type=jnp.float32)


def mm_tn(left, right):
    return lax.dot_general(left, right, (((0,), (0,)), ((), ())), preferred_element_type=jnp.float32)


def mm_nt(left, right):
    return lax.dot_general(left, right, (((1,), (1,)), ((), ())), preferred_element_type=jnp.float32)


class Place:
    def __init__(self, nz):
        self.nz = nz
        self.x = lax.axis_index("segment")
        d = lax.axis_index("dp")
        self.c = d % 2
        self.y = (d // 2) % 2
        self.z = d // 4
        par = self.z % 2
        self.q = par * ((self.z + 1) // 2) + (1 - par) * ((nz - self.z // 2) % nz)
        self.places = [self.z_at((self.q + 2 * nz - back) % nz) for back in range(nz + 1)]

    def z_at(self, q):
        nz = self.nz
        upper = ((q + nz - 1) % nz) // (nz // 2)
        return (1 - upper) * (2 * q - 1) + upper * ((2 * (nz - q)) % (2 * nz))

    def ring_z(self, back):
        return self.places[back]

    def device(self, x=None, z=None, y=None, c=None):
        x = self.x if x is None else x
        z = self.z if z is None else z
        y = self.y if y is None else y
        c = self.c if c is None else c
        return (x, (z * 2 + y) * 2 + c)

    def other(self, axis):
        return self.device(**{axis: 1 - getattr(self, axis)})

    def succ(self):
        return self.device(z=self.z_at((self.q + 1) % self.nz))

    def pred(self):
        return self.device(z=self.ring_z(1))


def greet(place):
    barrier = pltpu.get_barrier_semaphore()
    peers = [place.other("x"), place.other("y"), place.other("c"), place.succ(), place.pred()]
    for peer in peers:
        pl.semaphore_signal(barrier, inc=1, device_id=peer, device_id_type=MESH)
    pl.semaphore_wait(barrier, len(peers))


def part_of(shape, part):
    rows, cols = shape
    if part is None:
        return (slice(0, rows), slice(0, cols))
    if rows % 32 == 0:
        return (slice(part * rows // 2, (part + 1) * rows // 2), slice(0, cols))
    return (slice(0, rows), slice(part * cols // 2, (part + 1) * cols // 2))


def part_shape(shape, part):
    return tuple(cut.stop - cut.start for cut in part_of(shape, part))


def block_of(ref, cut, c, z, x=None, y=None):
    xs = pl.ds(0, 2) if x is None else x
    ys = pl.ds(0, 2) if y is None else y
    return ref.at[(xs, z, ys, c) + cut]


def gather_rounds(plan, place, nz, shards, outs, prepare, sems):
    which, parts, orders, starts = zip(*plan)
    cuts = [part_of(shards[k].shape, part) for k, part in zip(which, parts)]
    ins = [shards[k].at[cut] for k, cut in zip(which, cuts)]
    outs = [outs[k] for k in which]
    send, recv, local = sems
    ready = set()
    sent = []

    def put(do, i, k, src, dst, device):
        copy = pltpu.make_async_remote_copy(
            src_ref=src,
            dst_ref=dst,
            send_sem=send.at[i, k],
            recv_sem=recv.at[i, k],
            device_id=device,
            device_id_type=MESH,
        )
        do(copy.start)
        sent.append(copy.wait_send)
        return copy

    copies = [dict() for _ in plan]

    def stage(i, t, do):
        first, second, third = orders[i]
        out, mine = outs[i], copies[i]

        def shard(z, **at):
            return block_of(out, cuts[i], place.c, z, **at)

        def own(axis, z):
            return shard(z, **{axis: getattr(place, axis)})

        one = shard(place.z, x=place.x, y=place.y)
        if t == 0:
            if which[i] not in ready:
                ready.add(which[i])
                do(prepare[which[i]])
            mine["own"] = pltpu.make_async_copy(ins[i], one, local.at[i])
            do(mine["own"].start)
        if second == "z":
            if t == 0:
                mine["p"] = put(do, i, 0, ins[i], one, place.other(first))
                return
            if t == 1:
                do(mine["own"].wait)
                do(mine["p"].wait_recv)
            elif t <= nz:
                do(mine["z", t - 1].wait_recv)
            if t <= nz:
                block = own(third, place.ring_z(t - 1))
                if t < nz:
                    mine["z", t] = put(do, i, t, block, block, place.succ())
                mine["l", t] = put(do, i, nz + t, block, block, place.other(third))
                mine["c", t] = put(do, i, 2 * nz + t, block, block, place.other("c"))
            if t >= 2:
                do(mine["l", t - 1].wait_recv)
                block = shard(place.ring_z(t - 2), **{third: 1 - getattr(place, third)})
                mine["d", t - 1] = put(do, i, 3 * nz + t - 1, block, block, place.other("c"))
        else:
            if t <= nz - 1:
                if t > 0:
                    do(mine["z", t].wait_recv)
                z = place.ring_z(t)
                dst = shard(z, x=place.x, y=place.y)
                src = ins[i] if t == 0 else dst
                if t < nz - 1:
                    mine["z", t + 1] = put(do, i, t, src, dst, place.succ())
                mine["p", t + 1] = put(do, i, nz + t, src, dst, place.other(second))
            if 1 <= t <= nz:
                if t == 1:
                    do(mine["own"].wait)
                do(mine["p", t].wait_recv)
                block = own(third, place.ring_z(t - 1))
                mine["l", t] = put(do, i, 2 * nz + t, block, block, place.other(third))
                mine["c", t] = put(do, i, 3 * nz + t, block, block, place.other("c"))
            if t >= 2:
                do(mine["l", t - 1].wait_recv)
                block = shard(place.ring_z(t - 2), **{third: 1 - getattr(place, third)})
                mine["d", t - 1] = put(do, i, 4 * nz + t - 1, block, block, place.other("c"))

    rounds = []
    for t in range(nz + 2 + max(starts)):
        rounds.append([])
        for i in range(len(plan)):
            if 0 <= t - starts[i] < nz + 2:
                stage(i, t - starts[i], rounds[-1].append)
    last = [copy.wait_recv for mine in copies for key, copy in mine.items() if key[0] in "cd"]
    return rounds, last + sent


def gather_sems(plan, nz):
    return [
        pltpu.SemaphoreType.DMA((len(plan), 5 * nz + 2)),
        pltpu.SemaphoreType.DMA((len(plan), 5 * nz + 2)),
        pltpu.SemaphoreType.DMA((len(plan),)),
    ]


def gather_kernel(plan, nz, small_at, count, *refs):
    n = max(entry[0] for entry in plan) + 1
    far, vectors, own, refs = refs[: n - 1], refs[n - 1 : n - 1 + count], refs[n - 1 + count], refs[n + count :]
    outs, pair, raw, shards, refs = refs[:n], refs[n], refs[n + 1 : 2 * n + 1], refs[2 * n + 1 : 3 * n + 1], refs[3 * n + 1 :]
    near, (held, swap, loads), sems = refs[:count], refs[count : count + 3], refs[count + 3 :]
    place = Place(nz)
    moves = list(zip(vectors, near))
    moves += list(zip(far, [ref for k, ref in enumerate(raw) if k != small_at])) + [(own.at[place.x], held)]
    loading = [pltpu.make_async_copy(src, dst, loads.at[j]) for j, (src, dst) in enumerate(moves)]
    for copy in loading:
        copy.start()
    packing, loading = loading[:count], loading[count:]
    loading.insert(small_at, None)
    greet(place)
    stays = pltpu.make_async_copy(held, pair.at[place.x], swap.at[0])
    leaves = pltpu.make_async_remote_copy(
        src_ref=own.at[1 - place.x],
        dst_ref=pair.at[place.x],
        send_sem=swap.at[1],
        recv_sem=swap.at[2],
        device_id=place.other("x"),
        device_id_type=MESH,
    )

    def prepare(k):
        if k == small_at:
            raw[k][...] = jnp.zeros_like(raw[k])
            row = 0
            for copy, vector in zip(packing, near):
                copy.wait()
                for r, lo, many in pieces_of(vector.shape[1], row):
                    raw[k][r : r + 1, :many] = vector[:, lo : lo + many]
                row += rows_for(vector.shape[1])
        else:
            loading[k].wait()
        shards[k][...] = half(raw[k][...])

    ready = [functools.partial(prepare, k) for k in range(n)]
    rounds, last = gather_rounds(plan, place, nz, shards, outs, ready, sems)
    for t, acts in enumerate(rounds):
        for act in acts:
            act()
        if t == 0:
            leaves.start()
        if t == 1:
            loading[-1].wait()
            stays.start()
    for act in last:
        act()
    stays.wait()
    leaves.wait()


def gather_all(shards, plan, mesh, rows):
    nx, ndp = mesh.shape["segment"], mesh.shape["dp"]
    small_at = [isinstance(s, list) for s in shards].index(True)
    vectors = shards[small_at]
    if nx != 2 or ndp != 16:
        first = lax.axis_index("segment") == 0
        other = lax.ppermute(jnp.where(first, rows[1], rows[0]), "segment", [(0, 1), (1, 0)])
        pair = jnp.where(first, jnp.stack([rows[0], other]), jnp.stack([other, rows[1]]))
        packed = sixteens(jnp.concatenate([lanes(v) for v in vectors]))
        shards = [packed if j == small_at else s for j, s in enumerate(shards)]
        return [lax.all_gather(half(s), AXES, axis=0) for s in shards], pair
    nz, n, count = ndp // 4, len(shards), len(vectors)
    height = sum(rows_for(v.size) for v in vectors)
    shapes = [(height + -height % 16, 128) if j == small_at else s.shape for j, s in enumerate(shards)]
    far = [s for j, s in enumerate(shards) if j != small_at]
    *outs, pair = pl.pallas_call(
        functools.partial(gather_kernel, plan, nz, small_at, count),
        out_shape=[jax.ShapeDtypeStruct((2, nz, 2, 2) + s, jnp.bfloat16) for s in shapes]
        + [jax.ShapeDtypeStruct(rows.shape, rows.dtype)],
        in_specs=[pl.BlockSpec(memory_space=pl.ANY)] * (n + count),
        out_specs=[pl.BlockSpec(memory_space=pl.ANY)] * (n + 1),
        scratch_shapes=[pltpu.VMEM(s, jnp.float32) for s in shapes]
        + [pltpu.VMEM(s, jnp.bfloat16) for s in shapes]
        + [pltpu.VMEM(v.shape, v.dtype) for v in vectors]
        + [
            pltpu.VMEM(rows.shape[1:], rows.dtype),
            pltpu.SemaphoreType.DMA((3,)),
            pltpu.SemaphoreType.DMA((n + count,)),
        ]
        + gather_sems(plan, nz),
        compiler_params=pltpu.CompilerParams(collective_id=0, has_side_effects=True, vmem_limit_bytes=62 * 2**20),
        name="gather_weights",
    )(*far, *vectors, rows)
    return [o.reshape((nx * ndp,) + s) for o, s in zip(outs, shapes)], pair


def add_to(dst, src):
    lead = dst.shape[:-2]

    def one(j, carry):
        at = (j // 2, j % 2) if len(lead) == 2 else (j,)[: len(lead)]
        at = at + (slice(None), slice(None))
        dst[at] = dst[at] + src[at]
        return carry

    if lead:
        lax.fori_loop(0, math.prod(lead), one, 0)
    else:
        dst[...] = dst[...] + src[...]


def sum_rounds(plan, place, nz, ins, outs, refs):
    which, parts, orders, starts, only = zip(*plan)
    cuts = [part_of(outs[k].shape, part) for k, part in zip(which, parts)]
    ins = [ins[k] for k in which]
    outs = [outs[k].at[cut] for k, cut in zip(which, cuts)]
    n = len(plan)
    accs, stages, firsts, rings, lasts = (refs[j * n : (j + 1) * n] for j in range(5))
    send, recv, local = refs[5 * n :]
    sent = []

    def put(do, i, k, src, dst, device):
        copy = pltpu.make_async_remote_copy(
            src_ref=src,
            dst_ref=dst,
            send_sem=send.at[i, k],
            recv_sem=recv.at[i, k],
            device_id=device,
            device_id_type=MESH,
        )
        do(copy.start)
        sent.append(copy.wait_send)
        return copy

    live = [dict() for _ in plan]

    def source(i, c, z):
        if only[i] is None:
            return block_of(ins[i], cuts[i], c, z)
        return ins[i].at[(z, pl.ds(0, 2), c) + cuts[i]]

    def load(do, i, k):
        copy = pltpu.make_async_copy(source(i, place.c, place.ring_z(k)), stages[i].at[k % 2], local.at[i, k % 2])
        do(copy.start)
        live[i]["o", k] = copy

    def stage(i, s, do):
        first, second, third = orders[i]
        acc, mine = accs[i], live[i]
        early, ring, late = firsts[i], rings[i], lasts[i]

        def part(k, **own):
            at = (own.get("y", pl.ds(0, 2)),)
            if only[i] is None:
                at = (own.get("x", pl.ds(0, 2)),) + at
            return acc.at[(k - 1,) + at]

        here = {axis: getattr(place, axis) for axis in "xy"}
        one = {first: here[first]}

        def there(axis, **own):
            own[axis] = 1 - here[axis]
            return own

        def step(dst, src):
            do(lambda: add_to(dst(), src()))

        def write(left, right):
            def out():
                outs[i][...] = wide(left()[...]) + wide(right()[...])

            do(out)

        if s == 0:
            for k in range(1, nz + 1):
                mine["c", k] = put(do, i, k, source(i, 1 - place.c, place.ring_z(k)), acc.at[k - 1], place.other("c"))
            load(do, i, 1)
            load(do, i, 2)
        if 1 <= s <= nz:
            k = s
            do(mine["c", k].wait_recv)
            do(mine["o", k].wait)
            step(lambda: acc.at[k - 1], lambda: stages[i].at[k % 2])
            if k + 2 <= nz:
                load(do, i, k + 2)
            mine["p", k] = put(do, i, nz + k, part(k, **there(first)), early.at[k - 1], place.other(first))
        if 2 <= s <= nz + 1:
            j = s - 1
            do(mine["p", j].wait_recv)
            step(lambda: part(j, **one), lambda: early.at[j - 1])
        if second == "z":
            if s == 2:
                mine["z", 1] = put(do, i, 2 * nz + 1, part(1, **one), ring.at[0], place.succ())
            if 3 <= s <= nz + 1:
                t = s - 2
                do(mine["z", t].wait_recv)
                step(lambda: ring.at[t - 1], lambda: part(t + 1, **one))
                if t < nz - 1:
                    mine["z", t + 1] = put(do, i, 2 * nz + t + 1, ring.at[t - 1], ring.at[t], place.succ())
                else:
                    src = ring.at[t - 1] if only[i] is not None else ring.at[t - 1, 1 - here[third]]
                    mine["l"] = put(do, i, 3 * nz + 1, src, late, place.other(third))
            if s == nz + 2:
                do(mine["l"].wait_recv)
                write(lambda: ring.at[nz - 2] if only[i] is not None else ring.at[nz - 2, here[third]], lambda: late)
        else:
            if 2 <= s <= nz + 1:
                j = s - 1
                src = part(j, **there(second, **one))
                mine["l", j] = put(do, i, 3 * nz + j, src, late.at[j - 1], place.other(second))
            if 3 <= s <= nz + 2:
                h = s - 2
                do(mine["l", h].wait_recv)
                step(lambda: part(h, **here), lambda: late.at[h - 1])
                if h == 1:
                    mine["z", 1] = put(do, i, 2 * nz + 1, part(1, **here), ring.at[0], place.succ())
                else:
                    t = h - 1
                    do(mine["z", t].wait_recv)
                    if t < nz - 1:
                        step(lambda: ring.at[t - 1], lambda: part(t + 1, **here))
                        mine["z", t + 1] = put(do, i, 2 * nz + t + 1, ring.at[t - 1], ring.at[t], place.succ())
                    else:
                        write(lambda: ring.at[t - 1], lambda: part(nz, **here))

    rounds = []
    for t in range(nz + 3 + max(starts)):
        rounds.append([])
        for i in range(n):
            if 0 <= t - starts[i] < nz + 3:
                stage(i, t - starts[i], rounds[-1].append)
    return rounds, sent


def sum_scratch(plan, grads, nz):
    def scratch(lead):
        return [
            pltpu.VMEM(lead(order, () if only is not None else (2,)) + part_shape(grads[k].shape[-2:], part), grads[k].dtype)
            for k, part, order, _, only in plan
        ]

    return (
        scratch(lambda o, x: (nz,) + x + (2,))
        + scratch(lambda o, x: (2,) + x + (2,))
        + scratch(lambda o, x: (nz,) + x)
        + scratch(lambda o, x: (nz - 1,) + x if o[1] == "z" else (nz - 1,))
        + scratch(lambda o, x: () if o[1] == "z" else (nz,))
        + [
            pltpu.SemaphoreType.DMA((len(plan), 4 * nz + 2)),
            pltpu.SemaphoreType.DMA((len(plan), 4 * nz + 2)),
            pltpu.SemaphoreType.DMA((len(plan), 2)),
        ]
    )


def by_chip(grads, plan, nz):
    only = dict((k, entry) for k, _, _, _, entry in plan)
    return [
        g.reshape(((2,) if only[k] is None else ()) + (nz, 2, 2) + g.shape[1:]) for k, g in enumerate(grads)
    ]


def scatter_kernel(plan, nz, *refs):
    n = max(entry[0] for entry in plan) + 1
    ins, here, refs = refs[:n], refs[n : n + 2], refs[n + 2 :]
    outs, there, refs, swap = refs[:n], refs[n], refs[n + 1 : -1], refs[-1]
    place = Place(nz)
    greet(place)
    rounds, sent = sum_rounds(plan, place, nz, ins, outs, refs)
    swaps = [
        pltpu.make_async_remote_copy(
            src_ref=ref,
            dst_ref=there,
            send_sem=swap.at[0],
            recv_sem=swap.at[1],
            device_id=place.other("x"),
            device_id_type=MESH,
        )
        for ref in here
    ]
    for t, acts in enumerate(rounds):
        for act in acts:
            act()
        if t == 0:
            pl.when(place.x == 0)(swaps[1].start)
            pl.when(place.x == 1)(swaps[0].start)
    for act in sent:
        act()
    swaps[0].wait()


def finish_kernel(count, chosen, *refs):
    n = len(chosen)
    ys, other_ys, gin0, gin1, other_gins, refs = refs[:5] + (refs[5:],)
    ins = []
    for two in chosen:
        ins.append(refs[: 1 + two])
        refs = refs[1 + two :]
    packed, outs, refs = refs[0], refs[1 : 3 + n], refs[3 + n :]
    vectors, held, (rows, sem) = refs[:count], refs[count:-2], refs[-2:]
    x = lax.axis_index("segment")
    moves = [((ys.at[x],), rows.at[0, 0], outs[0].at[x]), ((other_ys,), rows.at[0, 1], outs[0].at[1 - x])]
    moves += [((gin0, gin1), rows.at[1, 0], outs[1].at[x]), ((other_gins,), rows.at[1, 1], outs[1].at[1 - x])]
    moves += list(zip(ins, held, outs[2:]))
    steps = []
    for j, (sources, via, dst) in enumerate(moves):
        loads = [pltpu.make_async_copy(src, via, sem.at[j, 0]) for src in sources]
        if len(loads) == 1:
            loads[0].start()
        else:
            pl.when(x == 0)(loads[0].start)
            pl.when(x == 1)(loads[1].start)
        steps.append((loads[0], pltpu.make_async_copy(via, dst, sem.at[j, 1])))
    row = 0
    for dst in vectors:
        for r, lo, many in pieces_of(dst.shape[1], row):
            dst[:, lo : lo + many] = packed[r : r + 1, :many]
        row += rows_for(dst.shape[1])
    for load, store in steps:
        load.wait()
        store.start()
    for load, store in steps:
        store.wait()


def finish(ys, other_ys, gins, other_gins, arrays, packed, sizes):
    chosen = [isinstance(a, tuple) for a in arrays]
    flat = [part for a in arrays for part in (a if isinstance(a, tuple) else (a,))]
    first = [a[0] if isinstance(a, tuple) else a for a in arrays]
    like = [jax.ShapeDtypeStruct(a.shape, a.dtype) for a in [ys, ys] + first]
    vectors = [jax.ShapeDtypeStruct((1, size), jnp.float32) for size in sizes]
    far, near = pl.BlockSpec(memory_space=pl.ANY), pl.BlockSpec(memory_space=pltpu.VMEM)
    got = pl.pallas_call(
        functools.partial(finish_kernel, len(sizes), chosen),
        out_shape=like + vectors,
        in_specs=[far] * (5 + len(flat)) + [near],
        out_specs=[far] * len(like) + [near] * len(sizes),
        scratch_shapes=[pltpu.VMEM(a.shape, a.dtype) for a in first]
        + [pltpu.VMEM((2,) + ys.shape, ys.dtype), pltpu.SemaphoreType.DMA((4 + len(arrays), 2))],
        compiler_params=pltpu.CompilerParams(vmem_limit_bytes=62 * 2**20),
        name="finish",
    )(ys, other_ys, *gins, other_gins, *flat, packed)
    return got[: len(like)], got[len(like) :]


def from_other(first_rows, second_rows):
    payload = jnp.where(lax.axis_index("segment") == 0, second_rows, first_rows)
    return lax.ppermute(payload, "segment", [(0, 1), (1, 0)])


def plain_sums(grads, plan):
    only = dict((k, entry) for k, _, _, _, entry in plan)
    got = []
    for k, g in enumerate(grads):
        if only[k] is None:
            got.append(wide(lax.psum_scatter(g, AXES, scatter_dimension=0, tiled=False)))
        else:
            got.append(wide(lax.psum_scatter(lax.psum(g, "segment"), "dp", scatter_dimension=0, tiled=False)))
    return got


def scatter_all(grads, plan, mesh, rows):
    nx, ndp = mesh.shape["segment"], mesh.shape["dp"]
    if nx != 2 or ndp != 16:
        return plain_sums(grads, plan), from_other(*rows)
    nz, n = ndp // 4, len(grads)
    far, near = pl.BlockSpec(memory_space=pl.ANY), pl.BlockSpec(memory_space=pltpu.VMEM)
    got = pl.pallas_call(
        functools.partial(scatter_kernel, plan, nz),
        out_shape=[jax.ShapeDtypeStruct(g.shape[1:], jnp.float32) for g in grads]
        + [jax.ShapeDtypeStruct(rows[0].shape, rows[0].dtype)],
        in_specs=[far] * (n + 2),
        out_specs=[near] * n + [far],
        scratch_shapes=sum_scratch(plan, grads, nz) + [pltpu.SemaphoreType.DMA((2,))],
        compiler_params=pltpu.CompilerParams(
            collective_id=1, has_side_effects=True, vmem_limit_bytes=62 * 2**20
        ),
        name="sum_gradients",
    )(*by_chip(grads, plan, nz), *rows)
    return got[:n], got[n]


ROWS = 512
HIDDEN = 768
GAIN1, BIAS1, VALUE_B, OUT_B, GAIN2, BIAS2, OUTER_B, FIRST_B = range(8)
VECTOR_ROWS = 7


def rows_for(size):
    return -(-size // 128)


def pieces_of(size, row):
    return [(row + j, j * 128, min(128, size - j * 128)) for j in range(rows_for(size))]


def unpack_rows(small, at, ndp, row, ref):
    size = ref.shape[1] // ndp
    for d in range(ndp):
        for r, lo, n in pieces_of(size, row):
            ref[:, d * size + lo : d * size + lo + n] = wide(small[at + d])[r : r + 1, :n]


def unpack_vectors(small, at, ndp, ref):
    size = ref.shape[1] // ndp
    for d in range(ndp):
        ref[:, d * size : (d + 1) * size] = wide(small[at + d])[: ref.shape[0], :size]


def pack_rows(ref, ndp, row, small, at):
    size = ref.shape[1] // ndp
    for d in range(ndp):
        for r, lo, n in pieces_of(size, row):
            small[at + d, r : r + 1, :n] = ref[:, d * size + lo : d * size + lo + n]


def pack_vectors(ref, ndp, small, at):
    size = ref.shape[1] // ndp
    for d in range(ndp):
        small[at + d, :VECTOR_ROWS, :size] = ref[:VECTOR_ROWS, d * size : (d + 1) * size]


def chunks(rows, size=ROWS):
    return [slice(at, at + size) for at in range(0, rows, size)]


def norm_parts(rows):
    centre = rows - jnp.mean(rows, axis=-1, keepdims=True)
    inv = lax.rsqrt(jnp.mean(centre * centre, axis=-1, keepdims=True) + EPSILON)
    return centre * inv, inv


def row_loop(rows, body, init):
    return lax.fori_loop(0, rows // 128, lambda j, c: body(pl.ds(pl.multiple_of(j * 128, 128), 128), c), init)


def norm_into(read, write, gain, shift, rows):
    def body(r, carry):
        write[r, :] = half(norm_parts(read(r))[0] * gain + shift)
        return carry

    row_loop(rows, body, 0)


def norm_back(read, grad, gain, rows, done):
    def body(r, carry):
        normal, inv = norm_parts(read(r))
        m_hat = grad(r)
        m = m_hat * gain
        part = inv * (
            m - jnp.mean(m, axis=-1, keepdims=True) - normal * jnp.mean(m * normal, axis=-1, keepdims=True)
        )
        done(r, part)
        return carry[0] + sums(m_hat * normal), carry[1] + sums(m_hat)

    zero = jnp.zeros_like(gain)
    return row_loop(rows, body, (zero, zero))


def sums(value):
    return jnp.sum(wide(value), axis=0, keepdims=True)


def gelu_both(t):
    square = t * t
    s = 0.5 + 0.5 * jnp.tanh(t * (GELU_SCALE + GELU_SCALE * 0.044715 * square))
    value = t * s
    slope = s + value * (1.0 - s) * (2 * GELU_SCALE + 6 * GELU_SCALE * 0.044715 * square)
    return value, slope


def masked_pair(head):
    return lax.broadcasted_iota(jnp.int32, (1, 2 * head), 1) < head


def beside(i, steps, rounds):
    for at, acts in zip(steps, rounds):

        @pl.when(i == at)
        def _(acts=acts):
            for act in acts:
                act()


def add_up(fresh, ref, at, value):
    @pl.when(fresh)
    def _():
        ref[at] = value

    @pl.when(jnp.logical_not(fresh))
    def _():
        ref[at] += value


def forward_start(read, vec, value_ref, a_ref, v_ref, first=None):
    rows = a_ref.shape[0]
    norm_into(read, a_ref, vec(GAIN1), vec(BIAS1), rows)
    for r in chunks(rows):
        v_ref[r] = half(mm(a_ref[r], value_ref[...]) + vec(VALUE_B))
        if first is not None:
            first_ref, first_b, p_ref, slope_ref = first
            value, slope = gelu_both(mm(a_ref[r], first_ref[...]) + first_b[...])
            p_ref[r] = half(value)
            slope_ref[r] = half(slope)


def both_heads(pair, head):
    lower = masked_pair(head)
    zero = jnp.zeros_like(pair)
    return jnp.concatenate([jnp.where(lower, pair, zero), jnp.where(lower, zero, pair)], axis=0)


def forward_heads(pair, length, v_ref, c_ref, probs_ref, logits_of, bounded=False):
    rows, width = v_ref.shape
    slots = probs_ref.shape[1] // 2
    head = width // HEADS
    at = pl.ds(pl.multiple_of(pair * 2 * head, 2 * head), 2 * head)
    shut = jnp.where(lax.broadcasted_iota(jnp.int32, (1, slots), 1) >= length, -1e30, 0.0)
    both = logits_of(shut)
    for h in range(2):
        logits = both[h]
        expo = jnp.exp(logits if bounded else logits - jnp.max(logits, axis=1, keepdims=True))
        probs_ref[:, h * slots : (h + 1) * slots] = half(expo * (1.0 / jnp.sum(expo, axis=1, keepdims=True)))
    c_ref[:, at] = half(mm(probs_ref[...], both_heads(v_ref[:, at], head)))


def forward_middle(read, vec, out_ref, c_ref, hid_ref, b_ref):
    rows = c_ref.shape[0]
    for r in chunks(rows):
        hid_ref[r] = read(r) + mm(c_ref[r], out_ref[...]) + vec(OUT_B)
    norm_into(lambda r: hid_ref[r, :], b_ref, vec(GAIN2), vec(BIAS2), rows)


def forward_hidden(fresh, b_ref, inner_ref, inner_b, outer_ref, q_ref, slope_ref, acc):
    for r in chunks(b_ref.shape[0]):
        value, slope = gelu_both(mm(b_ref[r], inner_ref[...]) + inner_b)
        q = half(value)
        q_ref[r] = q
        slope_ref[r] = half(slope)
        add_up(fresh, acc, r, mm(q, outer_ref[...]))


def forward_end(vec, hid_ref, acc, y_ref):
    for r in chunks(acc.shape[0]):
        y_ref[r] = half(hid_ref[r] + acc[r] + vec(OUTER_B))


def backward_hidden(fresh, g_ref, b_ref, q_ref, slope_ref, inner_ref, outer_ref, gz_ref, acc, g_outer, g_inner, g_inner_b):
    for r in chunks(g_ref.shape[0]):
        gz = half(mm_nt(g_ref[r], outer_ref[...]) * wide(slope_ref[r]))
        gz_ref[r] = gz
        add_up(fresh, acc, r, mm_nt(gz, inner_ref[...]))
    gz = gz_ref[...]
    g_outer[...] = half(mm_tn(q_ref[...], g_ref[...]))
    g_inner[...] = half(mm_tn(b_ref[...], gz))
    g_inner_b[...] = sums(gz)


def backward_middle(vec, put, g_ref, hid_ref, c_ref, out_ref, acc, ghid, gatt, gc_ref, g_out):
    rows = g_ref.shape[0]

    def done(r, part):
        total = wide(g_ref[r, :]) + part
        ghid[r, :] = total
        gatt[r, :] = half(total)

    gain, shift = norm_back(lambda r: hid_ref[r, :], lambda r: acc[r, :], vec(GAIN2), rows, done)
    put(GAIN2, gain)
    put(BIAS2, shift)
    put(OUTER_B, sums(g_ref[...]))
    put(OUT_B, sums(gatt[...]))
    g_out[...] = half(mm_tn(c_ref[...], gatt[...]))
    for r in chunks(rows):
        gc_ref[r] = half(mm_nt(gatt[r], out_ref[...]))


def backward_heads(pair, v_ref, c_ref, gc_ref, gv_ref, probs_ref, db):
    rows, width = v_ref.shape
    slots = probs_ref.shape[1] // 2
    head = width // HEADS
    at = pl.ds(pl.multiple_of(pair * 2 * head, 2 * head), 2 * head)
    both = mm_nt(gc_ref[:, at], both_heads(v_ref[:, at], head))
    along = wide(gc_ref[:, at]) * wide(c_ref[:, at])
    lower = masked_pair(head)
    for h in range(2):
        cols = slice(h * slots, (h + 1) * slots)
        mean = jnp.sum(jnp.where(lower if h == 0 else jnp.logical_not(lower), along, 0.0), axis=1, keepdims=True)
        db[:, cols] = half(wide(probs_ref[:, cols]) * (both[:, cols] - mean))
    values = mm_tn(probs_ref[...], gc_ref[:, at])
    gv_ref[:, at] = half(jnp.where(masked_pair(head), values[:slots], values[slots:]))


def backward_end(vec, put, read, gv_ref, value_ref, a_ref, acc, ghid, g_value, gx_ref, first=None):
    rows = gv_ref.shape[0]
    put(VALUE_B, sums(gv_ref[...]))
    g_value[...] = half(mm_tn(a_ref[...], gv_ref[...]))
    if first is not None:
        first_ref, slope_ref, gf_ref, g_first = first
        for r in chunks(rows):
            gf_ref[r] = half(acc[r] * wide(slope_ref[r]))
        put(FIRST_B, sums(gf_ref[...]))
        g_first[...] = half(mm_tn(a_ref[...], gf_ref[...]))
    else:
        put(FIRST_B, jnp.zeros((1, acc.shape[1]), jnp.float32))
    for r in chunks(rows):
        ga = mm_nt(gv_ref[r], value_ref[...])
        if first is not None:
            ga = ga + mm_nt(gf_ref[r], first_ref[...])
        acc[r] = ga

    def done(r, part):
        gx_ref[r, :] = half(ghid[r, :] + part)

    gain, shift = norm_back(read, lambda r: acc[r, :], vec(GAIN1), rows, done)
    put(GAIN1, gain)
    put(BIAS1, shift)


def forward_kernel(pairs, parts, host, length_ref, x_ref, small, value_ref, out_ref, first_ref, second_ref, inner_ref, outer_ref, *refs):
    n = 1 if host else 0
    far, y_ref, refs = refs[:n], refs[n], refs[n + 1 :]
    kept, probs_ref, q_ref, slope_ref, table, refs = refs[:7], refs[7], refs[8], refs[9], refs[10 : 10 + n], refs[10 + n :]
    a_ref, v_ref, p_ref, first_slope, c_ref, b_ref, hid_ref, acc, vectors, inner_b, first_b, second_b, sem, *refs = refs
    rounds, last = [], []
    if host:
        raw, shard, load, *sems = refs
        place = Place(host[1])
        loading = pltpu.make_async_copy(far[0], raw, load.at[0])

        def prepare():
            loading.start()
            greet(place)
            loading.wait()
            shard[...] = half(raw[...])

        rounds, last = gather_rounds(host[0], place, host[1], [shard], table, [prepare], sems)
    held = (a_ref, v_ref, p_ref, first_slope, c_ref, b_ref, hid_ref)
    copies = [pltpu.make_async_copy(src, dst, sem.at[j]) for j, (src, dst) in enumerate(zip(held, kept))]
    i = pl.program_id(0)
    slots = probs_ref.shape[2] // 2
    ndp, part = small.shape[0] // 2, q_ref.shape[1]

    def vec(k):
        return vectors[k : k + 1, :]

    x_ref, y_ref = x_ref.at[0], y_ref.at[0]
    length = length_ref[lax.axis_index("segment"), 0]

    def read(r):
        return wide(x_ref[r, :])

    beside(i, BESIDE_FORWARD, rounds)

    @pl.when(i == 0)
    def _():
        unpack_vectors(small, 0, ndp, vectors)
        unpack_rows(small, 0, ndp, VECTOR_ROWS, inner_b)
        row = VECTOR_ROWS + rows_for(inner_b.shape[1] // ndp)
        unpack_rows(small, 0, 2 * ndp, row, first_b)
        unpack_rows(small, 0, 2 * ndp, row + rows_for(first_b.shape[1] // (2 * ndp)), second_b)
        forward_start(read, vec, value_ref.at[0], a_ref, v_ref, (first_ref, first_b, p_ref, first_slope))
        for copy in copies[:4]:
            copy.start()

    @pl.when(i < pairs)
    def _():
        def logits_of(shut):
            bias = second_b[:, pl.ds(pl.multiple_of(i * 2 * slots, 2 * slots), 2 * slots)]
            logits = mm(p_ref[...], second_ref[...]) + (bias + jnp.concatenate([shut, shut], axis=1))
            return logits[:, :slots], logits[:, slots:]

        forward_heads(i, length, v_ref, c_ref, probs_ref.at[0], logits_of)

    @pl.when(i == pairs - 1)
    def _():
        forward_middle(read, vec, out_ref.at[0], c_ref, hid_ref, b_ref)
        for copy in copies[4:]:
            copy.start()

    @pl.when(i >= pairs)
    def _():
        bias = inner_b[:, pl.ds(pl.multiple_of((i - pairs) * part, part), part)]
        forward_hidden(i == pairs, b_ref, inner_ref.at[0], bias, outer_ref.at[0], q_ref, slope_ref, acc)

    @pl.when(i == pairs + parts - 1)
    def _():
        forward_end(vec, hid_ref, acc, y_ref)
        for copy in copies:
            copy.wait()
        for acts in rounds[len(BESIDE_FORWARD) :] + [last]:
            for act in acts:
                act()


def backward_kernel(pairs, parts, host, g_ref, b_ref, small, g_small1, q_ref, slope_ref, probs_ref, inner_ref, outer_ref, second_ref, *refs):
    far, refs = refs[:10], refs[13:]
    n, swaps = (max(entry[0] for entry in host[0]) + 1, 1) if host else (0, 0)
    sum_ins, ys, refs = refs[:n], refs[n : n + swaps], refs[n + swaps :]
    gx_ref, g_outer, g_inner, g_out, g_value, g_small, g_first, g_second = refs[:8]
    sum_outs, other_ys, refs = refs[8 : 8 + n], refs[8 + n : 8 + n + swaps], refs[8 + n + swaps :]
    near, refs = refs[:10], refs[10:]
    acc, ghid, gatt, gc_ref, gv_ref, db, gz_ref, vectors, g_vec, g_inner_b, g_second_b, sem, *refs = refs
    far = [ref.at[0] if len(ref.shape) == 3 else ref for ref in far]
    copies = [pltpu.make_async_copy(src, dst, sem.at[j]) for j, (src, dst) in enumerate(zip(far, near))]
    hid_ref, c_ref, out_ref, v_ref, p_ref, a_ref, value_ref, first_ref, first_slope, x_ref = near
    i = pl.program_id(0)
    rounds, sent = [], []
    if host:
        place = Place(host[1])
        pl.when(i == 0)(lambda: greet(place))
        *refs, swap = refs
        rounds, sent = sum_rounds(host[0], place, host[1], sum_ins, sum_outs, refs)
        swapped = pltpu.make_async_remote_copy(
            src_ref=ys[0].at[1 - place.x],
            dst_ref=other_ys[0],
            send_sem=swap.at[0],
            recv_sem=swap.at[1],
            device_id=place.other("x"),
            device_id_type=MESH,
        )
        rounds[0].append(swapped.start)
        sent.append(swapped.wait)
    slots = probs_ref.shape[2] // 2
    ndp, part = small.shape[0] // 2, q_ref.shape[1]

    def vec(k):
        return vectors[k : k + 1, :]

    def put(k, value):
        g_vec[k : k + 1, :] = value

    @pl.when(i == 0)
    def _():
        for copy in copies:
            copy.start()
        unpack_vectors(small, 0, ndp, vectors)

    beside(i, BESIDE_BACKWARD, rounds)

    @pl.when(i < parts)
    def _():
        bias = g_inner_b.at[:, pl.ds(pl.multiple_of(i * part, part), part)]
        backward_hidden(i == 0, g_ref, b_ref, q_ref, slope_ref, inner_ref.at[0], outer_ref.at[0], gz_ref, acc, g_outer, g_inner.at[0], bias)

    @pl.when(i == parts - 1)
    def _():
        for copy in copies[:3]:
            copy.wait()
        backward_middle(vec, put, g_ref, hid_ref, c_ref, out_ref, acc, ghid, gatt, gc_ref, g_out.at[0])
        for copy in copies[3:5]:
            copy.wait()

    @pl.when(i >= parts)
    def _():
        backward_heads(i - parts, v_ref, c_ref, gc_ref, gv_ref, probs_ref.at[0], db)
        g_second[...] = half(mm_tn(p_ref[...], db[...]))
        g_second_b[:, pl.ds(pl.multiple_of((i - parts) * 2 * slots, 2 * slots), 2 * slots)] = sums(db[...])
        add_up(i == parts, acc, slice(None), mm_nt(db[...], second_ref[...]))

    @pl.when(i == pairs + parts - 1)
    def _():
        for copy in copies[5:]:
            copy.wait()
        backward_end(
            vec, put, lambda r: wide(x_ref[r, :]), gv_ref, value_ref, a_ref, acc, ghid, g_value.at[0], gx_ref,
            (first_ref, first_slope, gatt, g_first),
        )
        g_small[:ndp] = jnp.zeros_like(g_small1)
        g_small[ndp:] = g_small1[...]
        pack_vectors(g_vec, ndp, g_small, 0)
        pack_rows(g_inner_b, ndp, VECTOR_ROWS, g_small, 0)
        row = VECTOR_ROWS + rows_for(g_inner_b.shape[1] // ndp)
        pack_rows(g_vec.at[FIRST_B : FIRST_B + 1, :], 2 * ndp, row, g_small, 0)
        row += rows_for(g_vec.shape[1] // (2 * ndp))
        pack_rows(g_second_b, 2 * ndp, row, g_small, 0)
        for acts in rounds[len(BESIDE_BACKWARD) :] + [sent]:
            for act in acts:
                act()


def both_kernel(pairs, parts, length_ref, x_ref, g_ref, small, value_ref, out_ref, table_ref, inner_ref, outer_ref, *refs):
    y_ref, gx_ref, g_outer, g_inner, g_out, g_value, g_small, g_table = refs[:8]
    acc, hid_ref, ghid, a_ref, v_ref, c_ref, b_ref, gatt, gc_ref, gv_ref, probs_ref, q_ref, slope_ref, db, gz_ref, *refs = refs[8:]
    vectors, inner_b, g_vec, g_inner_b = refs
    i = pl.program_id(0)
    slots = probs_ref.shape[2] // 2
    j = i - pairs
    k = j - parts
    n = k - parts

    ndp, part = small.shape[0] // 2, q_ref.shape[2]

    def vec(k):
        return vectors[k : k + 1, :]

    def put(k, value):
        g_vec[k : k + 1, :] = value

    def hidden(ref, k):
        return ref.at[:, pl.ds(pl.multiple_of(k * part, part), part)]

    x_ref, g_ref, y_ref = (ref.at[0] for ref in (x_ref, g_ref, y_ref))

    def read(r):
        return wide(x_ref[r, :])

    @pl.when(i == 0)
    def _():
        unpack_vectors(small, ndp, ndp, vectors)
        unpack_rows(small, ndp, ndp, VECTOR_ROWS, inner_b)
        forward_start(read, vec, value_ref.at[0], a_ref, v_ref)

    @pl.when(i < pairs)
    def _():
        def logits_of(shut):
            return wide(table_ref[:slots, :]) + shut, wide(table_ref[slots:, :]) + shut

        forward_heads(i, length_ref[lax.axis_index("segment"), 0], v_ref, c_ref, probs_ref.at[i], logits_of, True)

    @pl.when(i == pairs - 1)
    def _():
        forward_middle(read, vec, out_ref.at[0], c_ref, hid_ref, b_ref)

    @pl.when((j >= 0) & (j < parts))
    def _():
        forward_hidden(j == 0, b_ref, inner_ref.at[0], hidden(inner_b, j)[...], outer_ref.at[0], q_ref.at[j], slope_ref.at[j], acc)

    @pl.when(j == parts - 1)
    def _():
        forward_end(vec, hid_ref, acc, y_ref)

    @pl.when((k >= 0) & (k < parts))
    def _():
        at = parts - 1 - k
        backward_hidden(k == 0, g_ref, b_ref, q_ref.at[at], slope_ref.at[at], inner_ref.at[0], outer_ref.at[0], gz_ref, acc, g_outer, g_inner.at[0], hidden(g_inner_b, at))

    @pl.when(k == parts - 1)
    def _():
        backward_middle(vec, put, g_ref, hid_ref, c_ref, out_ref.at[0], acc, ghid, gatt, gc_ref, g_out.at[0])

    @pl.when(n >= 0)
    def _():
        backward_heads(n, v_ref, c_ref, gc_ref, gv_ref, probs_ref.at[n], db)
        g_table[:slots, :] = db[:, :slots]
        g_table[slots:, :] = db[:, slots:]

    @pl.when(n == pairs - 1)
    def _():
        backward_end(vec, put, read, gv_ref, value_ref.at[0], a_ref, acc, ghid, g_value.at[0], gx_ref)
        g_small[...] = jnp.zeros_like(g_small)
        pack_vectors(g_vec, ndp, g_small, 0)
        pack_rows(g_inner_b, ndp, VECTOR_ROWS, g_small, 0)


class Weights(NamedTuple):
    small: Any
    value: Any
    out: Any
    inner: Any
    outer: Any
    first: Any
    second: Any
    table: Any


def whole(shape, *at):
    at = tuple(at)
    block = (1,) * len(at) + tuple(shape[len(at) :])
    return pl.BlockSpec(block, lambda i: at + (0,) * (len(shape) - len(at)), pipeline_mode=pl.Buffered(1))


def whole_out(shape, *at):
    at = tuple(at)
    block = (1,) * len(at) + tuple(shape[len(at) :])
    return pl.BlockSpec(block, lambda i: at + (0,) * (len(shape) - len(at)))


def like(shape, dtype=jnp.bfloat16):
    return jax.ShapeDtypeStruct(shape, dtype)


FAR = pl.BlockSpec(memory_space=pl.ANY)


def sizes_of(x, w):
    rows, width = x.shape[-2:]
    parts = w.inner.shape[2] // HIDDEN
    return rows, width, HEADS // 2, parts, w.inner.shape[2] // parts


def forward(x, lengths, w, host=None, late=()):
    rows, width, pairs, parts, part = sizes_of(x, w)
    slots = rows

    def pair(i):
        return jnp.minimum(i, pairs - 1)

    def piece(i):
        return jnp.maximum(i - pairs, 0)

    ins = [lengths, x, w.small, w.value, w.out, w.first, w.second, w.inner, w.outer] + list(late)
    specs = [
        pl.BlockSpec(memory_space=pltpu.SMEM),
        whole(x.shape, 0),
        whole(w.small.shape),
        whole(w.value.shape, 0),
        whole(w.out.shape, 0),
        whole(w.first.shape),
        pl.BlockSpec((width, 2 * slots), lambda i: (0, pair(i))),
        pl.BlockSpec((1, width, part), lambda i: (0, 0, piece(i))),
        pl.BlockSpec((1, part, width), lambda i: (0, piece(i), 0)),
    ] + [FAR] * len(late)
    table = [like((2, host[1], 2, 2) + t.shape) for t in late]
    half_rows = like((rows, width))
    kept = [half_rows] * 6 + [like((rows, width), jnp.float32)]
    hidden_block = pl.BlockSpec((rows, part), lambda i: (0, piece(i)))
    y, *saved = pl.pallas_call(
        functools.partial(forward_kernel, pairs, parts, host),
        grid=(pairs + parts,),
        out_shape=[like(x.shape)] + kept + [like((pairs, rows, 2 * slots))] + [like((rows, part * parts))] * 2 + table,
        in_specs=specs,
        out_specs=[whole_out(x.shape, 0)]
        + [FAR] * 7
        + [pl.BlockSpec((1, rows, 2 * slots), lambda i: (pair(i), 0, 0))]
        + [hidden_block] * 2
        + [FAR] * len(table),
        scratch_shapes=[pltpu.VMEM(k.shape, k.dtype) for k in kept]
        + [
            pltpu.VMEM((rows, width), jnp.float32),
            pltpu.VMEM((8, width), jnp.float32),
            pltpu.VMEM((1, part * parts), jnp.float32),
            pltpu.VMEM((1, width), jnp.float32),
            pltpu.VMEM((1, w.second.shape[1]), jnp.float32),
            pltpu.SemaphoreType.DMA((7,)),
        ]
        + [pltpu.VMEM(t.shape, t.dtype) for t in late]
        + [pltpu.VMEM(t.shape, jnp.bfloat16) for t in late]
        + ([pltpu.SemaphoreType.DMA((1,))] + gather_sems(*host) if host else []),
        compiler_params=pltpu.CompilerParams(
            vmem_limit_bytes=62 * 2**20, **(dict(collective_id=3, has_side_effects=True) if host else {})
        ),
        name="forward_0",
    )(*ins)
    return y, saved[:10], saved[10:]


def backward(g, x, saved, w, before, small1, host=None, early=(), ys=()):
    rows, width, pairs, parts, part = sizes_of(x, w)
    slots = rows
    a, v, p, first_slope, c, b, hid, probs, q, slope = saved

    def pair(i):
        return jnp.maximum(i - parts, 0)

    def piece(i):
        return jnp.minimum(i, parts - 1)

    hidden_block = pl.BlockSpec((rows, part), lambda i: (0, piece(i)))
    inner_block = pl.BlockSpec((1, width, part), lambda i: (0, 0, piece(i)))
    outer_block = pl.BlockSpec((1, part, width), lambda i: (0, piece(i), 0))
    second_block = pl.BlockSpec((width, 2 * slots), lambda i: (0, pair(i)))
    far = [hid, c, w.out, v, p, a, w.value, w.first, first_slope, x]
    ins = [g, b, w.small, small1, q, slope, probs, w.inner, w.outer, w.second] + far
    specs = [whole((rows, width))] * 2 + [whole(w.small.shape), whole(small1.shape)] + [hidden_block] * 2
    specs += [pl.BlockSpec((1, rows, 2 * slots), lambda i: (pair(i), 0, 0)), inner_block, outer_block, second_block]
    specs += [FAR] * 10
    aliases = {len(ins) + j: 2 + j for j in range(3)}
    ins += list(before) + list(early) + list(ys)
    specs += [FAR] * (3 + len(early) + len(ys))
    outs = [like((rows, width)), like(w.outer.shape[1:])] + [like(k.shape, k.dtype) for k in before]
    out_specs = [whole_out((rows, width)), pl.BlockSpec((part, width), lambda i: (piece(i), 0)), inner_block]
    out_specs += [whole_out(w.out.shape, 0), whole_out(w.value.shape, 0)]
    outs += [like(w.small.shape, jnp.float32), like(w.first.shape), like(w.second.shape)]
    out_specs += [whole_out(w.small.shape), whole_out(w.first.shape), second_block]
    sums_of = [like(e.shape[-2:], jnp.float32) for e in early]
    gx, *grads = pl.pallas_call(
        functools.partial(backward_kernel, pairs, parts, host),
        grid=(pairs + parts,),
        out_shape=outs + sums_of + [like(y.shape[1:]) for y in ys],
        in_specs=specs,
        out_specs=out_specs + [whole_out(e.shape) for e in sums_of] + [FAR] * len(ys),
        scratch_shapes=[pltpu.VMEM(k.shape[-2:], k.dtype) for k in far]
        + [pltpu.VMEM((rows, width), jnp.float32)] * 2
        + [pltpu.VMEM((rows, width), jnp.bfloat16)] * 3
        + [pltpu.VMEM((rows, 2 * slots), jnp.bfloat16), pltpu.VMEM((rows, part), jnp.bfloat16)]
        + [pltpu.VMEM((8, width), jnp.float32)] * 2
        + [pltpu.VMEM((1, part * parts), jnp.float32), pltpu.VMEM((1, w.second.shape[1]), jnp.float32)]
        + [pltpu.SemaphoreType.DMA((10,))]
        + (sum_scratch(host[0], early, host[1]) + [pltpu.SemaphoreType.DMA((2,))] if host else []),
        input_output_aliases=aliases,
        compiler_params=pltpu.CompilerParams(
            vmem_limit_bytes=63 * 2**20, **(dict(collective_id=2, has_side_effects=True) if host else {})
        ),
        name="backward_0",
    )(*ins)
    return gx, grads[:7], grads[7:]


def both_ways(x, g, lengths, w):
    rows, width, pairs, parts, part = sizes_of(x, w)
    slots = rows

    def there(i):
        return jnp.minimum(i, pairs - 1)

    def back(i):
        return jnp.maximum(i - pairs - 2 * parts, 0)

    def piece(i):
        j = jnp.clip(i - pairs, 0, 2 * parts - 1)
        return jnp.minimum(j, 2 * parts - 1 - j)

    def late(i):
        return parts - 1 - jnp.clip(i - pairs - parts, 0, parts - 1)

    ins = [lengths, x, g, w.small, w.value, w.out, w.table, w.inner, w.outer]
    specs = [pl.BlockSpec(memory_space=pltpu.SMEM), whole(x.shape, 0), whole(g.shape, 1)]
    specs += [whole(w.small.shape), whole(w.value.shape, 1), whole(w.out.shape, 1)]
    specs += [
        pl.BlockSpec((2 * slots, slots), lambda i: (there(i), 0)),
        pl.BlockSpec((1, width, part), lambda i: (1, 0, piece(i))),
        pl.BlockSpec((1, part, width), lambda i: (1, piece(i), 0)),
    ]
    grads = [like(w.outer.shape[1:]), like(w.inner.shape), like(w.out.shape), like(w.value.shape)]
    small = (w.small.shape[0] // 2,) + w.small.shape[1:]
    grads += [like(small, jnp.float32), like(w.table.shape)]
    grad_specs = [
        pl.BlockSpec((part, width), lambda i: (late(i), 0)),
        pl.BlockSpec((1, width, part), lambda i: (1, 0, late(i))),
        whole_out(w.out.shape, 1),
        whole_out(w.value.shape, 1),
        whole_out(small),
        pl.BlockSpec((2 * slots, slots), lambda i: (back(i), 0)),
    ]
    y, gx, *grads = pl.pallas_call(
        functools.partial(both_kernel, pairs, parts),
        grid=(2 * pairs + 2 * parts,),
        out_shape=[like(x.shape), like((rows, width))] + grads,
        in_specs=specs,
        out_specs=[whole_out(x.shape, 1), whole_out((rows, width))] + grad_specs,
        scratch_shapes=[pltpu.VMEM((rows, width), jnp.float32)] * 3
        + [pltpu.VMEM((rows, width), jnp.bfloat16)] * 7
        + [pltpu.VMEM((pairs, rows, 2 * slots), jnp.bfloat16)]
        + [pltpu.VMEM((parts, rows, part), jnp.bfloat16)] * 2
        + [pltpu.VMEM((rows, 2 * slots), jnp.bfloat16), pltpu.VMEM((rows, part), jnp.bfloat16)]
        + [pltpu.VMEM((8, width), jnp.float32), pltpu.VMEM((1, part * parts), jnp.float32)] * 2,
        input_output_aliases={1: 0},
        compiler_params=pltpu.CompilerParams(vmem_limit_bytes=62 * 2**20),
        name="forward_backward_1",
    )(*ins)
    return y, gx, grads


ROW_VECTORS = (0, 1, 3, 5, 6, 7, 11)
VECTORS = ROW_VECTORS + (9, 13, 15)
MATRICES = (2, 4, 8, 10, 12, 14, 16)
SMALL = 17
GATHER = (
    (12, None, "zyx", 2),
    (4, None, "zyx", 2),
    (14, 0, "xzy", 3),
    (SMALL, None, "zyx", 3),
    (2, None, "xzy", 0),
    (14, 1, "yzx", 2),
    (10, None, "xzy", 1),
    (8, None, "zyx", 0),
)
LATE = ((16, 0, "zyx", 0), (16, 1, "xzy", 0))
BESIDE_FORWARD = (0, 1, 3, 5, 7, 9)
EARLY = ((10, 1, "yzx", 1, 1), (10, 0, "yzx", 0, 1), (16, 1, "yxz", 1, None), (16, 0, "xzy", 1, None))
BESIDE_BACKWARD = (0, 0, 1, 3, 4, 7, 9)
SUM = (
    (4, None, "yzx", 0, None),
    (14, 1, "yzx", 1, None),
    (10, None, "yzx", 2, 0),
    (2, None, "yzx", 3, None),
    (12, None, "yxz", 2, None),
    (14, 0, "xzy", 1, None),
    (8, None, "xyz", 2, None),
    (SMALL, None, "xzy", 2, None),
)


def numbered(plan):
    names = list(dict.fromkeys(entry[0] for entry in plan))
    return names, [(names.index(entry[0]),) + entry[1:] for entry in plan]


def planned(call, plan, arrays, mesh, rows):
    names, plan = numbered(plan)
    got, rows = call([arrays[k] for k in names], plan, mesh, rows)
    return dict(zip(names, got)), rows


def lanes(vector):
    rows = rows_for(vector.size)
    return jnp.pad(vector.reshape(-1), (0, rows * 128 - vector.size)).reshape(rows, 128)


def sixteens(rows):
    return jnp.pad(rows, ((0, -rows.shape[0] % 16), (0, 0)))


def per_device(mesh, boundary, lengths, *parts):
    nx, ndp = mesh.shape["segment"], mesh.shape["dp"]
    devices = nx * ndp
    fast = nx == 2 and ndp == 16
    sizes = [parts[k].size for k in VECTORS]

    shards = {k: parts[k].reshape(parts[k].shape[-2:]) for k in MATRICES}
    shards[SMALL] = [parts[k].reshape(1, -1) for k in VECTORS]
    full, pair = planned(gather_all, GATHER, shards, mesh, boundary[0, :, 0])
    if not fast:
        full[16] = lax.all_gather(half(shards[16]), AXES, axis=0)
    for k in full:
        if k == SMALL:
            continue
        g = full[k]
        full[k] = g.reshape((nx, ndp * g.shape[1]) + g.shape[2:]) if k < 12 else g.reshape(-1, g.shape[2])
    w = Weights(full[SMALL], full[2], full[4], full[8], full[10], full[12], full[14], full.get(16))

    if fast:
        outs, saved, (table,) = forward(pair, lengths, w, (numbered(LATE)[1], ndp // 4), [shards[16]])
        w = w._replace(table=table.reshape(-1, table.shape[-1]))
    else:
        outs, saved, _ = forward(pair, lengths, w)
    outs, gin1, (g_outer1, *both, g_small, g_table) = both_ways(outs, pair, lengths, w)
    early = {16: g_table.reshape((devices,) + parts[16].shape), 10: g_outer1.reshape((ndp,) + parts[10].shape[1:])}
    names, plan = numbered(EARLY)
    early = [early[k] for k in names]
    if fast:
        host, hosted = (plan, ndp // 4), by_chip(early, plan, ndp // 4)
        gin0, grads, (*sums_early, other_outs) = backward(gin1, pair, saved, w, both, g_small, host, hosted, [outs])
    else:
        gin0, grads, _ = backward(gin1, pair, saved, w, both, g_small)
        sums_early = plain_sums(early, plan)
        other_outs = from_other(outs[0], outs[1])
    sums_early = dict(zip(names, sums_early))

    g_outer0, g_inner, g_out, g_value, g_small, g_first, g_second = grads
    grads = {2: g_value, 4: g_out, 8: g_inner, 12: g_first, 14: g_second}
    grads = {k: g.reshape((devices,) + parts[k].shape[-2:]) for k, g in grads.items()}
    grads[10] = g_outer0.reshape((ndp,) + parts[10].shape[1:])
    grads[SMALL] = g_small
    summed, other_gins = planned(scatter_all, SUM, grads, mesh, [gin0, gin1])
    summed[16] = sums_early[16]
    summed[10] = (summed[10], sums_early[10])
    matrices = [summed[k] for k in MATRICES]
    arrays, vectors = finish(outs, other_outs, [gin0, gin1], other_gins, matrices, summed[SMALL], sizes)
    result = {k: g.reshape(parts[k].shape) for k, g in zip(MATRICES, arrays[2:])}
    for k, g in zip(VECTORS, vectors):
        result[k] = g.reshape(parts[k].shape)
    return tuple(a.reshape(boundary.shape) for a in arrays[:2]) + tuple(result[k] for k in range(17))


def solution(mesh):
    layer = [P("segment", "dp")] * 12
    layer[2] = layer[4] = layer[8] = layer[10] = P("segment", "dp", None)
    both = P(AXES)
    rows = P(AXES, None)
    boundary = P("segment", None, "dp", None, None)
    weights = tuple(layer) + (rows, both, rows, both, rows)
    return jax.shard_map(
        functools.partial(per_device, mesh),
        mesh=mesh,
        in_specs=(boundary, P(None, "dp")) + weights,
        out_specs=(boundary, boundary) + weights,
        check_vma=False,
    )
```

```python
import functools
import math
from typing import Any, NamedTuple

import jax
import jax.numpy as jnp
from jax import lax
from jax.experimental import pallas as pl
from jax.experimental.pallas import tpu as pltpu
from jax.sharding import PartitionSpec as P

MESH = pl.DeviceIdType.MESH
HEADS = 12
EPSILON = 1e-05
GELU_SCALE = 0.7978845608028654
AXES = ("segment", "dp")


def half(value):
    return value.astype(jnp.bfloat16)


def wide(value):
    return value.astype(jnp.float32)


def mm(left, right):
    return jnp.dot(left, right, preferred_element_type=jnp.float32)


def mm_tn(left, right):
    return lax.dot_general(left, right, (((0,), (0,)), ((), ())), preferred_element_type=jnp.float32)


def mm_nt(left, right):
    return lax.dot_general(left, right, (((1,), (1,)), ((), ())), preferred_element_type=jnp.float32)


class Place:
    def __init__(self, nz):
        self.nz = nz
        self.x = lax.axis_index("segment")
        d = lax.axis_index("dp")
        self.c = d % 2
        self.y = (d // 2) % 2
        self.z = d // 4
        par = self.z % 2
        self.q = par * ((self.z + 1) // 2) + (1 - par) * ((nz - self.z // 2) % nz)
        self.places = [self.z_at((self.q + 2 * nz - back) % nz) for back in range(nz + 1)]

    def z_at(self, q):
        nz = self.nz
        upper = ((q + nz - 1) % nz) // (nz // 2)
        return (1 - upper) * (2 * q - 1) + upper * ((2 * (nz - q)) % (2 * nz))

    def ring_z(self, back):
        return self.places[back]

    def device(self, x=None, z=None, y=None, c=None):
        x = self.x if x is None else x
        z = self.z if z is None else z
        y = self.y if y is None else y
        c = self.c if c is None else c
        return (x, (z * 2 + y) * 2 + c)

    def other(self, axis):
        return self.device(**{axis: 1 - getattr(self, axis)})

    def succ(self):
        return self.device(z=self.z_at((self.q + 1) % self.nz))

    def pred(self):
        return self.device(z=self.ring_z(1))


def greet(place):
    barrier = pltpu.get_barrier_semaphore()
    peers = [place.other("x"), place.other("y"), place.other("c"), place.succ(), place.pred()]
    for peer in peers:
        pl.semaphore_signal(barrier, inc=1, device_id=peer, device_id_type=MESH)
    pl.semaphore_wait(barrier, len(peers))


def part_of(shape, part):
    rows, cols = shape
    if part is None:
        return (slice(0, rows), slice(0, cols))
    if rows % 32 == 0:
        return (slice(part * rows // 2, (part + 1) * rows // 2), slice(0, cols))
    return (slice(0, rows), slice(part * cols // 2, (part + 1) * cols // 2))


def part_shape(shape, part):
    return tuple(cut.stop - cut.start for cut in part_of(shape, part))


def block_of(ref, cut, c, z, x=None, y=None):
    xs = pl.ds(0, 2) if x is None else x
    ys = pl.ds(0, 2) if y is None else y
    return ref.at[(xs, z, ys, c) + cut]


def gather_rounds(plan, place, nz, shards, outs, prepare, sems):
    which, parts, orders, starts = zip(*plan)
    cuts = [part_of(shards[k].shape, part) for k, part in zip(which, parts)]
    ins = [shards[k].at[cut] for k, cut in zip(which, cuts)]
    outs = [outs[k] for k in which]
    send, recv, local = sems
    ready = set()
    sent = []

    def put(do, i, k, src, dst, device):
        copy = pltpu.make_async_remote_copy(
            src_ref=src,
            dst_ref=dst,
            send_sem=send.at[i, k],
            recv_sem=recv.at[i, k],
            device_id=device,
            device_id_type=MESH,
        )
        do(copy.start)
        sent.append(copy.wait_send)
        return copy

    copies = [dict() for _ in plan]

    def stage(i, t, do):
        first, second, third = orders[i]
        out, mine = outs[i], copies[i]

        def shard(z, **at):
            return block_of(out, cuts[i], place.c, z, **at)

        def own(axis, z):
            return shard(z, **{axis: getattr(place, axis)})

        one = shard(place.z, x=place.x, y=place.y)
        if t == 0:
            if which[i] not in ready:
                ready.add(which[i])
                do(prepare[which[i]])
            mine["own"] = pltpu.make_async_copy(ins[i], one, local.at[i])
            do(mine["own"].start)
        if second == "z":
            if t == 0:
                mine["p"] = put(do, i, 0, ins[i], one, place.other(first))
                return
            if t == 1:
                do(mine["own"].wait)
                do(mine["p"].wait_recv)
            elif t <= nz:
                do(mine["z", t - 1].wait_recv)
            if t <= nz:
                block = own(third, place.ring_z(t - 1))
                if t < nz:
                    mine["z", t] = put(do, i, t, block, block, place.succ())
                mine["l", t] = put(do, i, nz + t, block, block, place.other(third))
                mine["c", t] = put(do, i, 2 * nz + t, block, block, place.other("c"))
            if t >= 2:
                do(mine["l", t - 1].wait_recv)
                block = shard(place.ring_z(t - 2), **{third: 1 - getattr(place, third)})
                mine["d", t - 1] = put(do, i, 3 * nz + t - 1, block, block, place.other("c"))
        else:
            if t <= nz - 1:
                if t > 0:
                    do(mine["z", t].wait_recv)
                z = place.ring_z(t)
                dst = shard(z, x=place.x, y=place.y)
                src = ins[i] if t == 0 else dst
                if t < nz - 1:
                    mine["z", t + 1] = put(do, i, t, src, dst, place.succ())
                mine["p", t + 1] = put(do, i, nz + t, src, dst, place.other(second))
            if 1 <= t <= nz:
                if t == 1:
                    do(mine["own"].wait)
                do(mine["p", t].wait_recv)
                block = own(third, place.ring_z(t - 1))
                mine["l", t] = put(do, i, 2 * nz + t, block, block, place.other(third))
                mine["c", t] = put(do, i, 3 * nz + t, block, block, place.other("c"))
            if t >= 2:
                do(mine["l", t - 1].wait_recv)
                block = shard(place.ring_z(t - 2), **{third: 1 - getattr(place, third)})
                mine["d", t - 1] = put(do, i, 4 * nz + t - 1, block, block, place.other("c"))

    rounds = []
    for t in range(nz + 2 + max(starts)):
        rounds.append([])
        for i in range(len(plan)):
            if 0 <= t - starts[i] < nz + 2:
                stage(i, t - starts[i], rounds[-1].append)
    last = [copy.wait_recv for mine in copies for key, copy in mine.items() if key[0] in "cd"]
    return rounds, last + sent


def gather_sems(plan, nz):
    return [
        pltpu.SemaphoreType.DMA((len(plan), 5 * nz + 2)),
        pltpu.SemaphoreType.DMA((len(plan), 5 * nz + 2)),
        pltpu.SemaphoreType.DMA((len(plan),)),
    ]


def gather_kernel(plan, nz, small_at, count, *refs):
    n = max(entry[0] for entry in plan) + 1
    far, vectors, own, refs = refs[: n - 1], refs[n - 1 : n - 1 + count], refs[n - 1 + count], refs[n + count :]
    outs, pair, raw, shards, refs = refs[:n], refs[n], refs[n + 1 : 2 * n + 1], refs[2 * n + 1 : 3 * n + 1], refs[3 * n + 1 :]
    near, (held, swap, loads), sems = refs[:count], refs[count : count + 3], refs[count + 3 :]
    place = Place(nz)
    moves = list(zip(vectors, near))
    moves += list(zip(far, [ref for k, ref in enumerate(raw) if k != small_at])) + [(own.at[place.x], held)]
    loading = [pltpu.make_async_copy(src, dst, loads.at[j]) for j, (src, dst) in enumerate(moves)]
    for copy in loading:
        copy.start()
    packing, loading = loading[:count], loading[count:]
    loading.insert(small_at, None)
    greet(place)
    stays = pltpu.make_async_copy(held, pair.at[place.x], swap.at[0])
    leaves = pltpu.make_async_remote_copy(
        src_ref=own.at[1 - place.x],
        dst_ref=pair.at[place.x],
        send_sem=swap.at[1],
        recv_sem=swap.at[2],
        device_id=place.other("x"),
        device_id_type=MESH,
    )

    def prepare(k):
        if k == small_at:
            raw[k][...] = jnp.zeros_like(raw[k])
            row = 0
            for copy, vector in zip(packing, near):
                copy.wait()
                for r, lo, many in pieces_of(vector.shape[1], row):
                    raw[k][r : r + 1, :many] = vector[:, lo : lo + many]
                row += rows_for(vector.shape[1])
        else:
            loading[k].wait()
        shards[k][...] = half(raw[k][...])

    ready = [functools.partial(prepare, k) for k in range(n)]
    rounds, last = gather_rounds(plan, place, nz, shards, outs, ready, sems)
    for t, acts in enumerate(rounds):
        for act in acts:
            act()
        if t == 0:
            leaves.start()
        if t == 1:
            loading[-1].wait()
            stays.start()
    for act in last:
        act()
    stays.wait()
    leaves.wait()


def gather_all(shards, plan, mesh, rows):
    nx, ndp = mesh.shape["segment"], mesh.shape["dp"]
    small_at = [isinstance(s, list) for s in shards].index(True)
    vectors = shards[small_at]
    if nx != 2 or ndp != 16:
        first = lax.axis_index("segment") == 0
        other = lax.ppermute(jnp.where(first, rows[1], rows[0]), "segment", [(0, 1), (1, 0)])
        pair = jnp.where(first, jnp.stack([rows[0], other]), jnp.stack([other, rows[1]]))
        packed = sixteens(jnp.concatenate([lanes(v) for v in vectors]))
        shards = [packed if j == small_at else s for j, s in enumerate(shards)]
        return [lax.all_gather(half(s), AXES, axis=0) for s in shards], pair
    nz, n, count = ndp // 4, len(shards), len(vectors)
    height = sum(rows_for(v.size) for v in vectors)
    shapes = [(height + -height % 16, 128) if j == small_at else s.shape for j, s in enumerate(shards)]
    far = [s for j, s in enumerate(shards) if j != small_at]
    *outs, pair = pl.pallas_call(
        functools.partial(gather_kernel, plan, nz, small_at, count),
        out_shape=[jax.ShapeDtypeStruct((2, nz, 2, 2) + s, jnp.bfloat16) for s in shapes]
        + [jax.ShapeDtypeStruct(rows.shape, rows.dtype)],
        in_specs=[pl.BlockSpec(memory_space=pl.ANY)] * (n + count),
        out_specs=[pl.BlockSpec(memory_space=pl.ANY)] * (n + 1),
        scratch_shapes=[pltpu.VMEM(s, jnp.float32) for s in shapes]
        + [pltpu.VMEM(s, jnp.bfloat16) for s in shapes]
        + [pltpu.VMEM(v.shape, v.dtype) for v in vectors]
        + [
            pltpu.VMEM(rows.shape[1:], rows.dtype),
            pltpu.SemaphoreType.DMA((3,)),
            pltpu.SemaphoreType.DMA((n + count,)),
        ]
        + gather_sems(plan, nz),
        compiler_params=pltpu.CompilerParams(collective_id=0, has_side_effects=True, vmem_limit_bytes=62 * 2**20),
        name="gather_weights",
    )(*far, *vectors, rows)
    return [o.reshape((nx * ndp,) + s) for o, s in zip(outs, shapes)], pair


def add_to(dst, src):
    lead = dst.shape[:-2]

    def one(j, carry):
        at = (j // 2, j % 2) if len(lead) == 2 else (j,)[: len(lead)]
        at = at + (slice(None), slice(None))
        dst[at] = dst[at] + src[at]
        return carry

    if lead:
        lax.fori_loop(0, math.prod(lead), one, 0)
    else:
        dst[...] = dst[...] + src[...]


def sum_rounds(plan, place, nz, ins, outs, refs):
    which, parts, orders, starts, only = zip(*plan)
    cuts = [part_of(outs[k].shape, part) for k, part in zip(which, parts)]
    ins = [ins[k] for k in which]
    outs = [outs[k].at[cut] for k, cut in zip(which, cuts)]
    n = len(plan)
    accs, stages, firsts, rings, lasts = (refs[j * n : (j + 1) * n] for j in range(5))
    send, recv, local = refs[5 * n :]
    sent = []

    def put(do, i, k, src, dst, device):
        copy = pltpu.make_async_remote_copy(
            src_ref=src,
            dst_ref=dst,
            send_sem=send.at[i, k],
            recv_sem=recv.at[i, k],
            device_id=device,
            device_id_type=MESH,
        )
        do(copy.start)
        sent.append(copy.wait_send)
        return copy

    live = [dict() for _ in plan]

    def source(i, c, z):
        if only[i] is None:
            return block_of(ins[i], cuts[i], c, z)
        return ins[i].at[(z, pl.ds(0, 2), c) + cuts[i]]

    def load(do, i, k):
        copy = pltpu.make_async_copy(source(i, place.c, place.ring_z(k)), stages[i].at[k % 2], local.at[i, k % 2])
        do(copy.start)
        live[i]["o", k] = copy

    def stage(i, s, do):
        first, second, third = orders[i]
        acc, mine = accs[i], live[i]
        early, ring, late = firsts[i], rings[i], lasts[i]

        def part(k, **own):
            at = (own.get("y", pl.ds(0, 2)),)
            if only[i] is None:
                at = (own.get("x", pl.ds(0, 2)),) + at
            return acc.at[(k - 1,) + at]

        here = {axis: getattr(place, axis) for axis in "xy"}
        one = {first: here[first]}

        def there(axis, **own):
            own[axis] = 1 - here[axis]
            return own

        def step(dst, src):
            do(lambda: add_to(dst(), src()))

        def write(left, right):
            def out():
                outs[i][...] = wide(left()[...]) + wide(right()[...])

            do(out)

        if s == 0:
            for k in range(1, nz + 1):
                mine["c", k] = put(do, i, k, source(i, 1 - place.c, place.ring_z(k)), acc.at[k - 1], place.other("c"))
            load(do, i, 1)
            load(do, i, 2)
        if 1 <= s <= nz:
            k = s
            do(mine["c", k].wait_recv)
            do(mine["o", k].wait)
            step(lambda: acc.at[k - 1], lambda: stages[i].at[k % 2])
            if k + 2 <= nz:
                load(do, i, k + 2)
            mine["p", k] = put(do, i, nz + k, part(k, **there(first)), early.at[k - 1], place.other(first))
        if 2 <= s <= nz + 1:
            j = s - 1
            do(mine["p", j].wait_recv)
            step(lambda: part(j, **one), lambda: early.at[j - 1])
        if second == "z":
            if s == 2:
                mine["z", 1] = put(do, i, 2 * nz + 1, part(1, **one), ring.at[0], place.succ())
            if 3 <= s <= nz + 1:
                t = s - 2
                do(mine["z", t].wait_recv)
                step(lambda: ring.at[t - 1], lambda: part(t + 1, **one))
                if t < nz - 1:
                    mine["z", t + 1] = put(do, i, 2 * nz + t + 1, ring.at[t - 1], ring.at[t], place.succ())
                else:
                    src = ring.at[t - 1] if only[i] is not None else ring.at[t - 1, 1 - here[third]]
                    mine["l"] = put(do, i, 3 * nz + 1, src, late, place.other(third))
            if s == nz + 2:
                do(mine["l"].wait_recv)
                write(lambda: ring.at[nz - 2] if only[i] is not None else ring.at[nz - 2, here[third]], lambda: late)
        else:
            if 2 <= s <= nz + 1:
                j = s - 1
                src = part(j, **there(second, **one))
                mine["l", j] = put(do, i, 3 * nz + j, src, late.at[j - 1], place.other(second))
            if 3 <= s <= nz + 2:
                h = s - 2
                do(mine["l", h].wait_recv)
                step(lambda: part(h, **here), lambda: late.at[h - 1])
                if h == 1:
                    mine["z", 1] = put(do, i, 2 * nz + 1, part(1, **here), ring.at[0], place.succ())
                else:
                    t = h - 1
                    do(mine["z", t].wait_recv)
                    if t < nz - 1:
                        step(lambda: ring.at[t - 1], lambda: part(t + 1, **here))
                        mine["z", t + 1] = put(do, i, 2 * nz + t + 1, ring.at[t - 1], ring.at[t], place.succ())
                    else:
                        write(lambda: ring.at[t - 1], lambda: part(nz, **here))

    rounds = []
    for t in range(nz + 3 + max(starts)):
        rounds.append([])
        for i in range(n):
            if 0 <= t - starts[i] < nz + 3:
                stage(i, t - starts[i], rounds[-1].append)
    return rounds, sent


def sum_scratch(plan, grads, nz):
    def scratch(lead):
        return [
            pltpu.VMEM(lead(order, () if only is not None else (2,)) + part_shape(grads[k].shape[-2:], part), grads[k].dtype)
            for k, part, order, _, only in plan
        ]

    return (
        scratch(lambda o, x: (nz,) + x + (2,))
        + scratch(lambda o, x: (2,) + x + (2,))
        + scratch(lambda o, x: (nz,) + x)
        + scratch(lambda o, x: (nz - 1,) + x if o[1] == "z" else (nz - 1,))
        + scratch(lambda o, x: () if o[1] == "z" else (nz,))
        + [
            pltpu.SemaphoreType.DMA((len(plan), 4 * nz + 2)),
            pltpu.SemaphoreType.DMA((len(plan), 4 * nz + 2)),
            pltpu.SemaphoreType.DMA((len(plan), 2)),
        ]
    )


def by_chip(grads, plan, nz):
    only = dict((k, entry) for k, _, _, _, entry in plan)
    return [
        g.reshape(((2,) if only[k] is None else ()) + (nz, 2, 2) + g.shape[1:]) for k, g in enumerate(grads)
    ]


def scatter_kernel(plan, nz, *refs):
    n = max(entry[0] for entry in plan) + 1
    ins, here, refs = refs[:n], refs[n : n + 2], refs[n + 2 :]
    outs, there, refs, swap = refs[:n], refs[n], refs[n + 1 : -1], refs[-1]
    place = Place(nz)
    greet(place)
    rounds, sent = sum_rounds(plan, place, nz, ins, outs, refs)
    swaps = [
        pltpu.make_async_remote_copy(
            src_ref=ref,
            dst_ref=there,
            send_sem=swap.at[0],
            recv_sem=swap.at[1],
            device_id=place.other("x"),
            device_id_type=MESH,
        )
        for ref in here
    ]
    for t, acts in enumerate(rounds):
        for act in acts:
            act()
        if t == 0:
            pl.when(place.x == 0)(swaps[1].start)
            pl.when(place.x == 1)(swaps[0].start)
    for act in sent:
        act()
    swaps[0].wait()


def finish_kernel(count, chosen, *refs):
    n = len(chosen)
    ys, other_ys, gin0, gin1, other_gins, refs = refs[:5] + (refs[5:],)
    ins = []
    for two in chosen:
        ins.append(refs[: 1 + two])
        refs = refs[1 + two :]
    packed, outs, refs = refs[0], refs[1 : 3 + n], refs[3 + n :]
    vectors, held, (rows, sem) = refs[:count], refs[count:-2], refs[-2:]
    x = lax.axis_index("segment")
    moves = [((ys.at[x],), rows.at[0, 0], outs[0].at[x]), ((other_ys,), rows.at[0, 1], outs[0].at[1 - x])]
    moves += [((gin0, gin1), rows.at[1, 0], outs[1].at[x]), ((other_gins,), rows.at[1, 1], outs[1].at[1 - x])]
    moves += list(zip(ins, held, outs[2:]))
    steps = []
    for j, (sources, via, dst) in enumerate(moves):
        loads = [pltpu.make_async_copy(src, via, sem.at[j, 0]) for src in sources]
        if len(loads) == 1:
            loads[0].start()
        else:
            pl.when(x == 0)(loads[0].start)
            pl.when(x == 1)(loads[1].start)
        steps.append((loads[0], pltpu.make_async_copy(via, dst, sem.at[j, 1])))
    row = 0
    for dst in vectors:
        for r, lo, many in pieces_of(dst.shape[1], row):
            dst[:, lo : lo + many] = packed[r : r + 1, :many]
        row += rows_for(dst.shape[1])
    for load, store in steps:
        load.wait()
        store.start()
    for load, store in steps:
        store.wait()


def finish(ys, other_ys, gins, other_gins, arrays, packed, sizes):
    chosen = [isinstance(a, tuple) for a in arrays]
    flat = [part for a in arrays for part in (a if isinstance(a, tuple) else (a,))]
    first = [a[0] if isinstance(a, tuple) else a for a in arrays]
    like = [jax.ShapeDtypeStruct(a.shape, a.dtype) for a in [ys, ys] + first]
    vectors = [jax.ShapeDtypeStruct((1, size), jnp.float32) for size in sizes]
    far, near = pl.BlockSpec(memory_space=pl.ANY), pl.BlockSpec(memory_space=pltpu.VMEM)
    got = pl.pallas_call(
        functools.partial(finish_kernel, len(sizes), chosen),
        out_shape=like + vectors,
        in_specs=[far] * (5 + len(flat)) + [near],
        out_specs=[far] * len(like) + [near] * len(sizes),
        scratch_shapes=[pltpu.VMEM(a.shape, a.dtype) for a in first]
        + [pltpu.VMEM((2,) + ys.shape, ys.dtype), pltpu.SemaphoreType.DMA((4 + len(arrays), 2))],
        compiler_params=pltpu.CompilerParams(vmem_limit_bytes=62 * 2**20),
        name="finish",
    )(ys, other_ys, *gins, other_gins, *flat, packed)
    return got[: len(like)], got[len(like) :]


def from_other(first_rows, second_rows):
    payload = jnp.where(lax.axis_index("segment") == 0, second_rows, first_rows)
    return lax.ppermute(payload, "segment", [(0, 1), (1, 0)])


def plain_sums(grads, plan):
    only = dict((k, entry) for k, _, _, _, entry in plan)
    got = []
    for k, g in enumerate(grads):
        if only[k] is None:
            got.append(wide(lax.psum_scatter(g, AXES, scatter_dimension=0, tiled=False)))
        else:
            got.append(wide(lax.psum_scatter(lax.psum(g, "segment"), "dp", scatter_dimension=0, tiled=False)))
    return got


def scatter_all(grads, plan, mesh, rows):
    nx, ndp = mesh.shape["segment"], mesh.shape["dp"]
    if nx != 2 or ndp != 16:
        return plain_sums(grads, plan), from_other(*rows)
    nz, n = ndp // 4, len(grads)
    far, near = pl.BlockSpec(memory_space=pl.ANY), pl.BlockSpec(memory_space=pltpu.VMEM)
    got = pl.pallas_call(
        functools.partial(scatter_kernel, plan, nz),
        out_shape=[jax.ShapeDtypeStruct(g.shape[1:], jnp.float32) for g in grads]
        + [jax.ShapeDtypeStruct(rows[0].shape, rows[0].dtype)],
        in_specs=[far] * (n + 2),
        out_specs=[near] * n + [far],
        scratch_shapes=sum_scratch(plan, grads, nz) + [pltpu.SemaphoreType.DMA((2,))],
        compiler_params=pltpu.CompilerParams(
            collective_id=1, has_side_effects=True, vmem_limit_bytes=62 * 2**20
        ),
        name="sum_gradients",
    )(*by_chip(grads, plan, nz), *rows)
    return got[:n], got[n]


ROWS = 512
HIDDEN = 768
GAIN1, BIAS1, VALUE_B, OUT_B, GAIN2, BIAS2, OUTER_B, FIRST_B = range(8)
VECTOR_ROWS = 7


def rows_for(size):
    return -(-size // 128)


def pieces_of(size, row):
    return [(row + j, j * 128, min(128, size - j * 128)) for j in range(rows_for(size))]


def unpack_rows(small, at, ndp, row, ref):
    size = ref.shape[1] // ndp
    for d in range(ndp):
        for r, lo, n in pieces_of(size, row):
            ref[:, d * size + lo : d * size + lo + n] = wide(small[at + d])[r : r + 1, :n]


def unpack_vectors(small, at, ndp, ref):
    size = ref.shape[1] // ndp
    for d in range(ndp):
        ref[:, d * size : (d + 1) * size] = wide(small[at + d])[: ref.shape[0], :size]


def pack_rows(ref, ndp, row, small, at):
    size = ref.shape[1] // ndp
    for d in range(ndp):
        for r, lo, n in pieces_of(size, row):
            small[at + d, r : r + 1, :n] = ref[:, d * size + lo : d * size + lo + n]


def pack_vectors(ref, ndp, small, at):
    size = ref.shape[1] // ndp
    for d in range(ndp):
        small[at + d, :VECTOR_ROWS, :size] = ref[:VECTOR_ROWS, d * size : (d + 1) * size]


def chunks(rows, size=ROWS):
    return [slice(at, at + size) for at in range(0, rows, size)]


def norm_parts(rows):
    centre = rows - jnp.mean(rows, axis=-1, keepdims=True)
    inv = lax.rsqrt(jnp.mean(centre * centre, axis=-1, keepdims=True) + EPSILON)
    return centre * inv, inv


def row_loop(rows, body, init):
    return lax.fori_loop(0, rows // 128, lambda j, c: body(pl.ds(pl.multiple_of(j * 128, 128), 128), c), init)


def norm_into(read, write, gain, shift, rows):
    def body(r, carry):
        write[r, :] = half(norm_parts(read(r))[0] * gain + shift)
        return carry

    row_loop(rows, body, 0)


def norm_back(read, grad, gain, rows, done):
    def body(r, carry):
        normal, inv = norm_parts(read(r))
        m_hat = grad(r)
        m = m_hat * gain
        part = inv * (
            m - jnp.mean(m, axis=-1, keepdims=True) - normal * jnp.mean(m * normal, axis=-1, keepdims=True)
        )
        done(r, part)
        return carry[0] + sums(m_hat * normal), carry[1] + sums(m_hat)

    zero = jnp.zeros_like(gain)
    return row_loop(rows, body, (zero, zero))


def sums(value):
    return jnp.sum(wide(value), axis=0, keepdims=True)


def gelu_both(t):
    square = t * t
    s = 0.5 + 0.5 * jnp.tanh(t * (GELU_SCALE + GELU_SCALE * 0.044715 * square))
    value = t * s
    slope = s + value * (1.0 - s) * (2 * GELU_SCALE + 6 * GELU_SCALE * 0.044715 * square)
    return value, slope


def masked_pair(head):
    return lax.broadcasted_iota(jnp.int32, (1, 2 * head), 1) < head


def beside(i, steps, rounds):
    for at, acts in zip(steps, rounds):

        @pl.when(i == at)
        def _(acts=acts):
            for act in acts:
                act()


def add_up(fresh, ref, at, value):
    @pl.when(fresh)
    def _():
        ref[at] = value

    @pl.when(jnp.logical_not(fresh))
    def _():
        ref[at] += value


def forward_start(read, vec, value_ref, a_ref, v_ref, first=None):
    rows = a_ref.shape[0]
    norm_into(read, a_ref, vec(GAIN1), vec(BIAS1), rows)
    for r in chunks(rows):
        v_ref[r] = half(mm(a_ref[r], value_ref[...]) + vec(VALUE_B))
        if first is not None:
            first_ref, first_b, p_ref, slope_ref = first
            value, slope = gelu_both(mm(a_ref[r], first_ref[...]) + first_b[...])
            p_ref[r] = half(value)
            slope_ref[r] = half(slope)


def both_heads(pair, head):
    lower = masked_pair(head)
    zero = jnp.zeros_like(pair)
    return jnp.concatenate([jnp.where(lower, pair, zero), jnp.where(lower, zero, pair)], axis=0)


def forward_heads(pair, length, v_ref, c_ref, probs_ref, logits_of, bounded=False):
    rows, width = v_ref.shape
    slots = probs_ref.shape[1] // 2
    head = width // HEADS
    at = pl.ds(pl.multiple_of(pair * 2 * head, 2 * head), 2 * head)
    shut = jnp.where(lax.broadcasted_iota(jnp.int32, (1, slots), 1) >= length, -1e30, 0.0)
    both = logits_of(shut)
    for h in range(2):
        logits = both[h]
        expo = jnp.exp(logits if bounded else logits - jnp.max(logits, axis=1, keepdims=True))
        probs_ref[:, h * slots : (h + 1) * slots] = half(expo * (1.0 / jnp.sum(expo, axis=1, keepdims=True)))
    c_ref[:, at] = half(mm(probs_ref[...], both_heads(v_ref[:, at], head)))


def forward_middle(read, vec, out_ref, c_ref, hid_ref, b_ref):
    rows = c_ref.shape[0]
    for r in chunks(rows):
        hid_ref[r] = read(r) + mm(c_ref[r], out_ref[...]) + vec(OUT_B)
    norm_into(lambda r: hid_ref[r, :], b_ref, vec(GAIN2), vec(BIAS2), rows)


def forward_hidden(fresh, b_ref, inner_ref, inner_b, outer_ref, q_ref, slope_ref, acc):
    for r in chunks(b_ref.shape[0]):
        value, slope = gelu_both(mm(b_ref[r], inner_ref[...]) + inner_b)
        q = half(value)
        q_ref[r] = q
        slope_ref[r] = half(slope)
        add_up(fresh, acc, r, mm(q, outer_ref[...]))


def forward_end(vec, hid_ref, acc, y_ref):
    for r in chunks(acc.shape[0]):
        y_ref[r] = half(hid_ref[r] + acc[r] + vec(OUTER_B))


def backward_hidden(fresh, g_ref, b_ref, q_ref, slope_ref, inner_ref, outer_ref, gz_ref, acc, g_outer, g_inner, g_inner_b):
    for r in chunks(g_ref.shape[0]):
        gz = half(mm_nt(g_ref[r], outer_ref[...]) * wide(slope_ref[r]))
        gz_ref[r] = gz
        add_up(fresh, acc, r, mm_nt(gz, inner_ref[...]))
    gz = gz_ref[...]
    g_outer[...] = half(mm_tn(q_ref[...], g_ref[...]))
    g_inner[...] = half(mm_tn(b_ref[...], gz))
    g_inner_b[...] = sums(gz)


def backward_middle(vec, put, g_ref, hid_ref, c_ref, out_ref, acc, ghid, gatt, gc_ref, g_out):
    rows = g_ref.shape[0]

    def done(r, part):
        total = wide(g_ref[r, :]) + part
        ghid[r, :] = total
        gatt[r, :] = half(total)

    gain, shift = norm_back(lambda r: hid_ref[r, :], lambda r: acc[r, :], vec(GAIN2), rows, done)
    put(GAIN2, gain)
    put(BIAS2, shift)
    put(OUTER_B, sums(g_ref[...]))
    put(OUT_B, sums(gatt[...]))
    g_out[...] = half(mm_tn(c_ref[...], gatt[...]))
    for r in chunks(rows):
        gc_ref[r] = half(mm_nt(gatt[r], out_ref[...]))


def backward_heads(pair, v_ref, c_ref, gc_ref, gv_ref, probs_ref, db):
    rows, width = v_ref.shape
    slots = probs_ref.shape[1] // 2
    head = width // HEADS
    at = pl.ds(pl.multiple_of(pair * 2 * head, 2 * head), 2 * head)
    both = mm_nt(gc_ref[:, at], both_heads(v_ref[:, at], head))
    along = wide(gc_ref[:, at]) * wide(c_ref[:, at])
    lower = masked_pair(head)
    for h in range(2):
        cols = slice(h * slots, (h + 1) * slots)
        mean = jnp.sum(jnp.where(lower if h == 0 else jnp.logical_not(lower), along, 0.0), axis=1, keepdims=True)
        db[:, cols] = half(wide(probs_ref[:, cols]) * (both[:, cols] - mean))
    values = mm_tn(probs_ref[...], gc_ref[:, at])
    gv_ref[:, at] = half(jnp.where(masked_pair(head), values[:slots], values[slots:]))


def backward_end(vec, put, read, gv_ref, value_ref, a_ref, acc, ghid, g_value, gx_ref, first=None):
    rows = gv_ref.shape[0]
    put(VALUE_B, sums(gv_ref[...]))
    g_value[...] = half(mm_tn(a_ref[...], gv_ref[...]))
    if first is not None:
        first_ref, slope_ref, gf_ref, g_first = first
        for r in chunks(rows):
            gf_ref[r] = half(acc[r] * wide(slope_ref[r]))
        put(FIRST_B, sums(gf_ref[...]))
        g_first[...] = half(mm_tn(a_ref[...], gf_ref[...]))
    else:
        put(FIRST_B, jnp.zeros((1, acc.shape[1]), jnp.float32))
    for r in chunks(rows):
        ga = mm_nt(gv_ref[r], value_ref[...])
        if first is not None:
            ga = ga + mm_nt(gf_ref[r], first_ref[...])
        acc[r] = ga

    def done(r, part):
        gx_ref[r, :] = half(ghid[r, :] + part)

    gain, shift = norm_back(read, lambda r: acc[r, :], vec(GAIN1), rows, done)
    put(GAIN1, gain)
    put(BIAS1, shift)


def forward_kernel(pairs, parts, host, length_ref, x_ref, small, value_ref, out_ref, first_ref, second_ref, inner_ref, outer_ref, *refs):
    n = 1 if host else 0
    far, y_ref, refs = refs[:n], refs[n], refs[n + 1 :]
    kept, probs_ref, q_ref, slope_ref, table, refs = refs[:7], refs[7], refs[8], refs[9], refs[10 : 10 + n], refs[10 + n :]
    a_ref, v_ref, p_ref, first_slope, c_ref, b_ref, hid_ref, acc, vectors, inner_b, first_b, second_b, sem, *refs = refs
    rounds, last = [], []
    if host:
        raw, shard, load, *sems = refs
        place = Place(host[1])
        loading = pltpu.make_async_copy(far[0], raw, load.at[0])

        def prepare():
            loading.start()
            greet(place)
            loading.wait()
            shard[...] = half(raw[...])

        rounds, last = gather_rounds(host[0], place, host[1], [shard], table, [prepare], sems)
    held = (a_ref, v_ref, p_ref, first_slope, c_ref, b_ref, hid_ref)
    copies = [pltpu.make_async_copy(src, dst, sem.at[j]) for j, (src, dst) in enumerate(zip(held, kept))]
    i = pl.program_id(0)
    slots = probs_ref.shape[2] // 2
    ndp, part = small.shape[0] // 2, q_ref.shape[1]

    def vec(k):
        return vectors[k : k + 1, :]

    x_ref, y_ref = x_ref.at[0], y_ref.at[0]
    length = length_ref[lax.axis_index("segment"), 0]

    def read(r):
        return wide(x_ref[r, :])

    beside(i, BESIDE_FORWARD, rounds)

    @pl.when(i == 0)
    def _():
        unpack_vectors(small, 0, ndp, vectors)
        unpack_rows(small, 0, ndp, VECTOR_ROWS, inner_b)
        row = VECTOR_ROWS + rows_for(inner_b.shape[1] // ndp)
        unpack_rows(small, 0, 2 * ndp, row, first_b)
        unpack_rows(small, 0, 2 * ndp, row + rows_for(first_b.shape[1] // (2 * ndp)), second_b)
        forward_start(read, vec, value_ref.at[0], a_ref, v_ref, (first_ref, first_b, p_ref, first_slope))
        for copy in copies[:4]:
            copy.start()

    @pl.when(i < pairs)
    def _():
        def logits_of(shut):
            bias = second_b[:, pl.ds(pl.multiple_of(i * 2 * slots, 2 * slots), 2 * slots)]
            logits = mm(p_ref[...], second_ref[...]) + (bias + jnp.concatenate([shut, shut], axis=1))
            return logits[:, :slots], logits[:, slots:]

        forward_heads(i, length, v_ref, c_ref, probs_ref.at[0], logits_of)

    @pl.when(i == pairs - 1)
    def _():
        forward_middle(read, vec, out_ref.at[0], c_ref, hid_ref, b_ref)
        for copy in copies[4:]:
            copy.start()

    @pl.when(i >= pairs)
    def _():
        bias = inner_b[:, pl.ds(pl.multiple_of((i - pairs) * part, part), part)]
        forward_hidden(i == pairs, b_ref, inner_ref.at[0], bias, outer_ref.at[0], q_ref, slope_ref, acc)

    @pl.when(i == pairs + parts - 1)
    def _():
        forward_end(vec, hid_ref, acc, y_ref)
        for copy in copies:
            copy.wait()
        for acts in rounds[len(BESIDE_FORWARD) :] + [last]:
            for act in acts:
                act()


def backward_kernel(pairs, parts, host, g_ref, b_ref, small, g_small1, q_ref, slope_ref, probs_ref, inner_ref, outer_ref, second_ref, *refs):
    far, refs = refs[:10], refs[13:]
    n, swaps = (max(entry[0] for entry in host[0]) + 1, 1) if host else (0, 0)
    sum_ins, ys, refs = refs[:n], refs[n : n + swaps], refs[n + swaps :]
    gx_ref, g_outer, g_inner, g_out, g_value, g_small, g_first, g_second = refs[:8]
    sum_outs, other_ys, refs = refs[8 : 8 + n], refs[8 + n : 8 + n + swaps], refs[8 + n + swaps :]
    near, refs = refs[:10], refs[10:]
    acc, ghid, gatt, gc_ref, gv_ref, db, gz_ref, vectors, g_vec, g_inner_b, g_second_b, sem, *refs = refs
    far = [ref.at[0] if len(ref.shape) == 3 else ref for ref in far]
    copies = [pltpu.make_async_copy(src, dst, sem.at[j]) for j, (src, dst) in enumerate(zip(far, near))]
    hid_ref, c_ref, out_ref, v_ref, p_ref, a_ref, value_ref, first_ref, first_slope, x_ref = near
    i = pl.program_id(0)
    rounds, sent = [], []
    if host:
        place = Place(host[1])
        pl.when(i == 0)(lambda: greet(place))
        *refs, swap = refs
        rounds, sent = sum_rounds(host[0], place, host[1], sum_ins, sum_outs, refs)
        swapped = pltpu.make_async_remote_copy(
            src_ref=ys[0].at[1 - place.x],
            dst_ref=other_ys[0],
            send_sem=swap.at[0],
            recv_sem=swap.at[1],
            device_id=place.other("x"),
            device_id_type=MESH,
        )
        rounds[0].append(swapped.start)
        sent.append(swapped.wait)
    slots = probs_ref.shape[2] // 2
    ndp, part = small.shape[0] // 2, q_ref.shape[1]

    def vec(k):
        return vectors[k : k + 1, :]

    def put(k, value):
        g_vec[k : k + 1, :] = value

    @pl.when(i == 0)
    def _():
        for copy in copies:
            copy.start()
        unpack_vectors(small, 0, ndp, vectors)

    beside(i, BESIDE_BACKWARD, rounds)

    @pl.when(i < parts)
    def _():
        bias = g_inner_b.at[:, pl.ds(pl.multiple_of(i * part, part), part)]
        backward_hidden(i == 0, g_ref, b_ref, q_ref, slope_ref, inner_ref.at[0], outer_ref.at[0], gz_ref, acc, g_outer, g_inner.at[0], bias)

    @pl.when(i == parts - 1)
    def _():
        for copy in copies[:3]:
            copy.wait()
        backward_middle(vec, put, g_ref, hid_ref, c_ref, out_ref, acc, ghid, gatt, gc_ref, g_out.at[0])
        for copy in copies[3:5]:
            copy.wait()

    @pl.when(i >= parts)
    def _():
        backward_heads(i - parts, v_ref, c_ref, gc_ref, gv_ref, probs_ref.at[0], db)
        g_second[...] = half(mm_tn(p_ref[...], db[...]))
        g_second_b[:, pl.ds(pl.multiple_of((i - parts) * 2 * slots, 2 * slots), 2 * slots)] = sums(db[...])
        add_up(i == parts, acc, slice(None), mm_nt(db[...], second_ref[...]))

    @pl.when(i == pairs + parts - 1)
    def _():
        for copy in copies[5:]:
            copy.wait()
        backward_end(
            vec, put, lambda r: wide(x_ref[r, :]), gv_ref, value_ref, a_ref, acc, ghid, g_value.at[0], gx_ref,
            (first_ref, first_slope, gatt, g_first),
        )
        g_small[:ndp] = jnp.zeros_like(g_small1)
        g_small[ndp:] = g_small1[...]
        pack_vectors(g_vec, ndp, g_small, 0)
        pack_rows(g_inner_b, ndp, VECTOR_ROWS, g_small, 0)
        row = VECTOR_ROWS + rows_for(g_inner_b.shape[1] // ndp)
        pack_rows(g_vec.at[FIRST_B : FIRST_B + 1, :], 2 * ndp, row, g_small, 0)
        row += rows_for(g_vec.shape[1] // (2 * ndp))
        pack_rows(g_second_b, 2 * ndp, row, g_small, 0)
        for acts in rounds[len(BESIDE_BACKWARD) :] + [sent]:
            for act in acts:
                act()


def both_kernel(pairs, parts, length_ref, x_ref, g_ref, small, value_ref, out_ref, table_ref, inner_ref, outer_ref, *refs):
    y_ref, gx_ref, g_outer, g_inner, far_g_out, g_value, g_small, g_table = refs[:8]
    acc, hid_ref, ghid, a_ref, v_ref, c_ref, b_ref, gatt, gc_ref, gv_ref, probs_ref, q_ref, slope_ref, db, gz_ref, *refs = refs[8:]
    vectors, inner_b, g_vec, g_inner_b, near_g, near_out, g_out, sem = refs
    i = pl.program_id(0)
    slots = probs_ref.shape[2] // 2
    j = i - pairs
    k = j - parts
    n = k - parts

    ndp, part = small.shape[0] // 2, q_ref.shape[2]

    def vec(k):
        return vectors[k : k + 1, :]

    def put(k, value):
        g_vec[k : k + 1, :] = value

    def hidden(ref, k):
        return ref.at[:, pl.ds(pl.multiple_of(k * part, part), part)]

    load_out = pltpu.make_async_copy(out_ref.at[1], near_out, sem.at[0])
    load_g = pltpu.make_async_copy(g_ref.at[1], near_g, sem.at[1])
    store_out = pltpu.make_async_copy(g_out, far_g_out.at[1], sem.at[2])
    x_ref, y_ref = x_ref.at[0], y_ref.at[0]
    g_ref, out_ref = near_g, near_out

    def read(r):
        return wide(x_ref[r, :])

    @pl.when(i == 0)
    def _():
        load_out.start()
        load_g.start()
        unpack_vectors(small, ndp, ndp, vectors)
        unpack_rows(small, ndp, ndp, VECTOR_ROWS, inner_b)
        forward_start(read, vec, value_ref.at[0], a_ref, v_ref)

    @pl.when(i < pairs)
    def _():
        def logits_of(shut):
            return wide(table_ref[:slots, :]) + shut, wide(table_ref[slots:, :]) + shut

        forward_heads(i, length_ref[lax.axis_index("segment"), 0], v_ref, c_ref, probs_ref.at[i], logits_of, True)

    @pl.when(i == pairs - 1)
    def _():
        load_out.wait()
        load_g.wait()
        forward_middle(read, vec, out_ref, c_ref, hid_ref, b_ref)

    @pl.when((j >= 0) & (j < parts))
    def _():
        forward_hidden(j == 0, b_ref, inner_ref.at[0], hidden(inner_b, j)[...], outer_ref.at[0], q_ref.at[j], slope_ref.at[j], acc)

    @pl.when(j == parts - 1)
    def _():
        forward_end(vec, hid_ref, acc, y_ref)

    @pl.when((k >= 0) & (k < parts))
    def _():
        at = parts - 1 - k
        backward_hidden(k == 0, g_ref, b_ref, q_ref.at[at], slope_ref.at[at], inner_ref.at[0], outer_ref.at[0], gz_ref, acc, g_outer, g_inner.at[0], hidden(g_inner_b, at))

    @pl.when(k == parts - 1)
    def _():
        backward_middle(vec, put, g_ref, hid_ref, c_ref, out_ref, acc, ghid, gatt, gc_ref, g_out)
        store_out.start()

    @pl.when(n >= 0)
    def _():
        backward_heads(n, v_ref, c_ref, gc_ref, gv_ref, probs_ref.at[n], db)
        g_table[:slots, :] = db[:, :slots]
        g_table[slots:, :] = db[:, slots:]

    @pl.when(n == pairs - 1)
    def _():
        backward_end(vec, put, read, gv_ref, value_ref.at[0], a_ref, acc, ghid, g_value.at[0], gx_ref)
        g_small[...] = jnp.zeros_like(g_small)
        pack_vectors(g_vec, ndp, g_small, 0)
        pack_rows(g_inner_b, ndp, VECTOR_ROWS, g_small, 0)
        store_out.wait()


class Weights(NamedTuple):
    small: Any
    value: Any
    out: Any
    inner: Any
    outer: Any
    first: Any
    second: Any
    table: Any


def whole(shape, *at):
    at = tuple(at)
    block = (1,) * len(at) + tuple(shape[len(at) :])
    return pl.BlockSpec(block, lambda i: at + (0,) * (len(shape) - len(at)), pipeline_mode=pl.Buffered(1))


def whole_out(shape, *at):
    at = tuple(at)
    block = (1,) * len(at) + tuple(shape[len(at) :])
    return pl.BlockSpec(block, lambda i: at + (0,) * (len(shape) - len(at)))


def like(shape, dtype=jnp.bfloat16):
    return jax.ShapeDtypeStruct(shape, dtype)


FAR = pl.BlockSpec(memory_space=pl.ANY)


def sizes_of(x, w):
    rows, width = x.shape[-2:]
    parts = w.inner.shape[2] // HIDDEN
    return rows, width, HEADS // 2, parts, w.inner.shape[2] // parts


def forward(x, lengths, w, host=None, late=()):
    rows, width, pairs, parts, part = sizes_of(x, w)
    slots = rows

    def pair(i):
        return jnp.minimum(i, pairs - 1)

    def piece(i):
        return jnp.maximum(i - pairs, 0)

    ins = [lengths, x, w.small, w.value, w.out, w.first, w.second, w.inner, w.outer] + list(late)
    specs = [
        pl.BlockSpec(memory_space=pltpu.SMEM),
        whole(x.shape, 0),
        whole(w.small.shape),
        whole(w.value.shape, 0),
        whole(w.out.shape, 0),
        whole(w.first.shape),
        pl.BlockSpec((width, 2 * slots), lambda i: (0, pair(i))),
        pl.BlockSpec((1, width, part), lambda i: (0, 0, piece(i))),
        pl.BlockSpec((1, part, width), lambda i: (0, piece(i), 0)),
    ] + [FAR] * len(late)
    table = [like((2, host[1], 2, 2) + t.shape) for t in late]
    half_rows = like((rows, width))
    kept = [half_rows] * 6 + [like((rows, width), jnp.float32)]
    hidden_block = pl.BlockSpec((rows, part), lambda i: (0, piece(i)))
    y, *saved = pl.pallas_call(
        functools.partial(forward_kernel, pairs, parts, host),
        grid=(pairs + parts,),
        out_shape=[like(x.shape)] + kept + [like((pairs, rows, 2 * slots))] + [like((rows, part * parts))] * 2 + table,
        in_specs=specs,
        out_specs=[whole_out(x.shape, 0)]
        + [FAR] * 7
        + [pl.BlockSpec((1, rows, 2 * slots), lambda i: (pair(i), 0, 0))]
        + [hidden_block] * 2
        + [FAR] * len(table),
        scratch_shapes=[pltpu.VMEM(k.shape, k.dtype) for k in kept]
        + [
            pltpu.VMEM((rows, width), jnp.float32),
            pltpu.VMEM((8, width), jnp.float32),
            pltpu.VMEM((1, part * parts), jnp.float32),
            pltpu.VMEM((1, width), jnp.float32),
            pltpu.VMEM((1, w.second.shape[1]), jnp.float32),
            pltpu.SemaphoreType.DMA((7,)),
        ]
        + [pltpu.VMEM(t.shape, t.dtype) for t in late]
        + [pltpu.VMEM(t.shape, jnp.bfloat16) for t in late]
        + ([pltpu.SemaphoreType.DMA((1,))] + gather_sems(*host) if host else []),
        compiler_params=pltpu.CompilerParams(
            vmem_limit_bytes=62 * 2**20, **(dict(collective_id=3, has_side_effects=True) if host else {})
        ),
        name="forward_0",
    )(*ins)
    return y, saved[:10], saved[10:]


def backward(g, x, saved, w, before, small1, host=None, early=(), ys=()):
    rows, width, pairs, parts, part = sizes_of(x, w)
    slots = rows
    a, v, p, first_slope, c, b, hid, probs, q, slope = saved

    def pair(i):
        return jnp.maximum(i - parts, 0)

    def piece(i):
        return jnp.minimum(i, parts - 1)

    hidden_block = pl.BlockSpec((rows, part), lambda i: (0, piece(i)))
    inner_block = pl.BlockSpec((1, width, part), lambda i: (0, 0, piece(i)))
    outer_block = pl.BlockSpec((1, part, width), lambda i: (0, piece(i), 0))
    second_block = pl.BlockSpec((width, 2 * slots), lambda i: (0, pair(i)))
    far = [hid, c, w.out, v, p, a, w.value, w.first, first_slope, x]
    ins = [g, b, w.small, small1, q, slope, probs, w.inner, w.outer, w.second] + far
    specs = [whole((rows, width))] * 2 + [whole(w.small.shape), whole(small1.shape)] + [hidden_block] * 2
    specs += [pl.BlockSpec((1, rows, 2 * slots), lambda i: (pair(i), 0, 0)), inner_block, outer_block, second_block]
    specs += [FAR] * 10
    aliases = {len(ins) + j: 2 + j for j in range(3)}
    ins += list(before) + list(early) + list(ys)
    specs += [FAR] * (3 + len(early) + len(ys))
    outs = [like((rows, width)), like(w.outer.shape[1:])] + [like(k.shape, k.dtype) for k in before]
    out_specs = [whole_out((rows, width)), pl.BlockSpec((part, width), lambda i: (piece(i), 0)), inner_block]
    out_specs += [whole_out(w.out.shape, 0), whole_out(w.value.shape, 0)]
    outs += [like(w.small.shape, jnp.float32), like(w.first.shape), like(w.second.shape)]
    out_specs += [whole_out(w.small.shape), whole_out(w.first.shape), second_block]
    sums_of = [like(e.shape[-2:], jnp.float32) for e in early]
    gx, *grads = pl.pallas_call(
        functools.partial(backward_kernel, pairs, parts, host),
        grid=(pairs + parts,),
        out_shape=outs + sums_of + [like(y.shape[1:]) for y in ys],
        in_specs=specs,
        out_specs=out_specs + [whole_out(e.shape) for e in sums_of] + [FAR] * len(ys),
        scratch_shapes=[pltpu.VMEM(k.shape[-2:], k.dtype) for k in far]
        + [pltpu.VMEM((rows, width), jnp.float32)] * 2
        + [pltpu.VMEM((rows, width), jnp.bfloat16)] * 3
        + [pltpu.VMEM((rows, 2 * slots), jnp.bfloat16), pltpu.VMEM((rows, part), jnp.bfloat16)]
        + [pltpu.VMEM((8, width), jnp.float32)] * 2
        + [pltpu.VMEM((1, part * parts), jnp.float32), pltpu.VMEM((1, w.second.shape[1]), jnp.float32)]
        + [pltpu.SemaphoreType.DMA((10,))]
        + (sum_scratch(host[0], early, host[1]) + [pltpu.SemaphoreType.DMA((2,))] if host else []),
        input_output_aliases=aliases,
        compiler_params=pltpu.CompilerParams(
            vmem_limit_bytes=63 * 2**20, **(dict(collective_id=2, has_side_effects=True) if host else {})
        ),
        name="backward_0",
    )(*ins)
    return gx, grads[:7], grads[7:]


def both_ways(x, g, lengths, w):
    rows, width, pairs, parts, part = sizes_of(x, w)
    slots = rows

    def there(i):
        return jnp.minimum(i, pairs - 1)

    def back(i):
        return jnp.maximum(i - pairs - 2 * parts, 0)

    def piece(i):
        j = jnp.clip(i - pairs, 0, 2 * parts - 1)
        return jnp.minimum(j, 2 * parts - 1 - j)

    def late(i):
        return parts - 1 - jnp.clip(i - pairs - parts, 0, parts - 1)

    ins = [lengths, x, g, w.small, w.value, w.out, w.table, w.inner, w.outer]
    specs = [pl.BlockSpec(memory_space=pltpu.SMEM), whole(x.shape, 0), FAR]
    specs += [whole(w.small.shape), whole(w.value.shape, 1), FAR]
    specs += [
        pl.BlockSpec((2 * slots, slots), lambda i: (there(i), 0)),
        pl.BlockSpec((1, width, part), lambda i: (1, 0, piece(i))),
        pl.BlockSpec((1, part, width), lambda i: (1, piece(i), 0)),
    ]
    grads = [like(w.outer.shape[1:]), like(w.inner.shape), like(w.out.shape), like(w.value.shape)]
    small = (w.small.shape[0] // 2,) + w.small.shape[1:]
    grads += [like(small, jnp.float32), like(w.table.shape)]
    grad_specs = [
        pl.BlockSpec((part, width), lambda i: (late(i), 0)),
        pl.BlockSpec((1, width, part), lambda i: (1, 0, late(i))),
        FAR,
        whole_out(w.value.shape, 1),
        whole_out(small),
        pl.BlockSpec((2 * slots, slots), lambda i: (back(i), 0)),
    ]
    y, gx, *grads = pl.pallas_call(
        functools.partial(both_kernel, pairs, parts),
        grid=(2 * pairs + 2 * parts,),
        out_shape=[like(x.shape), like((rows, width))] + grads,
        in_specs=specs,
        out_specs=[whole_out(x.shape, 1), whole_out((rows, width))] + grad_specs,
        scratch_shapes=[pltpu.VMEM((rows, width), jnp.float32)] * 3
        + [pltpu.VMEM((rows, width), jnp.bfloat16)] * 7
        + [pltpu.VMEM((pairs, rows, 2 * slots), jnp.bfloat16)]
        + [pltpu.VMEM((parts, rows, part), jnp.bfloat16)] * 2
        + [pltpu.VMEM((rows, 2 * slots), jnp.bfloat16), pltpu.VMEM((rows, part), jnp.bfloat16)]
        + [pltpu.VMEM((8, width), jnp.float32), pltpu.VMEM((1, part * parts), jnp.float32)] * 2
        + [pltpu.VMEM((rows, width), jnp.bfloat16)]
        + [pltpu.VMEM(w.out.shape[1:], jnp.bfloat16)] * 2
        + [pltpu.SemaphoreType.DMA((3,))],
        input_output_aliases={1: 0},
        compiler_params=pltpu.CompilerParams(vmem_limit_bytes=62 * 2**20),
        name="forward_backward_1",
    )(*ins)
    return y, gx, grads


ROW_VECTORS = (0, 1, 3, 5, 6, 7, 11)
VECTORS = ROW_VECTORS + (9, 13, 15)
MATRICES = (2, 4, 8, 10, 12, 14, 16)
SMALL = 17
GATHER = (
    (12, None, "zyx", 2),
    (4, None, "zyx", 2),
    (14, 0, "xzy", 3),
    (SMALL, None, "zyx", 3),
    (2, None, "xzy", 0),
    (14, 1, "yzx", 2),
    (10, None, "xzy", 1),
    (8, None, "zyx", 0),
)
LATE = ((16, 0, "zyx", 0), (16, 1, "xzy", 0))
BESIDE_FORWARD = (0, 1, 3, 5, 7, 9)
EARLY = ((10, 1, "yzx", 1, 1), (10, 0, "yzx", 0, 1), (16, 1, "yxz", 1, None), (16, 0, "xzy", 1, None))
BESIDE_BACKWARD = (0, 0, 1, 3, 4, 8)
SUM = (
    (4, None, "yzx", 0, None),
    (14, 1, "yzx", 1, None),
    (10, None, "yzx", 2, 0),
    (2, None, "yzx", 3, None),
    (12, None, "yxz", 2, None),
    (14, 0, "xzy", 1, None),
    (8, None, "xyz", 2, None),
    (SMALL, None, "xzy", 2, None),
)


def numbered(plan):
    names = list(dict.fromkeys(entry[0] for entry in plan))
    return names, [(names.index(entry[0]),) + entry[1:] for entry in plan]


def planned(call, plan, arrays, mesh, rows):
    names, plan = numbered(plan)
    got, rows = call([arrays[k] for k in names], plan, mesh, rows)
    return dict(zip(names, got)), rows


def lanes(vector):
    rows = rows_for(vector.size)
    return jnp.pad(vector.reshape(-1), (0, rows * 128 - vector.size)).reshape(rows, 128)


def sixteens(rows):
    return jnp.pad(rows, ((0, -rows.shape[0] % 16), (0, 0)))


def per_device(mesh, boundary, lengths, *parts):
    nx, ndp = mesh.shape["segment"], mesh.shape["dp"]
    devices = nx * ndp
    fast = nx == 2 and ndp == 16
    sizes = [parts[k].size for k in VECTORS]

    shards = {k: parts[k].reshape(parts[k].shape[-2:]) for k in MATRICES}
    shards[SMALL] = [parts[k].reshape(1, -1) for k in VECTORS]
    full, pair = planned(gather_all, GATHER, shards, mesh, boundary[0, :, 0])
    if not fast:
        full[16] = lax.all_gather(half(shards[16]), AXES, axis=0)
    for k in full:
        if k == SMALL:
            continue
        g = full[k]
        full[k] = g.reshape((nx, ndp * g.shape[1]) + g.shape[2:]) if k < 12 else g.reshape(-1, g.shape[2])
    w = Weights(full[SMALL], full[2], full[4], full[8], full[10], full[12], full[14], full.get(16))

    if fast:
        outs, saved, (table,) = forward(pair, lengths, w, (numbered(LATE)[1], ndp // 4), [shards[16]])
        w = w._replace(table=table.reshape(-1, table.shape[-1]))
    else:
        outs, saved, _ = forward(pair, lengths, w)
    outs, gin1, (g_outer1, *both, g_small, g_table) = both_ways(outs, pair, lengths, w)
    early = {16: g_table.reshape((devices,) + parts[16].shape), 10: g_outer1.reshape((ndp,) + parts[10].shape[1:])}
    names, plan = numbered(EARLY)
    early = [early[k] for k in names]
    if fast:
        host, hosted = (plan, ndp // 4), by_chip(early, plan, ndp // 4)
        gin0, grads, (*sums_early, other_outs) = backward(gin1, pair, saved, w, both, g_small, host, hosted, [outs])
    else:
        gin0, grads, _ = backward(gin1, pair, saved, w, both, g_small)
        sums_early = plain_sums(early, plan)
        other_outs = from_other(outs[0], outs[1])
    sums_early = dict(zip(names, sums_early))

    g_outer0, g_inner, g_out, g_value, g_small, g_first, g_second = grads
    grads = {2: g_value, 4: g_out, 8: g_inner, 12: g_first, 14: g_second}
    grads = {k: g.reshape((devices,) + parts[k].shape[-2:]) for k, g in grads.items()}
    grads[10] = g_outer0.reshape((ndp,) + parts[10].shape[1:])
    grads[SMALL] = g_small
    summed, other_gins = planned(scatter_all, SUM, grads, mesh, [gin0, gin1])
    summed[16] = sums_early[16]
    summed[10] = (summed[10], sums_early[10])
    matrices = [summed[k] for k in MATRICES]
    arrays, vectors = finish(outs, other_outs, [gin0, gin1], other_gins, matrices, summed[SMALL], sizes)
    result = {k: g.reshape(parts[k].shape) for k, g in zip(MATRICES, arrays[2:])}
    for k, g in zip(VECTORS, vectors):
        result[k] = g.reshape(parts[k].shape)
    return tuple(a.reshape(boundary.shape) for a in arrays[:2]) + tuple(result[k] for k in range(17))


def solution(mesh):
    layer = [P("segment", "dp")] * 12
    layer[2] = layer[4] = layer[8] = layer[10] = P("segment", "dp", None)
    both = P(AXES)
    rows = P(AXES, None)
    boundary = P("segment", None, "dp", None, None)
    weights = tuple(layer) + (rows, both, rows, both, rows)
    return jax.shard_map(
        functools.partial(per_device, mesh),
        mesh=mesh,
        in_specs=(boundary, P(None, "dp")) + weights,
        out_specs=(boundary, boundary) + weights,
        check_vma=False,
    )
```
